32 devices in a mesh: rows: 8 (over z, y), quant: 4 (over x, core).
Axes of the slice: x: 2, y: 2, z: 4, core: 2. Of those that a mesh axis runs over, the one named last changes fastest.
Arguments:
- observed_inputs: bfloat16 [32768, 376], P(('rows', 'quant')), may hold values from -6 to 6
- chosen_controls: bfloat16 [32768, 17], P(('rows', 'quant')), may hold values from -0.94921875 to 0.94921875
- present_gauss_draw: float32 [32768, 17], P(('rows', 'quant')), may hold values from -5 to 5
- successor_observations: bfloat16 [32768, 376], P('rows'), may hold values from -6 to 6
- successor_gauss_draw: float32 [32768, 17], P('rows'), may hold values from -5 to 5
- payoffs: float32 [32768], P('rows'), may hold values from -4 to 4
- terminal_indicator: int32 [32768], P('rows'), may hold values 0 or 1
- merged_support_order: int32 [32768, 125], P('rows'), may hold values from 0 to 124, each once within a row
- entry_layer_cast: bfloat16 [393, 2560], replicated, may hold values from -0.3125 to 0.3125
- inner_layer_cast: bfloat16 [512, 2560], replicated, may hold values from -0.25 to 0.25
- critic_inner_offsets: float32 [2, 2560], replicated, may hold values from -1.5 to 1.5
- readout_matrix_cast: bfloat16 [512, 128], P(None, 'quant'), may hold values from -0.25 to 0.25
- lagged_entry_layer: bfloat16 [393, 2560], replicated, may hold values from -0.3125 to 0.3125
- lagged_inner_layer: bfloat16 [512, 2560], replicated, may hold values from -0.25 to 0.25
- lagged_inner_offsets: float32 [2, 2560], replicated, may hold values from -1.5 to 1.5
- lagged_readout: bfloat16 [512, 128], P(None, 'quant'), may hold values from -0.25 to 0.25
- lagged_readout_offsets: float32 [128], replicated, may hold values from -1.5 to 1.5
- pilot_weights_cast: bfloat16 [666, 256], replicated, may hold values from -0.375 to 0.375
- update_counter: int32 [1], replicated, may hold values from 2 to 20
- entry_layer_main: float32 [393, 2560], P(None, ('rows', 'quant')), may hold values from -0.3125 to 0.3125
- entry_layer_moment_one: float32 [393, 2560], P(None, ('rows', 'quant')), may hold values from -2.3841858e-06 to 2.3841858e-06
- entry_layer_moment_two: float32 [393, 2560], P(None, ('rows', 'quant')), may hold values from 2.2e-15 to 9e-15
- inner_layer_main: float32 [512, 2560], P(None, ('rows', 'quant')), may hold values from -0.25 to 0.25
- inner_layer_moment_one: float32 [512, 2560], P(None, ('rows', 'quant')), may hold values from -7.6293945e-06 to 7.6293945e-06
- inner_layer_moment_two: float32 [512, 2560], P(None, ('rows', 'quant')), may hold values from 2e-14 to 8e-14
- offset_vector_main: float32 [2, 2560], P(None, ('rows', 'quant')), may hold values from -1.5 to 1.5
- offset_moment_one: float32 [2, 2560], P(None, ('rows', 'quant')), may hold values from -1.5258789e-05 to 1.5258789e-05
- offset_moment_two: float32 [2, 2560], P(None, ('rows', 'quant')), may hold values from 8e-14 to 3.2e-13
- readout_matrix_main: float32 [512, 128], P('rows', 'quant'), may hold values from -0.25 to 0.25
- readout_moment_one: float32 [512, 128], P('rows', 'quant'), may hold values from -0.00061035156 to 0.00061035156
- readout_moment_two: float32 [512, 128], P('rows', 'quant'), may hold values from 1.6e-10 to 6.4e-10
- pilot_weights_main: float32 [666, 256], replicated, may hold values from -0.375 to 0.375
- pilot_moment_one: float32 [666, 256], replicated, may hold values from -0.0078125 to 0.0078125
- pilot_moment_two: float32 [666, 256], replicated, may hold values from 2.5e-08 to 1e-07
- vector_params_main: float32 [674], replicated, may hold values from -1.5 to 1.5
- vector_moment_one: float32 [674], replicated, may hold values from -1 to 1, as said below
- vector_moment_two: float32 [674], replicated, may hold values from 0 to 1, as said below
- heat_logarithm_main: float32 [1], replicated, may hold values from -4 to -3
- heat_moment_one: float32 [1], replicated, may hold values from 1.5 to 5
- heat_moment_two: float32 [1], replicated, may hold values from 1 to 4
Outputs:
- objective_scalar: float32 [], replicated
- in_new: float32 [393, 2560], P(None, ('rows', 'quant'))
- in_first_new: float32 [393, 2560], P(None, ('rows', 'quant'))
- in_second_new: float32 [393, 2560], P(None, ('rows', 'quant'))
- mid_new: float32 [512, 2560], P(None, ('rows', 'quant'))
- mid_first_new: float32 [512, 2560], P(None, ('rows', 'quant'))
- mid_second_new: float32 [512, 2560], P(None, ('rows', 'quant'))
- bias_new: float32 [2, 2560], P(None, ('rows', 'quant'))
- bias_first_new: float32 [2, 2560], P(None, ('rows', 'quant'))
- bias_second_new: float32 [2, 2560], P(None, ('rows', 'quant'))
- head_new: float32 [512, 128], P('rows', 'quant')
- head_first_new: float32 [512, 128], P('rows', 'quant')
- head_second_new: float32 [512, 128], P('rows', 'quant')
- actor_new: float32 [666, 256], replicated
- actor_first_new: float32 [666, 256], replicated
- actor_second_new: float32 [666, 256], replicated
- small_new: float32 [674], replicated
- small_first_new: float32 [674], replicated
- small_second_new: float32 [674], replicated
- alpha_new: float32 [1], replicated
- alpha_first_new: float32 [1], replicated
- alpha_second_new: float32 [1], replicated
The draws below stay inside these ranges and needn't reach their ends.
Inputs may be any that keep to these rules, and one draw needn't show every extreme that they name: `vector_moment_one`: entries of both signs. `vector_moment_two`: positive entries.
All inputs are finite; a program needn't handle non-finite values. No bound on the sum of `terminal_indicator` on one device may be relied on, other than what follows from the above.
Results may differ from the reference program's by a relative error of at most 0.017.
Values may be sent and summed in bfloat16 or wider, within the bound.
No kernel may reach another device: no remote copies, remote signals or barrier semaphores. Data moves between devices by JAX's collectives and lax.ppermute only.
A program may use at most 512 MiB of HBM per device.

```python
import math
import jax
import jax.numpy as jnp
from jax import lax

OBS_DIM = 376
ACT_DIM = 17
HIDDEN_SIZE = 512
ACTOR_HIDDEN = 256
CRITICS = 5
QUANTS = 25
PADDED = 128
MERGED_SUPPORTS = 125
KEPT_ATOMS = 115
INPUTS = 393
FEATURES = 2560
ACTOR_ROWS = 666
SMALL_VEC = 674
OVERALL_SAMPLES = 32768


def small_scales():
    positions = jnp.arange(SMALL_VEC)
    return jnp.where(positions < 2 * ACTOR_HIDDEN + 2 * ACT_DIM, 0.01, 0.0008).astype(jnp.float32)


def draw_vector_moment_one(key, part):
    key = jax.random.fold_in(key, 11)
    values = 0.11 * small_scales() * jax.random.normal(key, (SMALL_VEC,), jnp.float32)
    return jnp.clip(values, -0.9, 0.9)


def draw_vector_moment_two(key, part):
    key = jax.random.fold_in(key, 23)
    factor = jnp.exp(jax.random.uniform(key, (SMALL_VEC,), jnp.float32, 0.0, math.log(4.0)))
    scales = small_scales()
    return 0.001 * scales * scales * factor


def plant(values, own_key, least, high):
    spot = [jax.random.randint(jax.random.fold_in(own_key, axis), (), 0, length) for axis, length in enumerate(values.shape)]
    widest = values.shape.index(max(values.shape))
    beside = spot[:widest] + [(spot[widest] + 1) % values.shape[widest]] + spot[widest + 1:]
    return values.at[tuple(spot)].set(least).at[tuple(beside)].set(high)


def block_levels(stream_key, shape, pieces, smallest, high):
    loudness, own = 1.0, jax.random.fold_in(stream_key, 6)
    for dim, shards_of in pieces:
        steps = jnp.exp(jax.random.uniform(jax.random.fold_in(own, dim), (shards_of,), jnp.float32, smallest / len(pieces), high / len(pieces)))
        loudness = loudness * jnp.repeat(steps, shape[dim] // shards_of).reshape([-1 if axis == dim else 1 for axis in range(len(shape))])
    return loudness


def gaussian(rng, shape, width, reach, cuts=(), held_as=jnp.bfloat16):
    loudness = block_levels(rng, shape, cuts, -0.22, 0.18) if cuts else 1.0
    entries = jax.random.normal(rng, shape, jnp.float32) * width * loudness
    return jnp.minimum(jnp.maximum(entries, -reach), reach).astype(held_as)


def setup_inputs(seed: int = 0) -> dict:
    seeds = jax.random.split(jax.random.key(seed), 41)
    observed_inputs = gaussian(seeds[0], (OVERALL_SAMPLES, OBS_DIM), 1.0, 6.0, ((0, 32),))
    chosen_controls = jnp.clip(jax.random.uniform(seeds[1], (OVERALL_SAMPLES, ACT_DIM), jnp.float32, -0.94921875, 0.94921875) * block_levels(seeds[1], (OVERALL_SAMPLES, ACT_DIM), ((0, 32),), -0.4, 0.0), -0.94921875, 0.94921875).astype(jnp.bfloat16)
    present_gauss_draw = gaussian(seeds[2], (OVERALL_SAMPLES, ACT_DIM), 1.0, 5.0, ((0, 32),), jnp.float32)
    successor_observations = gaussian(seeds[3], (OVERALL_SAMPLES, OBS_DIM), 1.0, 6.0, ((0, 8),))
    successor_gauss_draw = gaussian(seeds[4], (OVERALL_SAMPLES, ACT_DIM), 1.0, 5.0, ((0, 8),), jnp.float32)
    payoffs = gaussian(seeds[5], (OVERALL_SAMPLES,), 0.5, 4.0, ((0, 8),), jnp.float32)
    terminal_indicator = plant((jax.random.randint(seeds[6], (OVERALL_SAMPLES,), 0, 10) < 1).astype(jnp.int32), jax.random.fold_in(seeds[6], 1), 0, 1)
    merged_support_order = jax.vmap(lambda own: jax.random.permutation(own, MERGED_SUPPORTS))(jax.random.split(seeds[7], OVERALL_SAMPLES)).reshape((OVERALL_SAMPLES, MERGED_SUPPORTS)).astype(jnp.int32)
    entry_layer_cast = gaussian(seeds[8], (INPUTS, FEATURES), INPUTS ** -0.5, 0.3125)
    inner_layer_cast = gaussian(seeds[9], (HIDDEN_SIZE, FEATURES), HIDDEN_SIZE ** -0.5, 0.25)
    critic_inner_offsets = gaussian(seeds[10], (2, FEATURES), 0.3, 1.5, (), jnp.float32)
    readout_matrix_cast = gaussian(seeds[11], (HIDDEN_SIZE, PADDED), HIDDEN_SIZE ** -0.5, 0.25, ((1, 4),))
    lagged_entry_layer = gaussian(seeds[12], (INPUTS, FEATURES), INPUTS ** -0.5, 0.3125)
    lagged_inner_layer = gaussian(seeds[13], (HIDDEN_SIZE, FEATURES), HIDDEN_SIZE ** -0.5, 0.25)
    lagged_inner_offsets = gaussian(seeds[14], (2, FEATURES), 0.3, 1.5, (), jnp.float32)
    lagged_readout = gaussian(seeds[15], (HIDDEN_SIZE, PADDED), HIDDEN_SIZE ** -0.5, 0.25, ((1, 4),))
    lagged_readout_offsets = gaussian(seeds[16], (PADDED,), 0.3, 1.5, (), jnp.float32)
    pilot_weights_cast = gaussian(seeds[17], (ACTOR_ROWS, ACTOR_HIDDEN), ACTOR_HIDDEN ** -0.5, 0.375)
    update_counter = jax.random.randint(seeds[18], (1,), 2, 21).astype(jnp.int32)
    entry_layer_main = gaussian(seeds[19], (INPUTS, FEATURES), INPUTS ** -0.5, 0.3125, ((1, 32),), jnp.float32)
    entry_layer_moment_one = gaussian(seeds[20], (INPUTS, FEATURES), (1.7e-7), 2.384185791015625e-06, ((1, 32),), jnp.float32)
    entry_layer_moment_two = jnp.clip(jnp.exp(math.log(9.000000350284799e-15) - 1.40876728 * jax.random.uniform(seeds[21], (INPUTS, FEATURES), jnp.float32) ** block_levels(seeds[21], (INPUTS, FEATURES), ((1, 32),), -0.2, 0.2)), 2.199999944453015e-15, 9.000000350284799e-15)
    inner_layer_main = gaussian(seeds[22], (HIDDEN_SIZE, FEATURES), HIDDEN_SIZE ** -0.5, 0.25, ((1, 32),), jnp.float32)
    inner_layer_moment_one = gaussian(seeds[23], (HIDDEN_SIZE, FEATURES), (5e-7), 7.62939453125e-06, ((1, 32),), jnp.float32)
    inner_layer_moment_two = jnp.clip(jnp.exp(math.log(7.99999985961336e-14) - 1.3862944 * jax.random.uniform(seeds[24], (HIDDEN_SIZE, FEATURES), jnp.float32) ** block_levels(seeds[24], (HIDDEN_SIZE, FEATURES), ((1, 32),), -0.2, 0.2)), 1.99999996490334e-14, 7.99999985961336e-14)
    offset_vector_main = gaussian(seeds[25], (2, FEATURES), 0.3, 1.5, ((1, 32),), jnp.float32)
    offset_moment_one = gaussian(seeds[26], (2, FEATURES), (1e-6), 1.52587890625e-05, ((1, 32),), jnp.float32)
    offset_moment_two = jnp.clip(jnp.exp(math.log(3.199999943845344e-13) - 1.3862944 * jax.random.uniform(seeds[27], (2, FEATURES), jnp.float32) ** block_levels(seeds[27], (2, FEATURES), ((1, 32),), -0.2, 0.2)), 7.99999985961336e-14, 3.199999943845344e-13)
    readout_matrix_main = gaussian(seeds[28], (HIDDEN_SIZE, PADDED), HIDDEN_SIZE ** -0.5, 0.25, ((0, 8), (1, 4)), jnp.float32)
    readout_moment_one = gaussian(seeds[29], (HIDDEN_SIZE, PADDED), (4.4e-5), 0.00061035156, ((0, 8), (1, 4)), jnp.float32)
    readout_moment_two = jnp.clip(jnp.exp(math.log(6.399999974426862e-10) - 1.3862944 * jax.random.uniform(seeds[30], (HIDDEN_SIZE, PADDED), jnp.float32) ** block_levels(seeds[30], (HIDDEN_SIZE, PADDED), ((0, 8), (1, 4)), -0.2, 0.2)), 1.5999999936067155e-10, 6.399999974426862e-10)
    pilot_weights_main = gaussian(seeds[31], (ACTOR_ROWS, ACTOR_HIDDEN), ACTOR_HIDDEN ** -0.5, 0.375, (), jnp.float32)
    pilot_moment_one = gaussian(seeds[32], (ACTOR_ROWS, ACTOR_HIDDEN), (5.5e-4), 0.0078125, (), jnp.float32)
    pilot_moment_two = jnp.clip(jnp.exp(jax.random.uniform(seeds[33], (ACTOR_ROWS, ACTOR_HIDDEN), jnp.float32, math.log(2.5000000292152436e-08), math.log(1.0000000116860974e-07))), 2.5000000292152436e-08, 1.0000000116860974e-07)
    vector_params_main = gaussian(seeds[34], (SMALL_VEC,), 0.3, 1.5, (), jnp.float32)
    vector_moment_one = draw_vector_moment_one(jax.random.fold_in(seeds[40], 71), 0)
    vector_moment_two = draw_vector_moment_two(jax.random.fold_in(seeds[40], 71), 0)
    heat_logarithm_main = jnp.clip(jax.random.uniform(seeds[37], (1,), jnp.float32, -4.0, -3.0), -4.0, -3.0)
    heat_moment_one = jnp.clip(jax.random.uniform(seeds[38], (1,), jnp.float32, 1.5, 5.0), 1.5, 5.0)
    heat_moment_two = jnp.clip(jnp.exp(jax.random.uniform(seeds[39], (1,), jnp.float32, math.log(1.0), math.log(4.0))), 1.0, 4.0)
    return dict(observed_inputs=observed_inputs, chosen_controls=chosen_controls, present_gauss_draw=present_gauss_draw, successor_observations=successor_observations, successor_gauss_draw=successor_gauss_draw, payoffs=payoffs, terminal_indicator=terminal_indicator, merged_support_order=merged_support_order, entry_layer_cast=entry_layer_cast, inner_layer_cast=inner_layer_cast, critic_inner_offsets=critic_inner_offsets, readout_matrix_cast=readout_matrix_cast, lagged_entry_layer=lagged_entry_layer, lagged_inner_layer=lagged_inner_layer, lagged_inner_offsets=lagged_inner_offsets, lagged_readout=lagged_readout, lagged_readout_offsets=lagged_readout_offsets, pilot_weights_cast=pilot_weights_cast, update_counter=update_counter, entry_layer_main=entry_layer_main, entry_layer_moment_one=entry_layer_moment_one, entry_layer_moment_two=entry_layer_moment_two, inner_layer_main=inner_layer_main, inner_layer_moment_one=inner_layer_moment_one, inner_layer_moment_two=inner_layer_moment_two, offset_vector_main=offset_vector_main, offset_moment_one=offset_moment_one, offset_moment_two=offset_moment_two, readout_matrix_main=readout_matrix_main, readout_moment_one=readout_moment_one, readout_moment_two=readout_moment_two, pilot_weights_main=pilot_weights_main, pilot_moment_one=pilot_moment_one, pilot_moment_two=pilot_moment_two, vector_params_main=vector_params_main, vector_moment_one=vector_moment_one, vector_moment_two=vector_moment_two, heat_logarithm_main=heat_logarithm_main, heat_moment_one=heat_moment_one, heat_moment_two=heat_moment_two)


@jax.custom_vjp
def low(v):
    return lax.optimization_barrier(v.astype(jnp.bfloat16)).astype(jnp.float32)

@jax.custom_vjp
def low_back(v):
    return v

def low_keep(v):
    return (low(v), None)

def low_pass(kept, grad):
    return (grad,)

def back_keep(v):
    return (v, None)

def back_low(kept, grad):
    return (low(grad),)
low.defvjp(low_keep, low_pass)
low_back.defvjp(back_keep, back_low)
DISCOUNT = 0.99
BETA_FIRST = 0.9
BETA_SECOND = 0.999
EPSILON = 1e-08
WEIGHT_DECAY = 0.01
RATE_MATRIX = 0.05
RATE_VECTOR = 0.3
STEP_SIZE_SCALE = 0.5
LOG_TWO = math.log(2.0)
HALF_LOG_CIRCLE = 0.5 * math.log(2.0 * math.pi)

def matmul(left, right):
    return jnp.dot(left, right, precision=lax.Precision.HIGHEST, preferred_element_type=jnp.float32)

def owner_mask():
    owner_ids = jnp.arange(PADDED) // QUANTS
    return (owner_ids[None, :] == jnp.arange(CRITICS)[:, None]).astype(jnp.float32)

def admissible_indicator():
    return (jnp.arange(PADDED) < MERGED_SUPPORTS).astype(jnp.float32)

def critic(inputs, entry_weight_tensor, inner_weight_tensor, biases, head, head_bias):
    row_total = inputs.shape[0]
    z_one = low_back(matmul(inputs, entry_weight_tensor) + biases[0])
    h_one = low(jax.nn.relu(z_one))
    z_two = jnp.einsum('rck,kcm->rcm', h_one.reshape(row_total, CRITICS, HIDDEN_SIZE), inner_weight_tensor.reshape(HIDDEN_SIZE, CRITICS, HIDDEN_SIZE), precision=lax.Precision.HIGHEST)
    z_two = low_back(z_two.reshape(row_total, FEATURES) + biases[1])
    h_two = low(jax.nn.relu(z_two))
    expanded = (owner_mask()[:, None, :] * head[None]).reshape(FEATURES, PADDED)
    return low_back(matmul(h_two, expanded) + head_bias * admissible_indicator())

def policy(observed_inputs, weights, small, noise):
    z_one = low_back(matmul(observed_inputs, weights[:OBS_DIM]) + small[:ACTOR_HIDDEN])
    g_one = low(jax.nn.relu(z_one))
    z_two = low_back(matmul(g_one, weights[OBS_DIM:OBS_DIM + ACTOR_HIDDEN]) + small[ACTOR_HIDDEN:2 * ACTOR_HIDDEN])
    g_two = low(jax.nn.relu(z_two))
    output = low_back(matmul(g_two, weights[OBS_DIM + ACTOR_HIDDEN:].T) + small[2 * ACTOR_HIDDEN:2 * ACTOR_HIDDEN + 2 * ACT_DIM])
    means = output[:, :ACT_DIM]
    log_std = output[:, ACT_DIM:]
    pre_tanh = means + jnp.exp(log_std) * noise
    chosen_controls = jnp.tanh(pre_tanh)
    likelihood_logs = lax.optimization_barrier(jnp.sum(-0.5 * noise * noise - log_std - HALF_LOG_CIRCLE - 2.0 * (LOG_TWO - pre_tanh - jax.nn.softplus(-2.0 * pre_tanh)), axis=1))
    return (chosen_controls, likelihood_logs)

def quantile_sum(q_now, lagged_elements, keep_mask):
    levels = ((jnp.arange(PADDED) % QUANTS).astype(jnp.float32) + 0.5) / QUANTS
    diffs = lagged_elements[:, None, :] - q_now[:, :, None]
    weight = jnp.abs(levels[None, :, None] - (diffs < 0).astype(jnp.float32))
    huber_term = jnp.where(jnp.abs(diffs) <= 1.0, 0.5 * diffs * diffs, jnp.abs(diffs) - 0.5)
    return jnp.sum(admissible_indicator()[None, :, None] * keep_mask[:, None, :] * weight * huber_term)

def decoupled_decay_update(master, first, second, gradient, rate, tally):
    first_new = BETA_FIRST * first + (1.0 - BETA_FIRST) * gradient
    second_new = BETA_SECOND * second + (1.0 - BETA_SECOND) * gradient * gradient
    first_hat = first_new / (1.0 - jnp.power(BETA_FIRST, tally))
    second_hat = second_new / (1.0 - jnp.power(BETA_SECOND, tally))
    master_new = master - rate * (first_hat / (jnp.sqrt(second_hat) + EPSILON) + WEIGHT_DECAY * master)
    return (master_new, first_new, second_new)

def add_pair(first, second):
    return first + second

def reference(observed_inputs, chosen_controls, present_gauss_draw, successor_observations, successor_gauss_draw, payoffs, terminal_indicator, merged_support_order, entry_layer_cast, inner_layer_cast, critic_inner_offsets, readout_matrix_cast, lagged_entry_layer, lagged_inner_layer, lagged_inner_offsets, lagged_readout, lagged_readout_offsets, pilot_weights_cast, update_counter, entry_layer_main, entry_layer_moment_one, entry_layer_moment_two, inner_layer_main, inner_layer_moment_one, inner_layer_moment_two, offset_vector_main, offset_moment_one, offset_moment_two, readout_matrix_main, readout_moment_one, readout_moment_two, pilot_weights_main, pilot_moment_one, pilot_moment_two, vector_params_main, vector_moment_one, vector_moment_two, heat_logarithm_main, heat_moment_one, heat_moment_two):
    f32 = jnp.float32
    entry_weight_tensor = entry_layer_cast.astype(f32)
    inner_weight_tensor = inner_layer_cast.astype(f32)
    readout_weight_tensor = readout_matrix_cast.astype(f32)
    pilot_weight_tensor = pilot_weights_cast.astype(f32)
    t_in = lagged_entry_layer.astype(f32)
    t_mid = lagged_inner_layer.astype(f32)
    t_head = lagged_readout.astype(f32)
    disorder_coefficient = jnp.exp(heat_logarithm_main[0])
    head_bias = vector_params_main[SMALL_VEC - PADDED:]
    block_rows = min(OVERALL_SAMPLES, 1024)
    block_count = OVERALL_SAMPLES // block_rows

    def blocks(array):
        return array.reshape((block_count, block_rows) + array.shape[1:])
    parameter_tree = (entry_weight_tensor, inner_weight_tensor, critic_inner_offsets, readout_weight_tensor, vector_params_main, pilot_weight_tensor, heat_logarithm_main)

    def one_block(carry, batch_data):
        grads, loss_sum = carry
        states_b, action_b, noise_b, next_b, noise_next_b, payoff_slice, done_b, rank_b = batch_data
        states_f = states_b.astype(f32)
        next_f = next_b.astype(f32)
        next_act, successor_likelihood_logs = policy(next_f, pilot_weight_tensor, vector_params_main, noise_next_b)
        lagged_return_levels = critic(jnp.concatenate([next_f, low(next_act)], 1), t_in, t_mid, lagged_inner_offsets, t_head, lagged_readout_offsets)
        sample_decay_factors = DISCOUNT * (1.0 - done_b.astype(f32))
        lagged_elements = payoff_slice[:, None] + sample_decay_factors[:, None] * (lagged_return_levels - disorder_coefficient * successor_likelihood_logs[:, None])
        keep_mask = jnp.pad((rank_b < KEPT_ATOMS).astype(f32), ((0, 0), (0, PADDED - MERGED_SUPPORTS)))
        _, fixed_logp = policy(states_f, pilot_weight_tensor, vector_params_main, noise_b)
        entropy_part = (ACT_DIM * block_rows - jnp.sum(fixed_logp)) / OVERALL_SAMPLES

        def block_loss(values):
            p_in, p_mid, p_bias, p_head, p_small, p_actor, p_alpha = values
            q_now = critic(jnp.concatenate([states_f, action_b.astype(f32)], 1), p_in, p_mid, p_bias, p_head, p_small[SMALL_VEC - PADDED:])
            critic_loss = quantile_sum(q_now, lagged_elements, keep_mask) / (OVERALL_SAMPLES * MERGED_SUPPORTS * KEPT_ATOMS)
            new_act, likelihood_logs = policy(states_f, p_actor, p_small, noise_b)
            pilot_return_levels = critic(jnp.concatenate([states_f, low(new_act)], 1), entry_weight_tensor, inner_weight_tensor, critic_inner_offsets, readout_weight_tensor, head_bias)
            pilot_objective = jnp.sum(disorder_coefficient * likelihood_logs - lax.optimization_barrier(jnp.sum(pilot_return_levels * admissible_indicator(), axis=1)) / MERGED_SUPPORTS) / OVERALL_SAMPLES
            return critic_loss + pilot_objective + p_alpha[0] * entropy_part
        value, pullback = jax.vjp(block_loss, parameter_tree)
        block_grads, = pullback(jnp.ones_like(value))
        grads = jax.tree.map(add_pair, grads, block_grads)
        return ((grads, loss_sum + value), None)
    start_grads = jax.tree.map(jnp.zeros_like, parameter_tree)
    batch = (blocks(observed_inputs), blocks(chosen_controls), blocks(present_gauss_draw), blocks(successor_observations), blocks(successor_gauss_draw), blocks(payoffs), blocks(terminal_indicator), blocks(merged_support_order))
    (grads, objective_scalar), _ = lax.scan(one_block, (start_grads, jnp.zeros((), f32)), batch)
    g_in, g_mid, g_bias, g_head, g_small, g_actor, heat_derivative = grads
    tally = update_counter[0].astype(f32)
    in_out = decoupled_decay_update(entry_layer_main, entry_layer_moment_one, entry_layer_moment_two, g_in, RATE_MATRIX, tally)
    mid_out = decoupled_decay_update(inner_layer_main, inner_layer_moment_one, inner_layer_moment_two, g_mid, RATE_MATRIX, tally)
    bias_out = decoupled_decay_update(offset_vector_main, offset_moment_one, offset_moment_two, g_bias, RATE_VECTOR, tally)
    head_out = decoupled_decay_update(readout_matrix_main, readout_moment_one, readout_moment_two, g_head, RATE_MATRIX, tally)
    actor_out = decoupled_decay_update(pilot_weights_main, pilot_moment_one, pilot_moment_two, g_actor, RATE_MATRIX, tally)
    small_out = decoupled_decay_update(vector_params_main, vector_moment_one, vector_moment_two, g_small, RATE_VECTOR, tally)
    heat_result = decoupled_decay_update(heat_logarithm_main, heat_moment_one, heat_moment_two, heat_derivative, STEP_SIZE_SCALE, tally)
    return (objective_scalar, in_out[0], in_out[1], in_out[2], mid_out[0], mid_out[1], mid_out[2], bias_out[0], bias_out[1], bias_out[2], head_out[0], head_out[1], head_out[2], actor_out[0], actor_out[1], actor_out[2], small_out[0], small_out[1], small_out[2], heat_result[0], heat_result[1], heat_result[2])
```

```python
import math

import jax
import jax.numpy as jnp
from jax import lax
from jax.sharding import PartitionSpec as P

OBS_DIM = 376
ACT_DIM = 17
HIDDEN_SIZE = 512
ACTOR_HIDDEN = 256
CRITICS = 5
QUANTS = 25
PADDED = 128
MERGED_SUPPORTS = 125
KEPT_ATOMS = 115
INPUTS = 393
FEATURES = 2560
ACTOR_ROWS = 666
SMALL_VEC = 674
LANES = 1024

DISCOUNT = 0.99
BETA_FIRST = 0.9
BETA_SECOND = 0.999
EPSILON = 1e-08
WEIGHT_DECAY = 0.01
RATE_MATRIX = 0.05
RATE_VECTOR = 0.3
STEP_SIZE_SCALE = 0.5
LOG_TWO = math.log(2.0)
HALF_LOG_CIRCLE = 0.5 * math.log(2.0 * math.pi)
AXES = ("rows", "quant")
BF = jnp.bfloat16
F32 = jnp.float32


def product(left, right):
    return jnp.dot(left, right, preferred_element_type=F32)


def product_t(left, right):
    return lax.dot_general(left, right, (((0,), (0,)), ((), ())), preferred_element_type=F32)


def product_nt(left, right):
    return lax.dot_general(left, right, (((1,), (1,)), ((), ())), preferred_element_type=F32)


def column_sum(values):
    return jnp.sum(values.astype(F32), axis=0)


def exchange(value, flip):
    count = lax.axis_size("rows") * lax.axis_size("quant")
    return lax.ppermute(value, AXES, [(i, i ^ flip) for i in range(count)])


def scatter_sum(pieces):
    total = pieces.shape[0]
    z = total // 8
    view = pieces.reshape((z, 4, 2) + pieces.shape[1:])
    got = exchange(view[:, :, 1], 1)
    view = view[:, :, 0].astype(F32) + got.astype(F32)
    low = view.astype(BF)
    view = view[:, 0] + sum(exchange(low[:, k], 2 * k).astype(F32) for k in (1, 2, 3))
    low = view.astype(BF)
    return view[0] + sum(exchange(low[k], 8 * k).astype(F32) for k in range(1, z))


def all_sum(value):
    total = lax.axis_size("rows") * lax.axis_size("quant")
    flip = 1
    while flip < total:
        value = value + exchange(value, flip)
        flip *= 2
    return value


def all_sum_low(value):
    total = lax.axis_size("rows") * lax.axis_size("quant")
    flip = 1
    while flip < total:
        low = value.astype(BF)
        value = low.astype(F32) + exchange(low, flip).astype(F32)
        flip *= 2
    return value


def split(array, e):
    return array[:, e * HIDDEN_SIZE : (e + 1) * HIDDEN_SIZE]


def hidden_forward(inputs, first, second, biases, e):
    h_one = jax.nn.relu(product(inputs, split(first, e)) + split(biases, e)[0]).astype(BF)
    h_two = jax.nn.relu(product(h_one, split(second, e)) + split(biases, e)[1]).astype(BF)
    return h_one, h_two


def policy_forward(observed_inputs, weights, small, noise):
    g_one = jax.nn.relu(product(observed_inputs, weights[:OBS_DIM]) + small[:ACTOR_HIDDEN]).astype(BF)
    g_two = jax.nn.relu(
        product(g_one, weights[OBS_DIM : OBS_DIM + ACTOR_HIDDEN])
        + small[ACTOR_HIDDEN : 2 * ACTOR_HIDDEN]
    ).astype(BF)
    output = (
        product_nt(g_two, weights[OBS_DIM + ACTOR_HIDDEN :])
        + small[2 * ACTOR_HIDDEN : 2 * ACTOR_HIDDEN + 2 * ACT_DIM]
    )
    log_std = output[:, ACT_DIM:]
    spread = jnp.exp(log_std)
    pre_tanh = output[:, :ACT_DIM] + spread * noise
    act = jnp.tanh(pre_tanh)
    logp = jnp.sum(
        -0.5 * noise * noise
        - log_std
        - HALF_LOG_CIRCLE
        - 2.0 * (LOG_TWO - pre_tanh - jax.nn.softplus(-2.0 * pre_tanh)),
        axis=1,
    )
    return (g_one, g_two, spread, act), logp


def policy_backward(observed_inputs, saved, noise, weights, action_gradient, weight_logp):
    g_one, g_two, spread, act = saved
    grad_pre = action_gradient * (1.0 - act * act) + weight_logp * 2.0 * act
    grad_out = jnp.concatenate([grad_pre, grad_pre * spread * noise - weight_logp], 1).astype(BF)
    g_last = product_t(grad_out, g_two)
    dz_two = jnp.where(g_two > 0, product(grad_out, weights[OBS_DIM + ACTOR_HIDDEN :]), 0.0).astype(BF)
    g_mid = product_t(g_one, dz_two)
    dz_one = jnp.where(
        g_one > 0, product_nt(dz_two, weights[OBS_DIM : OBS_DIM + ACTOR_HIDDEN]), 0.0
    ).astype(BF)
    g_first = product_t(observed_inputs, dz_one)
    grad_weights = jnp.concatenate([g_first, g_mid, g_last], 0)
    grad_biases = jnp.concatenate([column_sum(dz_one), column_sum(dz_two), column_sum(grad_out)])
    return grad_weights, grad_biases


def quantile_terms(q_now, lagged_elements, keep_mask, pair_scale):
    row_total, col_count = q_now.shape
    columns = jnp.arange(col_count)
    levels = ((columns % QUANTS).astype(F32) + 0.5) / QUANTS
    valid_entries = (columns < MERGED_SUPPORTS).astype(F32)
    block_rows = min(row_total, 128)
    block_count = row_total // block_rows

    def pair_block(pieces):
        q_part, target_part, keep_part = pieces
        diffs = target_part[:, None, :] - q_part[:, :, None]
        weight = jnp.abs(levels[None, :, None] - (diffs < 0).astype(F32))
        weight = weight * valid_entries[None, :, None] * keep_part[:, None, :]
        huber_term = jnp.where(jnp.abs(diffs) <= 1.0, 0.5 * diffs * diffs, jnp.abs(diffs) - 0.5)
        return (
            jnp.sum(weight * huber_term),
            -jnp.sum(weight * jnp.clip(diffs, -1.0, 1.0), axis=2) * pair_scale,
        )

    totals, grads = lax.map(
        pair_block,
        (
            q_now.reshape(block_count, block_rows, col_count),
            lagged_elements.reshape(block_count, block_rows, PADDED),
            keep_mask.reshape(block_count, block_rows, PADDED),
        ),
    )
    return jnp.sum(totals) * pair_scale, grads.reshape(row_total, col_count)


def adamw(master, first, second, gradient, rate, tally):
    first_new = BETA_FIRST * first + (1.0 - BETA_FIRST) * gradient
    second_new = BETA_SECOND * second + (1.0 - BETA_SECOND) * gradient * gradient
    first_hat = first_new / (1.0 - jnp.power(BETA_FIRST, tally))
    second_hat = second_new / (1.0 - jnp.power(BETA_SECOND, tally))
    master_new = master - rate * (
        first_hat / (jnp.sqrt(second_hat) + EPSILON) + WEIGHT_DECAY * master
    )
    return (master_new, first_new, second_new)


def local(
    obs, chosen, noise_now, next_obs_all, noise_next_all, payoffs_all, done_all, order_all,
    w_one, w_two, biases, head_part, t_one, t_two, t_biases, t_head_part, t_head_bias,
    actor, counter,
    in_w, in_m, in_v, mid_w, mid_m, mid_v, bias_w, bias_m, bias_v, head_w, head_m, head_v,
    actor_w, actor_m, actor_v, small_w, small_m, small_v, heat, heat_m, heat_v,
):
    n_rows, n_quant = lax.axis_size("rows"), lax.axis_size("quant")
    devices = n_rows * n_quant
    me = lax.axis_index("rows") * n_quant + lax.axis_index("quant")
    rows = obs.shape[0]
    samples = rows * devices
    start = lax.axis_index("quant") * rows
    temperature = jnp.exp(heat[0])
    pair_scale = 1.0 / (samples * MERGED_SUPPORTS * KEPT_ATOMS)
    head_bias = small_w[SMALL_VEC - PADDED :]
    valid = (jnp.arange(PADDED) < MERGED_SUPPORTS).astype(F32)

    heads = jnp.concatenate([head_part.T, t_head_part.T], 1)
    heads = lax.all_gather(heads, "quant", axis=0, tiled=True)
    head_t, t_head_t = heads[:, :HIDDEN_SIZE], heads[:, HIDDEN_SIZE:]

    def mine(array):
        return lax.dynamic_slice_in_dim(array, start, rows, 0)

    next_obs, noise_next = mine(next_obs_all), mine(noise_next_all)
    payoffs, done, order = mine(payoffs_all), mine(done_all), mine(order_all)

    saved, logp_now = policy_forward(obs, actor, small_w, noise_now)
    saved_next, logp_next = policy_forward(next_obs, actor, small_w, noise_next)
    x_target = jnp.concatenate([next_obs, saved_next[3].astype(BF)], 1)
    x_now = jnp.concatenate([obs, chosen], 1)
    x_pi = jnp.concatenate([obs, saved[3].astype(BF)], 1)

    pi_level = jnp.asarray(-1.0 / (MERGED_SUPPORTS * samples), F32).astype(BF)
    pilot_total = rows * jnp.sum(head_bias * valid)
    action_gradient = 0.0
    for e in range(CRITICS):
        head_sum = jnp.sum(head_t[e * QUANTS : (e + 1) * QUANTS].astype(F32), axis=0)
        h_one, h_two = hidden_forward(x_pi, w_one, w_two, biases, e)
        pilot_total = pilot_total + jnp.sum(h_two.astype(F32) * head_sum)
        dz_two = jnp.where(h_two > 0, (head_sum * pi_level.astype(F32)).astype(BF), 0)
        dz_one = jnp.where(h_one > 0, product_nt(dz_two, split(w_two, e)), 0.0).astype(BF)
        action_gradient = action_gradient + product_nt(dz_one, split(w_one, e)[OBS_DIM:])
    g_actor, g_actor_bias = policy_backward(
        obs, saved, noise_now, actor, action_gradient, temperature / samples
    )
    actor_sum = all_sum_low(g_actor)

    target = t_head_bias * valid
    for e in range(CRITICS):
        _, h_two = hidden_forward(x_target, t_one, t_two, t_biases, e)
        part = product_nt(h_two, t_head_t[e * QUANTS : (e + 1) * QUANTS])
        target = target + jnp.pad(part, ((0, 0), (e * QUANTS, PADDED - (e + 1) * QUANTS)))
    decay = DISCOUNT * (1.0 - done.astype(F32))
    lagged = payoffs[:, None] + decay[:, None] * (target - temperature * logp_next[:, None])
    keep = jnp.pad((order < KEPT_ATOMS).astype(F32), ((0, 0), (0, PADDED - MERGED_SUPPORTS)))

    q_now = head_bias * valid
    hidden = []
    for e in range(CRITICS):
        h_one, h_two = hidden_forward(x_now, w_one, w_two, biases, e)
        hidden.append((h_one, h_two))
        part = product_nt(h_two, head_t[e * QUANTS : (e + 1) * QUANTS])
        q_now = q_now + jnp.pad(part, ((0, 0), (e * QUANTS, PADDED - (e + 1) * QUANTS)))
    critic_part, grad_q = quantile_terms(q_now, lagged, keep, pair_scale)
    grad_q = grad_q.astype(BF)

    blocks, head_blocks = [], []
    for e in range(CRITICS):
        h_one, h_two = hidden[e]
        dq = grad_q[:, e * QUANTS : (e + 1) * QUANTS]
        head_e = head_t[e * QUANTS : (e + 1) * QUANTS]
        head_blocks.append(product_t(dq, h_two))
        dz_two = jnp.where(h_two > 0, product(dq, head_e), 0.0).astype(BF)
        dz_one = jnp.where(h_one > 0, product_nt(dz_two, split(w_two, e)), 0.0).astype(BF)
        blocks.append(
            jnp.concatenate(
                [
                    product_t(dz_two, h_one),
                    product_t(dz_one, x_now),
                    column_sum(dz_one)[:, None],
                    column_sum(dz_two)[:, None],
                    jnp.zeros((HIDDEN_SIZE, LANES - HIDDEN_SIZE - INPUTS - 2), F32),
                ],
                1,
            ).astype(BF)
        )
    width = FEATURES // devices
    pieces = jnp.concatenate(blocks, 0).reshape(devices, width, LANES)
    head_grad = jnp.concatenate(head_blocks + [jnp.zeros((3, HIDDEN_SIZE), F32)], 0).astype(BF)
    head_pieces = (
        head_grad.reshape(n_quant, PADDED // n_quant, n_rows, HIDDEN_SIZE // n_rows)
        .transpose(2, 0, 1, 3)
        .reshape(devices, -1, 128)
    )
    order_of = me ^ jnp.arange(devices)
    own = scatter_sum(jnp.take(pieces, order_of, axis=0))
    own_head = scatter_sum(jnp.take(head_pieces, order_of, axis=0))
    own_head = own_head.reshape(PADDED // n_quant, HIDDEN_SIZE // n_rows).T
    mid_grad = own[:, :HIDDEN_SIZE].T
    in_grad = own[:, HIDDEN_SIZE : HIDDEN_SIZE + INPUTS].T
    bias_grad = own[:, HIDDEN_SIZE + INPUTS : HIDDEN_SIZE + INPUTS + 2].T

    actor_share = (temperature * jnp.sum(logp_now) - pilot_total / MERGED_SUPPORTS) / samples
    small = jnp.concatenate(
        [
            g_actor_bias,
            column_sum(grad_q),
            jnp.stack([critic_part, actor_share, jnp.sum(logp_now)]),
            jnp.zeros((LANES - SMALL_VEC - 3,), F32),
        ]
    )
    small = all_sum(small.reshape(8, 128)).reshape(-1)
    small_grad = small[:SMALL_VEC]
    shortfall = (ACT_DIM * samples - small[SMALL_VEC + 2]) / samples
    objective = small[SMALL_VEC] + small[SMALL_VEC + 1] + heat[0] * shortfall
    tally = counter[0].astype(F32)
    return (
        objective,
        *adamw(in_w, in_m, in_v, in_grad, RATE_MATRIX, tally),
        *adamw(mid_w, mid_m, mid_v, mid_grad, RATE_MATRIX, tally),
        *adamw(bias_w, bias_m, bias_v, bias_grad, RATE_VECTOR, tally),
        *adamw(head_w, head_m, head_v, own_head, RATE_MATRIX, tally),
        *adamw(actor_w, actor_m, actor_v, actor_sum, RATE_MATRIX, tally),
        *adamw(small_w, small_m, small_v, small_grad, RATE_VECTOR, tally),
        *adamw(heat, heat_m, heat_v, jnp.reshape(shortfall, (1,)), STEP_SIZE_SCALE, tally),
    )


def solution(mesh):
    both, row, none = P(AXES), P("rows"), P()
    column, shard = P(None, "quant"), P(None, AXES)
    placed = (
        (both,) * 3 + (row,) * 5 + (none,) * 3 + (column,) + (none,) * 3 + (column,) + (none,) * 3
        + (shard,) * 9 + (P("rows", "quant"),) * 3 + (none,) * 9
    )
    return jax.shard_map(
        local,
        mesh=mesh,
        in_specs=placed,
        out_specs=(none,) + (shard,) * 9 + (P("rows", "quant"),) * 3 + (none,) * 9,
        check_vma=False,
    )
```

```python
import functools
import math

import jax
import jax.numpy as jnp
import ml_dtypes
import numpy as np
from jax import lax
from jax.experimental import pallas as pl
from jax.experimental.pallas import tpu as pltpu
from jax.sharding import PartitionSpec as P

OBS_DIM = 376
ACT_DIM = 17
HIDDEN_SIZE = 512
ACTOR_HIDDEN = 256
CRITICS = 5
QUANTS = 25
SLOT = 32
PADDED = 128
MERGED_SUPPORTS = 125
KEPT_ATOMS = 115
INPUTS = 393
FEATURES = 2560
SMALL_VEC = 674
LANES = 1024
EXTRA = 128
TILE = 512
MiB = 1024 * 1024

DISCOUNT = 0.99
BETA_FIRST = 0.9
BETA_SECOND = 0.999
EPSILON = 1e-08
WEIGHT_DECAY = 0.01
RATE_MATRIX = 0.05
RATE_VECTOR = 0.3
STEP_SIZE_SCALE = 0.5
LOG_TWO = math.log(2.0)
HALF_LOG_CIRCLE = 0.5 * math.log(2.0 * math.pi)
AXES = ("rows", "quant")
BF = jnp.bfloat16
F32 = jnp.float32
WHOLE = pl.BlockSpec(memory_space=pltpu.VMEM)
SCALAR = pl.BlockSpec(memory_space=pltpu.SMEM)


def dot_nn(left, right):
    return jnp.dot(left, right, preferred_element_type=F32)


def dot_tn(left, right):
    return lax.dot_general(left, right, (((0,), (0,)), ((), ())), preferred_element_type=F32)


def dot_nt(left, right):
    return lax.dot_general(left, right, (((1,), (1,)), ((), ())), preferred_element_type=F32)


def params(limit=48, steps=0):
    semantics = ("arbitrary",) * steps if steps else None
    return pltpu.CompilerParams(vmem_limit_bytes=limit * MiB, dimension_semantics=semantics)


def cost(flops, moved):
    return pl.CostEstimate(flops=int(flops), bytes_accessed=int(moved), transcendentals=0)


def column(row):
    return jnp.transpose(jnp.broadcast_to(row, (8, row.shape[1])))[:, :1]


def actor_kernel(
    index, obs, next_obs, noise_now, noise_next, actor, small,
    g_one_out, g_two_out, act_out, scaled_out, next_act_out, logp_out, out_scratch,
):
    s_one = column(small[:, :ACTOR_HIDDEN])
    s_two = column(small[:, ACTOR_HIDDEN : 2 * ACTOR_HIDDEN])
    s_three = column(small[:, 2 * ACTOR_HIDDEN : 2 * ACTOR_HIDDEN + PADDED])[: 2 * ACT_DIM]
    first = actor[:OBS_DIM]
    second = actor[OBS_DIM : OBS_DIM + ACTOR_HIDDEN]
    third = actor[OBS_DIM + ACTOR_HIDDEN :]
    for which, (inputs, noise) in enumerate(((obs, noise_now), (next_obs, noise_next))):
        g_one = jnp.maximum(dot_tn(first, inputs[...]) + s_one, 0.0).astype(BF)
        g_two = jnp.maximum(dot_tn(second, g_one) + s_two, 0.0).astype(BF)
        out_scratch[: 2 * ACT_DIM] = dot_nn(third, g_two) + s_three
        mean = out_scratch[:ACT_DIM]
        log_std = out_scratch[ACT_DIM : 2 * ACT_DIM]
        draw = noise[...]
        scaled = jnp.exp(log_std) * draw
        pre = mean + scaled
        act = jnp.tanh(pre)
        soft = jnp.maximum(-2.0 * pre, 0.0) + jnp.log(1.0 + jnp.exp(-2.0 * jnp.abs(pre)))
        logp = jnp.sum(
            -0.5 * draw * draw - log_std - HALF_LOG_CIRCLE - 2.0 * (LOG_TWO - pre - soft),
            axis=0,
            keepdims=True,
        )
        logp_out[which : which + 1] = logp
        if which == 0:
            g_one_out[...] = g_one
            g_two_out[...] = g_two
            act_out[...] = act
            scaled_out[...] = scaled
        else:
            next_act_out[...] = act


def actor_forward(index, obs, next_obs, noise_now, noise_next, actor, small):
    rows = obs.shape[1]
    whole = lambda shape: pl.BlockSpec(shape, lambda i, ix: (0, 0))
    part = lambda shape: pl.BlockSpec(shape, lambda i, ix: (0, ix[0]))
    return pl.pallas_call(
        actor_kernel,
        grid_spec=pltpu.PrefetchScalarGridSpec(
            num_scalar_prefetch=1,
            grid=(1,),
            in_specs=[
                whole((OBS_DIM, rows)), part((OBS_DIM, rows)), whole((ACT_DIM, rows)),
                part((ACT_DIM, rows)), whole(actor.shape), whole(small.shape),
            ],
            out_specs=[
                whole((ACTOR_HIDDEN, rows)), whole((ACTOR_HIDDEN, rows)), whole((ACT_DIM, rows)),
                whole((ACT_DIM, rows)), whole((ACT_DIM, rows)), whole((2, rows)),
            ],
            scratch_shapes=[pltpu.VMEM((40, rows), F32)],
        ),
        out_shape=[
            jax.ShapeDtypeStruct((ACTOR_HIDDEN, rows), BF),
            jax.ShapeDtypeStruct((ACTOR_HIDDEN, rows), BF),
            jax.ShapeDtypeStruct((ACT_DIM, rows), F32),
            jax.ShapeDtypeStruct((ACT_DIM, rows), F32),
            jax.ShapeDtypeStruct((ACT_DIM, rows), F32),
            jax.ShapeDtypeStruct((2, rows), F32),
        ],
        compiler_params=params(),
        cost_estimate=cost(0.7e9, 4e6),
        name="actor_forward",
    )(index, obs, next_obs, noise_now, noise_next, actor, small)


def heads_kernel(me, own, got_one, got_two, got_three, small, lag_bias, out, bias_out, stage, col):
    quarter = own.shape[0]
    for k, got in enumerate((own, got_one, got_two, got_three)):
        first = pl.multiple_of((me[0] ^ k) * quarter, quarter)
        stage[pl.ds(first, quarter)] = got[...].astype(F32)
    keep = lax.broadcasted_iota(jnp.int32, (SLOT, 1), 0) < QUANTS
    bias = small[:, SMALL_VEC - PADDED :]
    both = jnp.concatenate([bias, lag_bias[...], jnp.zeros((6, PADDED), F32)], 0)
    col[:PADDED] = jnp.transpose(both)
    for e in range(CRITICS):
        rows = pl.ds(e * QUANTS, SLOT)
        out[e] = jnp.where(keep, stage[rows], 0.0).astype(BF)
        columns = jnp.where(keep, col[rows], 0.0)
        for net in range(2):
            bias_out[net, e] = jnp.broadcast_to(columns[:, net : net + 1], (SLOT, PADDED))


def heads(me, own, got, small, lag_bias):
    return pl.pallas_call(
        heads_kernel,
        in_specs=[SCALAR] + [WHOLE] * 6,
        out_specs=[WHOLE, WHOLE],
        out_shape=[
            jax.ShapeDtypeStruct((CRITICS, SLOT, 2 * HIDDEN_SIZE), BF),
            jax.ShapeDtypeStruct((2, CRITICS, SLOT, PADDED), F32),
        ],
        scratch_shapes=[pltpu.VMEM((136, 2 * HIDDEN_SIZE), F32), pltpu.VMEM((136, 8), F32)],
        compiler_params=params(),
        cost_estimate=cost(1e6, 1e6),
        name="heads",
    )(me, own, *got, small, lag_bias)


def fill_inputs(tall, inputs, obs, act):
    rows = obs.shape[1]
    body = OBS_DIM // 16 * 16
    inputs[:body] = obs[:body]
    tall[:8] = obs[body:OBS_DIM].astype(F32)
    tall[8 : 8 + ACT_DIM] = act.astype(F32)
    tall[8 + ACT_DIM : 32] = jnp.zeros((24 - ACT_DIM, rows), F32)
    tall[8 + ACT_DIM : 11 + ACT_DIM] = jnp.ones((3, rows), F32)
    inputs[body : body + 32] = tall[...].astype(BF)
    inputs[body + 32 :] = jnp.zeros((HIDDEN_SIZE - body - 32, rows), BF)


def fill_first(tall, filled, first, bias):
    body = INPUTS // 16 * 16
    high = bias.astype(BF).astype(F32)
    middle = (bias - high).astype(BF).astype(F32)
    filled[:body] = first[:body]
    tall[: INPUTS - body] = first[body:].astype(F32)
    tall[INPUTS - body : 32] = jnp.zeros((32 - INPUTS + body, HIDDEN_SIZE), F32)
    tall[INPUTS - body : INPUTS - body + 1] = high
    tall[INPUTS - body + 1 : INPUTS - body + 2] = middle
    tall[INPUTS - body + 2 : INPUTS - body + 3] = bias - high - middle
    filled[body : body + 32] = tall[...].astype(BF)
    filled[body + 32 :] = jnp.zeros((HIDDEN_SIZE - body - 32, HIDDEN_SIZE), BF)


def tiles(rows):
    width = min(rows, TILE)
    return [pl.ds(i * width, width) for i in range(rows // width)]


def pack(packed, slots):
    for e in range(CRITICS):
        packed[e * QUANTS : e * QUANTS + SLOT] = slots[e * SLOT : (e + 1) * SLOT]


def target_kernel(
    heat, obs, act, logp, payoffs, done, order, first, second, bias, head, head_bias,
    lagged, keep, inputs, filled, tall_x, tall_w, slots, packed,
):
    rows = act.shape[1]
    step = pl.program_id(0)

    @pl.when(step == 0)
    def _():
        fill_inputs(tall_x, inputs, obs[...], act[...].astype(BF))
        for i in range(rows // PADDED):
            part = pl.ds(i * PADDED, PADDED)
            kept = (order[part] < KEPT_ATOMS).astype(F32)
            kept = jnp.concatenate([kept, jnp.zeros((PADDED, PADDED - MERGED_SUPPORTS), F32)], 1)
            keep[:, part] = jnp.transpose(kept).astype(BF)

    fill_first(tall_w, filled, first[...], bias[:1])
    b_two = column(bias[1:2])
    for part in tiles(rows):
        h_one = jnp.maximum(dot_tn(filled[...], inputs[:, part]), 0.0).astype(BF)
        h_two = jnp.maximum(dot_tn(second[...], h_one) + b_two, 0.0).astype(BF)
        slots[pl.ds(pl.multiple_of(step * SLOT, SLOT), SLOT), part] = (
            dot_nn(head[0], h_two) + head_bias[0, 0, :, :1]
        )

    @pl.when(step == CRITICS - 1)
    def _():
        pack(packed, slots)
        decay = DISCOUNT * (1.0 - done[...].astype(F32))
        temperature = jnp.exp(jnp.full((1, 1), heat[0], F32))
        lagged[...] = payoffs[...] + decay * (packed[:PADDED] - temperature * logp[1:2])


def critic_specs(rows, net, base=0):
    lanes = lambda count: pl.BlockSpec((count, HIDDEN_SIZE), lambda e: (0, base + e))
    return [
        lanes(INPUTS), lanes(HIDDEN_SIZE), lanes(2),
        pl.BlockSpec((1, SLOT, HIDDEN_SIZE), lambda e: (base + e, 0, net)),
        pl.BlockSpec((1, 1, SLOT, PADDED), lambda e: (net, base + e, 0, 0)),
    ]


def target_pass(index, heat, next_obs, act, logp, payoffs, done, order, first, second, bias, head, head_bias):
    rows = act.shape[1]
    add = lambda spec: pl.BlockSpec(spec.block_shape, lambda e, ix, f=spec.index_map: f(e))
    fixed = lambda shape: pl.BlockSpec(shape, lambda e, ix: (0, 0))
    mine = lambda shape: pl.BlockSpec(shape, lambda e, ix: (0, ix[0]))
    return pl.pallas_call(
        lambda ix, *refs: target_kernel(*refs),
        grid_spec=pltpu.PrefetchScalarGridSpec(
            num_scalar_prefetch=1,
            grid=(CRITICS,),
            in_specs=[
                SCALAR, mine((OBS_DIM, rows)), fixed((ACT_DIM, rows)), fixed((2, rows)),
                mine((1, rows)), mine((1, rows)),
                pl.BlockSpec((rows, MERGED_SUPPORTS), lambda e, ix: (ix[0], 0)),
            ]
            + [add(spec) for spec in critic_specs(rows, 1)],
            out_specs=[fixed((PADDED, rows)), fixed((PADDED, rows))],
            scratch_shapes=[
                pltpu.VMEM((HIDDEN_SIZE, rows), BF),
                pltpu.VMEM((HIDDEN_SIZE, HIDDEN_SIZE), BF),
                pltpu.VMEM((32, rows), F32),
                pltpu.VMEM((32, HIDDEN_SIZE), F32),
                pltpu.VMEM((CRITICS * SLOT, rows), F32),
                pltpu.VMEM((136, rows), F32),
            ],
        ),
        out_shape=[jax.ShapeDtypeStruct((PADDED, rows), F32), jax.ShapeDtypeStruct((PADDED, rows), BF)],
        compiler_params=params(steps=1),
        cost_estimate=cost(7e9, 7e6),
        name="target_pass",
    )(index, heat, next_obs, act, logp, payoffs, done, order, first, second, bias, head, head_bias)


HALF = 336


def two_terms(value):
    high = value.astype(BF).astype(F32)
    both = jnp.concatenate([high, value - high], 1)
    return jnp.concatenate([both, jnp.zeros((8, 2 * PADDED), F32)], 0).astype(BF)


def pilot_kernel(
    level, share, me, heat, obs, act, scaled, logp, g_one, g_two, actor, first, second, bias, head, head_bias,
    own_out, send_out, inputs, filled, tall_x, tall_w, dact, total, tail, dout_scratch, grad_out, small_out,
):
    rows = obs.shape[1]
    step = pl.program_id(0)

    @pl.when(step == 0)
    def _():
        fill_inputs(tall_x, inputs, obs[...], act[...].astype(BF))
        dact[...] = jnp.zeros(dact.shape, F32)
        total[...] = jnp.zeros(total.shape, F32)
        tail[...] = jnp.zeros(tail.shape, F32)

    fill_first(tall_w, filled, first[...], bias[:1])
    b_two = column(bias[1:2])
    head_sum = jnp.sum(head[0].astype(F32), axis=0, keepdims=True)
    weight = column(head_sum)
    push = column(head_sum * level)
    tail[...] += head_bias[0, 0]
    for part in tiles(rows):
        h_one = jnp.maximum(dot_tn(filled[...], inputs[:, part]), 0.0).astype(BF)
        h_two = jnp.maximum(dot_tn(second[...], h_one) + b_two, 0.0)
        weighted = h_two * weight
        total[:, part] += jnp.sum(weighted.reshape(-1, 8, weighted.shape[1]), axis=0)
        dz_two = jnp.where(h_two > 0, push, 0.0).astype(BF)
        grad = dot_nn(second[...], dz_two)
        dz_one = jnp.where(h_one > 0, grad, 0.0).astype(BF)
        dact[:, part] += dot_nn(first[OBS_DIM // 16 * 16 :], dz_one)

    @pl.when(step == CRITICS - 1)
    def _():
        temperature_share = jnp.exp(jnp.full((1, 1), heat[0], F32)) * share
        skip = OBS_DIM % 16
        action_grad = dact[skip : skip + ACT_DIM]
        value = act[...]
        pre = action_grad * (1.0 - value * value) + 2.0 * temperature_share * value
        dout_scratch[:ACT_DIM] = pre
        dout_scratch[ACT_DIM : 2 * ACT_DIM] = pre * scaled[...] - temperature_share
        dout = dout_scratch[: 2 * ACT_DIM].astype(BF)
        a_two = actor[OBS_DIM : OBS_DIM + ACTOR_HIDDEN]
        a_three = actor[OBS_DIM + ACTOR_HIDDEN :]
        two, one = g_two[...], g_one[...]
        dz_two = jnp.where(two > 0, dot_tn(a_three, dout), 0.0).astype(BF)
        dz_one = jnp.where(one > 0, dot_nn(a_two, dz_two), 0.0).astype(BF)
        grad_out[OBS_DIM + ACTOR_HIDDEN : OBS_DIM + ACTOR_HIDDEN + 2 * ACT_DIM] = dot_nt(dout, two)
        grad_out[OBS_DIM + ACTOR_HIDDEN + 2 * ACT_DIM :] = jnp.zeros((6, ACTOR_HIDDEN), F32)
        grad_out[OBS_DIM : OBS_DIM + ACTOR_HIDDEN] = dot_nt(one, dz_two)
        grad_out[:OBS_DIM] = dot_nt(obs[...], dz_one)
        ones = jnp.ones((16, rows), BF)
        small_out[...] = jnp.zeros(small_out.shape, F32)
        sum_one = dot_nt(ones, dz_one)[:1]
        sum_two = dot_nt(ones, dz_two)[:1]
        small_out[0:1] = sum_one[:, :PADDED]
        small_out[1:2] = sum_one[:, PADDED:]
        small_out[2:3] = sum_two[:, :PADDED]
        small_out[3:4] = sum_two[:, PADDED:]
        small_out[4:5, : 2 * ACT_DIM] = dot_nt(ones, dout)[:1]
        pilot_total = jnp.sum(total[...]) + rows * jnp.sum(tail[:, :1])
        small_out[5:6] = jnp.broadcast_to(pilot_total, (1, PADDED))
        small_out[6:7] = jnp.broadcast_to(jnp.sum(logp[:1]), (1, PADDED))
        packed = two_terms(small_out[...])
        side = me[0] & 1
        for out, which in ((own_out, side), (send_out, 1 - side)):
            out[:HALF] = grad_out[pl.ds(pl.multiple_of(which * HALF, 16), HALF)].astype(BF)
            out[HALF:] = packed


def pilot_pass(level, share, me, heat, obs, act, scaled, logp, g_one, g_two, actor, first, second, bias, head, head_bias):
    rows = obs.shape[1]
    whole = lambda array: pl.BlockSpec(array.shape, lambda e: (0, 0))
    return pl.pallas_call(
        functools.partial(pilot_kernel, level, share),
        grid=(CRITICS,),
        in_specs=[SCALAR, SCALAR]
        + [whole(a) for a in (obs, act, scaled, logp, g_one, g_two, actor)]
        + critic_specs(rows, 0),
        out_specs=[pl.BlockSpec((HALF + 16, ACTOR_HIDDEN), lambda e: (0, 0))] * 2,
        out_shape=[jax.ShapeDtypeStruct((HALF + 16, ACTOR_HIDDEN), BF)] * 2,
        scratch_shapes=[
            pltpu.VMEM((HIDDEN_SIZE, rows), BF),
            pltpu.VMEM((HIDDEN_SIZE, HIDDEN_SIZE), BF),
            pltpu.VMEM((32, rows), F32),
            pltpu.VMEM((32, HIDDEN_SIZE), F32),
            pltpu.VMEM((INPUTS - OBS_DIM // 16 * 16, rows), F32),
            pltpu.VMEM((8, rows), F32),
            pltpu.VMEM((SLOT, PADDED), F32),
            pltpu.VMEM((40, rows), F32),
            pltpu.VMEM((2 * HALF, ACTOR_HIDDEN), F32),
            pltpu.VMEM((8, PADDED), F32),
        ],
        compiler_params=params(steps=1),
        cost_estimate=cost(10e9, 9e6),
        name="pilot_pass",
    )(me, heat, obs, act, scaled, logp, g_one, g_two, actor, first, second, bias, head, head_bias)


def pair_terms(q_ref, lagged, keep, dq_ref, scale, rows):
    dq_ref[QUANTS:] = jnp.zeros((SLOT - QUANTS, rows), F32)

    def group(i, loss):
        part = pl.ds(pl.multiple_of(i * PADDED, PADDED), PADDED)
        q = q_ref[:, part]
        shift = jnp.sum(q, axis=0, keepdims=True) * (1.0 / QUANTS)
        y = (lagged[:, part] - shift).astype(BF).reshape(8, 16, PADDED)
        upper = keep[:, part].reshape(8, 16, PADDED)
        lower = -upper
        q = q - shift
        for j in range(QUANTS):
            level = jnp.broadcast_to(q[j : j + 1], (16, PADDED)).astype(BF)
            d = y - level[None]
            c = jnp.minimum(jnp.maximum(d, lower), upper)
            half = c * jnp.asarray(0.5, BF)
            weighted = half + jnp.abs(c) * jnp.asarray((j + 0.5) / QUANTS - 0.5, BF)
            h = weighted * (d - half)
            g = weighted[:4] + weighted[4:]
            g = g[:2] + g[2:]
            g = (g[0] + g[1]).astype(F32)
            h = h[:4] + h[4:]
            h = h[:2] + h[2:]
            h = (h[0] + h[1]).astype(F32)
            loss = loss + h[:8] + h[8:]
            dq_ref[j : j + 1, part] = jnp.sum(g, axis=0, keepdims=True) * (-scale)
        return loss

    return lax.fori_loop(0, rows // PADDED, group, jnp.zeros((8, PADDED), F32))


def critic_kernel(
    count, last, rows_scale, split,
    me, obs, act, lagged, keep, first, second, bias, head, head_bias, *refs,
):
    if last:
        dq_before, dh_before, loss_before = refs[:3]
        refs = refs[3:]
    outs, scratch = refs[:-14], refs[-14:]
    inputs, filled, tall_x, tall_w, h_one, h_two, q, dq, grads, dq_all, dh_all, loss_all = scratch[:12]
    dq_packed, dh_packed = scratch[12:]
    rows = obs.shape[1]
    step = pl.program_id(0)

    @pl.when(step == 0)
    def _():
        fill_inputs(tall_x, inputs, obs[...], act[...])
        if last:
            dq_all[...] = dq_before[...]
            dh_all[...] = dh_before[...]
            loss_all[...] = loss_before[...]
        else:
            loss_all[...] = jnp.zeros(loss_all.shape, F32)
            dh_all[...] = jnp.zeros(dh_all.shape, F32)
            dq_all[...] = jnp.zeros(dq_all.shape, F32)

    fill_first(tall_w, filled, first[...], bias[:1])
    b_two = column(bias[1:2])
    for part in tiles(rows):
        one = jnp.maximum(dot_tn(filled[...], inputs[:, part]), 0.0).astype(BF)
        h_one[:, part] = one
        two = jnp.maximum(dot_tn(second[...], one) + b_two, 0.0).astype(BF)
        h_two[:, part] = two
        q[:, part] = dot_nn(head[0], two) + head_bias[0, 0, :, :1]
    loss_all[...] += pair_terms(q, lagged, keep, dq, rows_scale, rows)
    base = (CRITICS - count if last else 0) * SLOT
    low = dq[...].astype(BF)
    slot = pl.ds(pl.multiple_of(base + step * SLOT, SLOT), SLOT)
    dq_all[slot] = low.astype(F32)
    dh_all[slot] = dot_nt(low, h_two[...])
    sums = jnp.zeros((HIDDEN_SIZE, PADDED), F32)
    for part in tiles(rows):
        two = h_two[:, part]
        dz_two = jnp.where(two > 0, dot_tn(head[0], low[:, part.start : part.start + part.size]), 0.0)
        for i in range(part.size // PADDED):
            sums = sums + dz_two[:, i * PADDED : (i + 1) * PADDED]
        dz_two = dz_two.astype(BF)
        h_two[:, part] = dz_two
        one = h_one[:, part]
        dz_one = jnp.where(one > 0, dot_nn(second[...], dz_two), 0.0).astype(BF)
        part_grad = dot_nt(dz_one, inputs[:, part])
        if part.start:
            first_grad += part_grad
            second_grad += dot_nt(dz_two, one)
        else:
            first_grad = part_grad
            second_grad = dot_nt(dz_two, one)
    grads[:, :, :HIDDEN_SIZE] = second_grad.astype(BF).reshape(-1, 16, HIDDEN_SIZE)
    grads[:, :, HIDDEN_SIZE : LANES - PADDED] = (
        first_grad[:, : HIDDEN_SIZE - PADDED].astype(BF).reshape(-1, 16, HIDDEN_SIZE - PADDED)
    )
    lane = lax.broadcasted_iota(jnp.int32, (HIDDEN_SIZE, PADDED), 1)
    tail = jnp.where(
        lane == INPUTS + 1 - HIDDEN_SIZE + PADDED,
        jnp.sum(sums, axis=1, keepdims=True),
        first_grad[:, HIDDEN_SIZE - PADDED :],
    )
    grads[:, :, LANES - PADDED : LANES] = tail.astype(BF).reshape(-1, 16, PADDED)
    sent, kept = outs[0], outs[1]
    pieces = HIDDEN_SIZE // 16
    for k in range(pieces):
        source = me[0] ^ k
        target = kept if k % 2 == 0 else sent
        target[k // 2 % 4, k // 8, step, :, :LANES] = grads[source, :, :LANES]

    @pl.when(step == count - 1)
    def _():
        if last:
            n_rows, n_quant = split
            pack(dq_packed, dq_all)
            pack(dh_packed, dh_all)
            ones = jnp.ones((8, rows), BF)
            dq_low = dq_packed[:PADDED].astype(BF)
            sums_row = dot_nt(ones, dq_low)[:1]
            loss = jnp.full((1, PADDED), jnp.sum(loss_all[...]) * rows_scale, F32)
            extra = jnp.concatenate([sums_row, loss, jnp.zeros((14, PADDED), F32)], 0).astype(BF)
            if not n_rows:
                outs[2][...] = dh_packed[:PADDED]
                outs[3][...] = jnp.concatenate([sums_row, loss, jnp.zeros((6, PADDED), F32)], 0)
                return
            width = HIDDEN_SIZE // n_rows
            high = PADDED // n_quant
            dh = dh_packed[:PADDED].astype(BF).astype(F32)
            for r in range(n_rows):
                for c in range(n_quant):
                    block = dh[c * high : (c + 1) * high, r * width : (r + 1) * width]
                    block = jnp.concatenate([block[:16], block[16:]], 1)
                    grads[r * n_quant + c, :, LANES:] = block.astype(BF)
            for k in range(pieces):
                target = kept if k % 2 == 0 else sent
                target[k // 2 % 4, k // 8, 0, :, LANES:] = grads[me[0] ^ k, :, LANES:]
                target[k // 2 % 4, k // 8, 1, :, LANES:] = extra
        else:
            outs[2][...] = dq_all[...]
            outs[3][...] = dh_all[...]
            outs[4][...] = loss_all[...]


def critic_pass(base, count, last, rows_scale, split, me, obs, act, lagged, keep, first, second, bias, head, head_bias, before):
    rows = obs.shape[1]
    fixed = lambda array: pl.BlockSpec(array.shape, lambda e, n=array.ndim: (0,) * n)
    lanes = LANES + (EXTRA if last and split[0] else 0)
    pieces = jax.ShapeDtypeStruct((4, HIDDEN_SIZE // 128, count, 16, lanes), BF)
    out_shape = [pieces, pieces]
    if not last:
        out_shape += [
            jax.ShapeDtypeStruct((CRITICS * SLOT, rows), F32),
            jax.ShapeDtypeStruct((CRITICS * SLOT, HIDDEN_SIZE), F32),
            jax.ShapeDtypeStruct((8, PADDED), F32),
        ]
    elif not split[0]:
        out_shape += [
            jax.ShapeDtypeStruct((PADDED, HIDDEN_SIZE), F32),
            jax.ShapeDtypeStruct((8, PADDED), F32),
        ]
    return pl.pallas_call(
        functools.partial(critic_kernel, count, last, rows_scale, split),
        grid=(count,),
        in_specs=[SCALAR]
        + [fixed(a) for a in (obs, act, lagged, keep)]
        + critic_specs(rows, 0, base)
        + [fixed(a) for a in before],
        out_specs=[fixed(a) for a in out_shape],
        out_shape=out_shape,
        scratch_shapes=[
            pltpu.VMEM((HIDDEN_SIZE, rows), BF),
            pltpu.VMEM((HIDDEN_SIZE, HIDDEN_SIZE), BF),
            pltpu.VMEM((32, rows), F32),
            pltpu.VMEM((32, HIDDEN_SIZE), F32),
            pltpu.VMEM((HIDDEN_SIZE, rows), BF),
            pltpu.VMEM((HIDDEN_SIZE, rows), BF),
            pltpu.VMEM((SLOT, rows), F32),
            pltpu.VMEM((SLOT, rows), F32),
            pltpu.VMEM((HIDDEN_SIZE // 16, 16, lanes), BF),
            pltpu.VMEM((CRITICS * SLOT, rows), F32),
            pltpu.VMEM((CRITICS * SLOT, HIDDEN_SIZE), F32),
            pltpu.VMEM((8, PADDED), F32),
            pltpu.VMEM((136, rows), F32),
            pltpu.VMEM((136, HIDDEN_SIZE), F32),
        ],
        compiler_params=params(steps=1),
        cost_estimate=cost(8e9 * count, 4e6 * count),
        name="critic_pass",
    )(me, obs, act, lagged, keep, first, second, bias, head, head_bias, *before)


def add_kernel(a, b, out):
    out[:HALF] = (a[:HALF].astype(F32) + b[:HALF].astype(F32)).astype(BF)
    pair = [r[HALF:].astype(F32) for r in (a, b)]
    pair = [p[:8, :PADDED] + p[:8, PADDED:] for p in pair]
    out[HALF:] = two_terms(pair[0] + pair[1])


def add_actor(a, b):
    return pl.pallas_call(
        add_kernel,
        in_specs=[WHOLE, WHOLE],
        out_specs=WHOLE,
        out_shape=jax.ShapeDtypeStruct(a.shape, BF),
        compiler_params=params(),
        cost_estimate=cost(1e5, 6e5),
        name="add_actor",
    )(a, b)


def core_kernel(kept, got, *outs):
    for k in range(4):
        outs[k][...] = (kept[k].astype(F32) + got[k].astype(F32)).astype(BF)


def add_core(kept, got):
    return pl.pallas_call(
        core_kernel,
        in_specs=[WHOLE, WHOLE],
        out_specs=[WHOLE] * 4,
        out_shape=[jax.ShapeDtypeStruct(kept.shape[1:], BF)] * 4,
        compiler_params=params(),
        cost_estimate=cost(1e6, 3 * kept.size),
        name="add_core",
    )(kept, got)


def tree(values):
    while len(values) > 1:
        values = [a + b for a, b in zip(values[::2], values[1::2])]
    return values[0]


def square_kernel(*refs):
    sums = tree([r[...].astype(F32) for r in refs[:4]]).astype(BF)
    for k, out in enumerate(refs[4:]):
        out[...] = sums[k]


def add_square(parts):
    z = parts[0].shape[0]
    return pl.pallas_call(
        square_kernel,
        in_specs=[WHOLE] * 4,
        out_specs=[WHOLE] * z,
        out_shape=[jax.ShapeDtypeStruct(parts[0].shape[1:], BF)] * z,
        compiler_params=params(),
        cost_estimate=cost(1e6, 6 * parts[0].size),
        name="add_square",
    )(*parts)


def last_kernel(count, z, which, *refs):
    early, late = refs[:z], refs[z : 2 * z]
    blocks, head, row, every = refs[2 * z : 2 * z + 5], refs[-3], refs[-2], refs[-1]
    every[:count] = tree([r[...].astype(F32) for r in early]).astype(BF)
    sums = tree([r[...].astype(F32) for r in late])
    every[count:] = sums[:, :, :LANES].astype(BF)
    extra = sums[:, :, LANES:]
    head[...] = jnp.concatenate([extra[0, :, : PADDED // 2], extra[0, :, PADDED // 2 :]], 0)
    row[...] = extra[1, :8]
    for s in range(CRITICS):
        blocks[s][...] = every[which[s]]


def add_last(which, early, late):
    count, z = early[0].shape[0], len(early)
    return pl.pallas_call(
        functools.partial(last_kernel, count, z),
        in_specs=[SCALAR] + [WHOLE] * (2 * z),
        out_specs=[WHOLE] * 7,
        out_shape=[jax.ShapeDtypeStruct((16, LANES), BF)] * CRITICS
        + [jax.ShapeDtypeStruct((SLOT, PADDED // 2), F32), jax.ShapeDtypeStruct((8, PADDED), F32)],
        scratch_shapes=[pltpu.VMEM((CRITICS, 16, LANES), BF)],
        compiler_params=params(),
        cost_estimate=cost(1e6, 2e6),
        name="add_last",
    )(which, *early, *late)


def adamw(weight, first, second, grad, rate, factors, outs):
    first_new = BETA_FIRST * first[...] + (1.0 - BETA_FIRST) * grad
    second_new = BETA_SECOND * second[...] + (1.0 - BETA_SECOND) * grad * grad
    old = weight[...]
    step = (first_new * factors[0]) / (jnp.sqrt(second_new * factors[1]) + EPSILON)
    outs[0][...] = old - rate * (step + WEIGHT_DECAY * old)
    outs[1][...] = first_new
    outs[2][...] = second_new


def actor_update_kernel(me, factors, own, peer, weight, first, second, w_out, m_out, v_out, small, grad):
    side = me[0] & 1
    grad[pl.ds(pl.multiple_of(side * HALF, 16), HALF)] = own[:HALF].astype(F32)
    grad[pl.ds(pl.multiple_of((1 - side) * HALF, 16), HALF)] = peer[:HALF].astype(F32)
    count = weight.shape[0]
    adamw(weight, first, second, grad[:count], RATE_MATRIX, factors, (w_out, m_out, v_out))
    pair = own[HALF:].astype(F32)
    small[...] = pair[:8, :PADDED] + pair[:8, PADDED:]


def actor_update(me, factors, own, peer, weight, first, second):
    shape = jax.ShapeDtypeStruct(weight.shape, F32)
    return pl.pallas_call(
        actor_update_kernel,
        in_specs=[SCALAR, SCALAR] + [WHOLE] * 5,
        out_specs=[WHOLE] * 4,
        out_shape=[shape, shape, shape, jax.ShapeDtypeStruct((8, PADDED), F32)],
        scratch_shapes=[pltpu.VMEM((2 * HALF, ACTOR_HIDDEN), F32)],
        compiler_params=params(),
        cost_estimate=cost(2e6, 5e6),
        name="actor_update",
    )(me, factors, own, peer, weight, first, second)


def update_kernel(samples, count, factors, *refs):
    blocks, refs = refs[:count], refs[count:]
    head_grad, row, small_sums = refs[:3]
    state, outs, grad = refs[3:21], refs[21:40], refs[40]
    total = jnp.concatenate([b[...].astype(F32) for b in blocks], 0)
    adamw(*state[0:3], total[:, HIDDEN_SIZE : HIDDEN_SIZE + INPUTS], RATE_MATRIX, factors, outs[1:4])
    adamw(*state[3:6], total[:, :HIDDEN_SIZE], RATE_MATRIX, factors, outs[4:7])
    edge = INPUTS - HIDDEN_SIZE + PADDED
    bias_grad = jnp.transpose(total[:, LANES - PADDED :])[edge : edge + 2]
    adamw(*state[6:9], bias_grad, RATE_VECTOR, factors, outs[7:10])
    adamw(*state[9:12], head_grad[...], RATE_MATRIX, factors, outs[10:13])
    for i in range(4):
        grad[:, i * PADDED : (i + 1) * PADDED] = small_sums[i : i + 1]
    wide = jnp.concatenate([jnp.broadcast_to(row[:1], (8, PADDED)), jnp.zeros((8, PADDED), F32)], 1)
    wide = pltpu.roll(wide, 2 * ACT_DIM, 1)[:1]
    wide = wide + jnp.concatenate([small_sums[4:5], jnp.zeros((1, PADDED), F32)], 1)
    grad[:, 4 * PADDED :] = wide
    adamw(*state[12:15], grad[:, :SMALL_VEC], RATE_VECTOR, factors, outs[13:16])
    heat = state[15][...]
    logp_sum = small_sums[6:7, :1]
    shortfall = (ACT_DIM * samples - logp_sum) / samples
    adamw(*state[15:18], shortfall, STEP_SIZE_SCALE, factors, outs[16:19])
    actor_loss = (jnp.exp(heat) * logp_sum - small_sums[5:6, :1] / MERGED_SUPPORTS) / samples
    outs[0][...] = row[1:2, :1] + actor_loss + heat * shortfall


def update(samples, factors, blocks, head_grad, row, small_sums, state):
    shapes = [jax.ShapeDtypeStruct((1, 1), F32)] + [jax.ShapeDtypeStruct(a.shape, F32) for a in state]
    count = len(blocks)
    return pl.pallas_call(
        functools.partial(update_kernel, samples, count),
        in_specs=[SCALAR] + [WHOLE] * (count + 3 + len(state)),
        out_specs=[WHOLE] * len(shapes),
        out_shape=shapes,
        scratch_shapes=[pltpu.VMEM((1, 6 * PADDED), F32)],
        compiler_params=params(),
        cost_estimate=cost(2e6, 6e6),
        name="update",
    )(factors, *blocks, head_grad, row, small_sums, *state)


def exchange(value, flip):
    count = lax.axis_size("rows") * lax.axis_size("quant")
    return lax.ppermute(value, AXES, [(i, i ^ flip) for i in range(count)])


def all_sum(value):
    total = lax.axis_size("rows") * lax.axis_size("quant")
    flip = 1
    while flip < total:
        value = value + exchange(value, flip)
        flip *= 2
    return value


def scatter_sum(pieces):
    total = pieces.shape[0]
    flip = total // 2
    while flip:
        low = pieces.astype(BF)
        pieces = low[:flip].astype(F32) + exchange(low[flip:], flip).astype(F32)
        flip //= 2
    return pieces[0]


def reduce_chunk(sent, kept):
    parts = add_core(kept, exchange(sent, 1))
    parts = add_square([parts[0]] + [exchange(parts[k], 2 * k) for k in (1, 2, 3)])
    return [parts[0]] + [exchange(parts[k], 8 * k) for k in range(1, len(parts))]


def local(
    obs, chosen, noise_now, next_obs, noise_next, payoffs, done, order,
    w_one, w_two, biases, head_part, t_one, t_two, t_biases, t_head_part, t_head_bias,
    actor, counter,
    in_w, in_m, in_v, mid_w, mid_m, mid_v, bias_w, bias_m, bias_v, head_w, head_m, head_v,
    actor_w, actor_m, actor_v, small_w, small_m, small_v, heat, heat_m, heat_v,
):
    n_rows, n_quant = lax.axis_size("rows"), lax.axis_size("quant")
    devices = n_rows * n_quant
    rows = obs.shape[0]
    samples = rows * devices
    index = lax.axis_index("quant").reshape(1)
    device = lax.axis_index("rows") * n_quant + lax.axis_index("quant")
    me = device.reshape(1)
    direct = devices * 16 == HIDDEN_SIZE
    small_row = small_w.reshape(1, -1)
    tally = counter.astype(F32)
    factors = jnp.concatenate(
        [1.0 / (1.0 - jnp.power(BETA_FIRST, tally)), 1.0 / (1.0 - jnp.power(BETA_SECOND, tally))]
    )

    own_head = jnp.concatenate([head_part.T, t_head_part.T], 1)
    got = [
        lax.ppermute(own_head, "quant", [(i, i ^ k) for i in range(n_quant)]) for k in (1, 2, 3)
    ]
    g_one, g_two, act, scaled, next_act, logp = actor_forward(
        index, obs.T, next_obs.T, noise_now.T, noise_next.T, actor, small_row
    )
    head, head_bias = heads(index, own_head, got, small_row, t_head_bias.reshape(1, -1))

    level = float(np.asarray(-1.0 / (MERGED_SUPPORTS * samples), ml_dtypes.bfloat16))
    own, send = pilot_pass(
        level, 1.0 / samples, me, heat, obs.T, act, scaled, logp, g_one, g_two, actor,
        w_one, w_two, biases, head, head_bias,
    )
    lagged, keep = target_pass(
        index, heat, next_obs.T, next_act, logp, payoffs.reshape(1, -1), done.reshape(1, -1), order,
        t_one, t_two, t_biases, head, head_bias,
    )
    flip = 1
    own = add_actor(own, exchange(send, 1))
    while flip < devices // 2:
        flip *= 2
        own = add_actor(own, exchange(own, flip))
    peer = exchange(own, 1)
    *actor_new, small_sums = actor_update(me, factors, own, peer, actor_w, actor_m, actor_v)

    scale = 1.0 / (samples * MERGED_SUPPORTS * KEPT_ATOMS)
    split = (n_rows, n_quant) if direct else (0, 0)
    shared = (obs.T, chosen.T, lagged, keep, w_one, w_two, biases, head, head_bias)
    place = me if direct else jnp.zeros_like(me)
    sent, kept, *before = critic_pass(0, 3, False, scale, split, place, *shared, ())
    sent_late, kept_late, *extra = critic_pass(3, 2, True, scale, split, place, *shared, before)
    if direct:
        early = reduce_chunk(sent, kept)
        late = reduce_chunk(sent_late, kept_late)
        inverse = pow(CRITICS, -1, devices)
        slots = jnp.arange(CRITICS)
        which = (CRITICS * (((device - slots) * inverse) % devices) + slots) // devices
        *pieces, head_grad, row = add_last(which, early, late)
        blocks = [
            lax.ppermute(piece, AXES, [((CRITICS * i + s) % devices, i) for i in range(devices)])
            for s, piece in enumerate(pieces)
        ]
    else:
        both = [jnp.concatenate(pair, 2) for pair in ((kept, kept_late), (sent, sent_late))]
        grads = jnp.stack(both)
        grads = grads.transpose(3, 2, 1, 0, 4, 5).reshape(devices, -1, LANES)
        order_of = device ^ jnp.arange(devices)
        blocks = [scatter_sum(jnp.take(grads, order_of, axis=0))]
        head_grad = extra[0].reshape(n_quant, PADDED // n_quant, n_rows, HIDDEN_SIZE // n_rows)
        head_grad = head_grad.transpose(2, 0, 1, 3).reshape((devices,) + (PADDED // n_quant, -1))
        head_grad = scatter_sum(jnp.take(head_grad, order_of, axis=0))
        row = all_sum(extra[1])
    state = (
        in_w.T, in_m.T, in_v.T, mid_w.T, mid_m.T, mid_v.T, bias_w, bias_m, bias_v,
        head_w.T, head_m.T, head_v.T, small_row, small_m.reshape(1, -1), small_v.reshape(1, -1),
        heat.reshape(1, 1), heat_m.reshape(1, 1), heat_v.reshape(1, 1),
    )
    objective, *new = update(samples, factors, blocks, head_grad, row, small_sums, state)
    return (
        objective.reshape(()),
        *(a.T for a in new[:6]),
        *new[6:9],
        *(a.T for a in new[9:12]),
        *actor_new,
        *(a.reshape(-1) for a in new[12:]),
    )


def solution(mesh):
    both, row, none = P(AXES), P("rows"), P()
    column_of, shard = P(None, "quant"), P(None, AXES)
    placed = (
        (both,) * 3 + (row,) * 5 + (none,) * 3 + (column_of,) + (none,) * 3 + (column_of,) + (none,) * 3
        + (shard,) * 9 + (P("rows", "quant"),) * 3 + (none,) * 9
    )
    return jax.shard_map(
        local,
        mesh=mesh,
        in_specs=placed,
        out_specs=(none,) + (shard,) * 9 + (P("rows", "quant"),) * 3 + (none,) * 9,
        check_vma=False,
    )
```

```python
import functools
import math

import jax
import jax.numpy as jnp
import ml_dtypes
import numpy as np
from jax import lax
from jax.experimental import pallas as pl
from jax.experimental.pallas import tpu as pltpu
from jax.sharding import PartitionSpec as P

OBS_DIM = 376
ACT_DIM = 17
HIDDEN_SIZE = 512
ACTOR_HIDDEN = 256
CRITICS = 5
QUANTS = 25
SLOT = 32
PADDED = 128
MERGED_SUPPORTS = 125
KEPT_ATOMS = 115
INPUTS = 393
FEATURES = 2560
SMALL_VEC = 674
LANES = 1024
EXTRA = 128
TILE = 512
MiB = 1024 * 1024

DISCOUNT = 0.99
BETA_FIRST = 0.9
BETA_SECOND = 0.999
EPSILON = 1e-08
WEIGHT_DECAY = 0.01
RATE_MATRIX = 0.05
RATE_VECTOR = 0.3
STEP_SIZE_SCALE = 0.5
LOG_TWO = math.log(2.0)
HALF_LOG_CIRCLE = 0.5 * math.log(2.0 * math.pi)
AXES = ("rows", "quant")
BF = jnp.bfloat16
F32 = jnp.float32
WHOLE = pl.BlockSpec(memory_space=pltpu.VMEM)
SCALAR = pl.BlockSpec(memory_space=pltpu.SMEM)
UNREAD = pl.BlockSpec(memory_space=pl.ANY)


def dot_nn(left, right):
    return jnp.dot(left, right, preferred_element_type=F32)


def dot_tn(left, right):
    return lax.dot_general(left, right, (((0,), (0,)), ((), ())), preferred_element_type=F32)


def dot_nt(left, right):
    return lax.dot_general(left, right, (((1,), (1,)), ((), ())), preferred_element_type=F32)


def params(limit=32, steps=0):
    semantics = ("arbitrary",) * steps if steps else None
    return pltpu.CompilerParams(vmem_limit_bytes=limit * MiB, dimension_semantics=semantics)


def cost(flops, moved):
    return pl.CostEstimate(flops=int(flops), bytes_accessed=int(moved), transcendentals=0)


def column(row):
    return jnp.transpose(jnp.broadcast_to(row, (8, row.shape[1])))[:, :1]


def fill_inputs(tall, inputs, obs, act):
    rows = obs.shape[1]
    body = OBS_DIM // 16 * 16
    inputs[:body] = obs[:body]
    tall[:8] = obs[body:OBS_DIM].astype(F32)
    tall[8 : 8 + ACT_DIM] = act.astype(F32)
    tall[8 + ACT_DIM : 32] = jnp.zeros((24 - ACT_DIM, rows), F32)
    tall[8 + ACT_DIM : 11 + ACT_DIM] = jnp.ones((3, rows), F32)
    inputs[body : body + 32] = tall[...].astype(BF)
    inputs[body + 32 :] = jnp.zeros((HIDDEN_SIZE - body - 32, rows), BF)


def actor_layers(inputs, draw, actor, small, out_scratch):
    s_one = column(small[:, :ACTOR_HIDDEN])
    s_two = column(small[:, ACTOR_HIDDEN : 2 * ACTOR_HIDDEN])
    s_three = column(small[:, 2 * ACTOR_HIDDEN : 2 * ACTOR_HIDDEN + PADDED])[: 2 * ACT_DIM]
    g_one = jnp.maximum(dot_tn(actor[:OBS_DIM], inputs) + s_one, 0.0).astype(BF)
    g_two = jnp.maximum(dot_tn(actor[OBS_DIM : OBS_DIM + ACTOR_HIDDEN], g_one) + s_two, 0.0).astype(BF)
    out_scratch[: 2 * ACT_DIM] = dot_nn(actor[OBS_DIM + ACTOR_HIDDEN :], g_two) + s_three
    mean = out_scratch[:ACT_DIM]
    log_std = out_scratch[ACT_DIM : 2 * ACT_DIM]
    scaled = jnp.exp(log_std) * draw
    pre = mean + scaled
    act = jnp.tanh(pre)
    soft = jnp.maximum(-2.0 * pre, 0.0) + jnp.log(1.0 + jnp.exp(-2.0 * jnp.abs(pre)))
    logp = jnp.sum(
        -0.5 * draw * draw - log_std - HALF_LOG_CIRCLE - 2.0 * (LOG_TWO - pre - soft),
        axis=0,
        keepdims=True,
    )
    return g_one, g_two, scaled, act, logp


def heads_kernel(me, own, got_one, got_two, got_three, small, lag_bias, out, bias_out, stage, col):
    quarter = own.shape[0]
    for k, got in enumerate((own, got_one, got_two, got_three)):
        first = pl.multiple_of((me[0] ^ k) * quarter, quarter)
        stage[pl.ds(first, quarter)] = got[...].astype(F32)
    keep = lax.broadcasted_iota(jnp.int32, (SLOT, 1), 0) < QUANTS
    bias = small[:, SMALL_VEC - PADDED :]
    both = jnp.concatenate([bias, lag_bias[...], jnp.zeros((6, PADDED), F32)], 0)
    col[:PADDED] = jnp.transpose(both)
    for e in range(CRITICS):
        rows = pl.ds(e * QUANTS, SLOT)
        out[e] = jnp.where(keep, stage[rows], 0.0).astype(BF)
        columns = jnp.where(keep, col[rows], 0.0)
        for net in range(2):
            bias_out[net, e] = jnp.broadcast_to(columns[:, net : net + 1], (SLOT, PADDED))


def heads(me, own, got, small, lag_bias):
    return pl.pallas_call(
        heads_kernel,
        in_specs=[SCALAR] + [WHOLE] * 6,
        out_specs=[WHOLE, WHOLE],
        out_shape=[
            jax.ShapeDtypeStruct((CRITICS, SLOT, 2 * HIDDEN_SIZE), BF),
            jax.ShapeDtypeStruct((2, CRITICS, SLOT, PADDED), F32),
        ],
        scratch_shapes=[pltpu.VMEM((136, 2 * HIDDEN_SIZE), F32), pltpu.VMEM((136, 8), F32)],
        compiler_params=params(),
        cost_estimate=cost(3e10, 1e6),
        name="heads",
    )(me, own, *got, small, lag_bias)


def fill_first(tall, filled, first, bias):
    body = INPUTS // 16 * 16
    high = bias.astype(BF).astype(F32)
    middle = (bias - high).astype(BF).astype(F32)
    filled[:body] = first[:body]
    tall[: INPUTS - body] = first[body:].astype(F32)
    tall[INPUTS - body : 32] = jnp.zeros((32 - INPUTS + body, HIDDEN_SIZE), F32)
    tall[INPUTS - body : INPUTS - body + 1] = high
    tall[INPUTS - body + 1 : INPUTS - body + 2] = middle
    tall[INPUTS - body + 2 : INPUTS - body + 3] = bias - high - middle
    filled[body : body + 32] = tall[...].astype(BF)
    filled[body + 32 :] = jnp.zeros((HIDDEN_SIZE - body - 32, HIDDEN_SIZE), BF)


def tiles(rows):
    width = min(rows, TILE)
    return [pl.ds(i * width, width) for i in range(rows // width)]


def target_kernel(
    index, heat, inputs, logp, payoffs, done, order_in, first, second, bias, head, head_bias, after,
    lagged, keep, filled, tall_w, packed, order, sems,
):
    rows = inputs.shape[1]
    mine = pl.ds(pl.multiple_of(index[0] * rows, PADDED), rows)
    copy = pltpu.make_async_copy(order_in.at[mine], order, sems.at[0])
    copy.start()
    for e in range(CRITICS):
        lanes = slice(e * HIDDEN_SIZE, (e + 1) * HIDDEN_SIZE)
        fill_first(tall_w, filled, first[:, lanes], bias[:1, lanes])
        b_two = column(bias[1:2, lanes])
        w_two = second[:, lanes]
        for part in tiles(rows):
            h_one = jnp.maximum(dot_tn(filled[...], inputs[:, part]), 0.0).astype(BF)
            h_two = jnp.maximum(dot_tn(w_two, h_one) + b_two, 0.0).astype(BF)
            value = dot_nn(head[e, :, HIDDEN_SIZE:], h_two) + head_bias[1, e, :, :1]
            packed[e * QUANTS : e * QUANTS + SLOT, part] = value
    copy.wait()
    for i in range(rows // PADDED):
        part = pl.ds(i * PADDED, PADDED)
        kept = (order[part] < KEPT_ATOMS).astype(F32)
        kept = jnp.concatenate([kept, jnp.zeros((PADDED, PADDED - MERGED_SUPPORTS), F32)], 1)
        keep[:, part] = jnp.transpose(kept).astype(BF)
    decay = DISCOUNT * (1.0 - done[:, mine].astype(F32))
    temperature = jnp.exp(jnp.full((1, 1), heat[0], F32))
    lagged[...] = payoffs[:, mine] + decay * (packed[:PADDED] - temperature * logp[...])


def target_pass(index, heat, inputs, logp, payoffs, done, order, first, second, bias, head, head_bias, after):
    rows = inputs.shape[1]
    return pl.pallas_call(
        target_kernel,
        in_specs=[SCALAR] * 2 + [WHOLE] * 4 + [pl.BlockSpec(memory_space=pltpu.HBM)] + [WHOLE] * 5 + [UNREAD],
        out_specs=[WHOLE] * 2,
        out_shape=[jax.ShapeDtypeStruct((PADDED, rows), F32), jax.ShapeDtypeStruct((PADDED, rows), BF)],
        scratch_shapes=[
            pltpu.VMEM((HIDDEN_SIZE, HIDDEN_SIZE), BF),
            pltpu.VMEM((32, HIDDEN_SIZE), F32),
            pltpu.VMEM((136, rows), F32),
            pltpu.VMEM((rows, MERGED_SUPPORTS), jnp.int32),
            pltpu.SemaphoreType.DMA((1,)),
        ],
        compiler_params=params(24),
        cost_estimate=cost(7e9, 7e6),
        name="target_pass",
    )(index, heat, inputs, logp, payoffs, done, order, first, second, bias, head, head_bias, after)


HALF = 336


def two_terms(value):
    high = value.astype(BF).astype(F32)
    both = jnp.concatenate([high, value - high], 1)
    return jnp.concatenate([both, jnp.zeros((8, 2 * PADDED), F32)], 0).astype(BF)


def pilot_kernel(
    level, share, me, index, heat, obs, next_in, noise, noise_next_in, chosen, actor, small,
    first, second, bias, head, head_bias,
    own_out, send_out, x_now, x_target, logp_next,
    inputs, filled, tall_x, tall_w, dact, total, out_scratch, grad_out, small_out, next_obs, noise_next, sems,
):
    rows = obs.shape[1]
    mine = pl.ds(pl.multiple_of(index[0] * rows, PADDED), rows)
    copies = [
        pltpu.make_async_copy(next_in.at[:, mine], next_obs, sems.at[0]),
        pltpu.make_async_copy(noise_next_in.at[:, mine], noise_next, sems.at[1]),
    ]
    for copy in copies:
        copy.start()
    g_one, g_two, scaled, act, logp = actor_layers(obs[...], noise[...], actor, small, out_scratch)
    fill_inputs(tall_x, inputs, obs, act.astype(BF))
    fill_inputs(tall_x, x_now, obs, chosen[...])
    for copy in copies:
        copy.wait()
    _, _, _, next_act, next_logp = actor_layers(next_obs[...], noise_next[...], actor, small, out_scratch)
    fill_inputs(tall_x, x_target, next_obs, next_act.astype(BF))
    logp_next[...] = next_logp

    dact[...] = jnp.zeros(dact.shape, F32)
    total[...] = jnp.zeros(total.shape, F32)
    tail = jnp.zeros((SLOT, 1), F32)
    for e in range(CRITICS):
        lanes = slice(e * HIDDEN_SIZE, (e + 1) * HIDDEN_SIZE)
        fill_first(tall_w, filled, first[:, lanes], bias[:1, lanes])
        b_two = column(bias[1:2, lanes])
        head_sum = jnp.sum(head[e, :, :HIDDEN_SIZE].astype(F32), axis=0, keepdims=True)
        weight = column(head_sum)
        push = column(head_sum * level)
        tail = tail + head_bias[0, e, :, :1]
        w_two = second[:, lanes]
        for part in tiles(rows):
            h_one = jnp.maximum(dot_tn(filled[...], inputs[:, part]), 0.0).astype(BF)
            h_two = jnp.maximum(dot_tn(w_two, h_one) + b_two, 0.0)
            weighted = h_two * weight
            total[:, part] += jnp.sum(weighted.reshape(-1, 8, weighted.shape[1]), axis=0)
            dz_two = jnp.where(h_two > 0, push, 0.0).astype(BF)
            grad = dot_nn(w_two, dz_two)
            dz_one = jnp.where(h_one > 0, grad, 0.0).astype(BF)
            dact[:, part] += dot_nn(first[OBS_DIM // 16 * 16 :, lanes], dz_one)

    temperature_share = jnp.exp(jnp.full((1, 1), heat[0], F32)) * share
    skip = OBS_DIM % 16
    action_grad = dact[skip : skip + ACT_DIM]
    pre = action_grad * (1.0 - act * act) + 2.0 * temperature_share * act
    out_scratch[:ACT_DIM] = pre
    out_scratch[ACT_DIM : 2 * ACT_DIM] = pre * scaled - temperature_share
    dout = out_scratch[: 2 * ACT_DIM].astype(BF)
    a_two = actor[OBS_DIM : OBS_DIM + ACTOR_HIDDEN]
    a_three = actor[OBS_DIM + ACTOR_HIDDEN :]
    dz_two = jnp.where(g_two > 0, dot_tn(a_three, dout), 0.0).astype(BF)
    dz_one = jnp.where(g_one > 0, dot_nn(a_two, dz_two), 0.0).astype(BF)
    grad_out[OBS_DIM + ACTOR_HIDDEN : OBS_DIM + ACTOR_HIDDEN + 2 * ACT_DIM] = dot_nt(dout, g_two)
    grad_out[OBS_DIM + ACTOR_HIDDEN + 2 * ACT_DIM :] = jnp.zeros((6, ACTOR_HIDDEN), F32)
    grad_out[OBS_DIM : OBS_DIM + ACTOR_HIDDEN] = dot_nt(g_one, dz_two)
    grad_out[:OBS_DIM] = dot_nt(obs[...], dz_one)
    ones = jnp.ones((16, rows), BF)
    small_out[...] = jnp.zeros(small_out.shape, F32)
    sum_one = dot_nt(ones, dz_one)[:1]
    sum_two = dot_nt(ones, dz_two)[:1]
    small_out[0:1] = sum_one[:, :PADDED]
    small_out[1:2] = sum_one[:, PADDED:]
    small_out[2:3] = sum_two[:, :PADDED]
    small_out[3:4] = sum_two[:, PADDED:]
    small_out[4:5, : 2 * ACT_DIM] = dot_nt(ones, dout)[:1]
    pilot_total = jnp.sum(total[...]) + rows * jnp.sum(tail)
    small_out[5:6] = jnp.broadcast_to(pilot_total, (1, PADDED))
    small_out[6:7] = jnp.broadcast_to(jnp.sum(logp), (1, PADDED))
    packed = two_terms(small_out[...])
    side = me[0] & 1
    for out, which in ((own_out, side), (send_out, 1 - side)):
        out[:HALF] = grad_out[pl.ds(pl.multiple_of(which * HALF, 16), HALF)].astype(BF)
        out[HALF:] = packed


def pilot_pass(
    level, share, me, index, heat, obs, next_obs, noise, noise_next, chosen, actor, small,
    first, second, bias, head, head_bias,
):
    rows = obs.shape[1]
    far = pl.BlockSpec(memory_space=pltpu.HBM)
    filled = jax.ShapeDtypeStruct((HIDDEN_SIZE, rows), BF)
    return pl.pallas_call(
        functools.partial(pilot_kernel, level, share),
        in_specs=[SCALAR] * 3 + [WHOLE, far, WHOLE, far] + [WHOLE] * 8,
        out_specs=[WHOLE] * 5,
        out_shape=[jax.ShapeDtypeStruct((HALF + 16, ACTOR_HIDDEN), BF)] * 2
        + [filled, filled, jax.ShapeDtypeStruct((1, rows), F32)],
        scratch_shapes=[
            pltpu.VMEM((HIDDEN_SIZE, rows), BF),
            pltpu.VMEM((HIDDEN_SIZE, HIDDEN_SIZE), BF),
            pltpu.VMEM((32, rows), F32),
            pltpu.VMEM((32, HIDDEN_SIZE), F32),
            pltpu.VMEM((INPUTS - OBS_DIM // 16 * 16, rows), F32),
            pltpu.VMEM((8, rows), F32),
            pltpu.VMEM((40, rows), F32),
            pltpu.VMEM((2 * HALF, ACTOR_HIDDEN), F32),
            pltpu.VMEM((8, PADDED), F32),
            pltpu.VMEM((OBS_DIM, rows), BF),
            pltpu.VMEM((ACT_DIM, rows), F32),
            pltpu.SemaphoreType.DMA((2,)),
        ],
        compiler_params=params(24),
        cost_estimate=cost(14e9, 9e6),
        name="pilot_pass",
    )(me, index, heat, obs, next_obs, noise, noise_next, chosen, actor, small, first, second, bias, head, head_bias)


def pair_terms(q_ref, lagged, keep, parts, rows):
    def group(i, carry):
        part = pl.ds(pl.multiple_of(i * PADDED, PADDED), PADDED)
        q = q_ref[:, part]
        shift = jnp.sum(q, axis=0, keepdims=True) * (1.0 / QUANTS)
        y = (lagged[:, part] - shift).astype(BF).reshape(8, 16, PADDED)
        upper = keep[:, part].reshape(8, 16, PADDED)
        lower = -upper
        q_ref[:, part] = q - shift
        for j in range(QUANTS):
            level = jnp.broadcast_to(q_ref[j : j + 1, part], (16, PADDED)).astype(BF)
            d = y - level[None]
            c = jnp.minimum(jnp.maximum(d, lower), upper)
            half = c * jnp.asarray(0.5, BF)
            g = half + jnp.abs(c) * jnp.asarray((j + 0.5) / QUANTS - 0.5, BF)
            h = g * (d - half)
            g = g[:4] + g[4:]
            g = g[:2] + g[2:]
            parts[j * 16 : j * 16 + 16, part] = g[0] + g[1]
            h = h[:4] + h[4:]
            h = h[:2] + h[2:]
            parts[(QUANTS + j) * 16 : (QUANTS + j) * 16 + 16, part] = h[0] + h[1]
        return carry

    lax.fori_loop(0, rows // PADDED, group, 0)
    shape = (48, 2 * QUANTS * 16)
    row = lax.broadcasted_iota(jnp.int32, shape, 0)
    owner = jnp.minimum(lax.broadcasted_iota(jnp.int32, shape, 1) // 16, SLOT)
    owner = jnp.where(owner >= QUANTS, SLOT, owner)
    return dot_nn((row == owner).astype(F32).astype(BF), parts[...])


PARITY = 18


def granules(e):
    mine = range(32 * e, 32 * e + 32)
    return [[g for g in mine if g // CRITICS % 2 == parity] for parity in range(2)]


def granule_places(chunk):
    places = np.zeros(CRITICS * 32, np.int32)
    for i, e in enumerate(chunk):
        for way in granules(e):
            for t, g in enumerate(way):
                places[g] = i * PARITY + t
    return places


SENT = (6, 6, 6, 4)


def store_piece(outs, t, value):
    for out in outs:
        if t < out.shape[0]:
            out[t] = value
            return
        t -= out.shape[0]


def critic_kernel(
    e, waits, rows_scale, split, me, inputs, lagged, keep, first, second, bias, head, head_bias, *refs,
):
    last = e == CRITICS - 1
    refs = refs[waits:]
    if e:
        before, refs = refs[:3], refs[3:]
    outs, scratch = refs[:-9], refs[-9:]
    filled, tall_w, h_one, h_two, q, parts, grads, packed, extra = scratch
    rows = inputs.shape[1]
    lanes = slice(e * HIDDEN_SIZE, (e + 1) * HIDDEN_SIZE)
    second = second.at[:, lanes]
    head = head.at[e : e + 1, :, :HIDDEN_SIZE]
    head_bias = head_bias.at[:1, e : e + 1]
    fill_first(tall_w, filled, first[:, lanes], bias[:1, lanes])
    b_two = column(bias[1:2, lanes])
    for part in tiles(rows):
        one = jnp.maximum(dot_tn(filled[...], inputs[:, part]), 0.0).astype(BF)
        h_one[:, part] = one
        two = jnp.maximum(dot_tn(second[...], one) + b_two, 0.0).astype(BF)
        h_two[:, part] = two
        q[:, part] = dot_nn(head[0], two) + head_bias[0, 0, :, :1]
    terms = pair_terms(q, lagged, keep, parts, rows)
    low = (terms[:SLOT] * -rows_scale).astype(BF)
    loss = terms[SLOT : SLOT + 1]
    head_grad = dot_nt(low, h_two[...])
    count = jnp.ones((8, rows), BF)
    bias_grad = dot_nt(count, low)[:1]
    sums = jnp.zeros((HIDDEN_SIZE, PADDED), F32)
    for part in tiles(rows):
        two = h_two[:, part]
        dz_two = jnp.where(two > 0, dot_tn(head[0], low[:, part.start : part.start + part.size]), 0.0)
        for i in range(part.size // PADDED):
            sums = sums + dz_two[:, i * PADDED : (i + 1) * PADDED]
        dz_two = dz_two.astype(BF)
        h_two[:, part] = dz_two
        one = h_one[:, part]
        h_one[:, part] = jnp.where(one > 0, dot_nn(second[...], dz_two), 0.0).astype(BF)
        second_part = dot_nt(dz_two, one)
        second_grad = second_grad + second_part if part.start else second_part
    grads[:, :, :HIDDEN_SIZE] = second_grad.astype(BF).reshape(-1, 16, HIDDEN_SIZE)
    first_grad = dot_nt(h_one[...], inputs[...])
    grads[:, :, HIDDEN_SIZE : LANES - PADDED] = (
        first_grad[:, : HIDDEN_SIZE - PADDED].astype(BF).reshape(-1, 16, HIDDEN_SIZE - PADDED)
    )
    lane = lax.broadcasted_iota(jnp.int32, (HIDDEN_SIZE, PADDED), 1)
    tail = jnp.where(
        lane == INPUTS + 1 - HIDDEN_SIZE + PADDED,
        jnp.sum(sums, axis=1, keepdims=True),
        first_grad[:, HIDDEN_SIZE - PADDED :],
    )
    grads[:, :, LANES - PADDED : LANES] = tail.astype(BF).reshape(-1, 16, PADDED)
    direct = split[0] > 0
    rest = outs[1 + (len(SENT) if last else 1) :] if direct else outs[1:]
    if not last:
        all_heads, all_bias, all_loss = rest
        if e:
            all_heads[...] = before[0][...]
            all_bias[...] = before[1][...]
            all_loss[...] = before[2][...] + loss
        else:
            all_heads[...] = jnp.zeros(all_heads.shape, F32)
            all_bias[...] = jnp.zeros(all_bias.shape, F32)
            all_loss[...] = loss
        all_heads[e * SLOT : (e + 1) * SLOT] = head_grad
        all_bias[e : e + 1, :SLOT] = bias_grad
    else:
        n_rows, n_quant = split
        for i in range(CRITICS):
            packed[i * QUANTS : i * QUANTS + SLOT] = (
                before[0][i * SLOT : (i + 1) * SLOT] if i < e else head_grad
            )
        bias_row = jnp.zeros((1, PADDED), F32)
        lane = lax.broadcasted_iota(jnp.int32, (1, PADDED), 1)
        spare = jnp.zeros((1, PADDED - SLOT), F32)
        for i in range(CRITICS):
            piece = before[1][i : i + 1] if i < e else jnp.concatenate([bias_grad, spare], 1)
            piece = pltpu.roll(jnp.broadcast_to(piece, (8, PADDED)), i * QUANTS, 1)[:1]
            inside = (lane >= i * QUANTS) & (lane < (i + 1) * QUANTS)
            bias_row = jnp.where(inside, piece, bias_row)
        value = jnp.sum(before[2][...] + loss, axis=1, keepdims=True) * rows_scale
        value = jnp.broadcast_to(value, (1, PADDED))
        if direct:
            width = HIDDEN_SIZE // n_rows
            high = PADDED // n_quant
            lane = lax.broadcasted_iota(jnp.int32, (16, PADDED), 1)
            halves = [bias_row, pltpu.roll(jnp.broadcast_to(bias_row, (8, PADDED)), 64, 1)[:1], value]
            common = jnp.concatenate(halves + [jnp.zeros((13, PADDED), F32)], 0)
            for j in range(8):
                y, c = j // 4, j % 4
                for z in range(n_rows // 2):
                    r = 2 * z + y
                    block = packed[c * high : (c + 1) * high, r // 2 * PADDED : (r // 2 + 1) * PADDED]
                    if r % 2 == 0:
                        block = pltpu.roll(block, width, 1)
                    base = 2 * z * PADDED
                    extra[j, :, base : base + PADDED] = jnp.where(lane < 64, common, block[:16]).astype(BF)
                    extra[j, :, base + PADDED : base + 2 * PADDED] = block[16:].astype(BF)
        else:
            rest[0][...] = packed[:PADDED]
            rest[1][...] = jnp.concatenate([bias_row, value, jnp.zeros((6, PADDED), F32)], 0)
    if not direct:
        outs[0][...] = grads[...]
        return
    sent, kept = outs[: len(SENT) if last else 1], outs[len(SENT) if last else 1]
    side = me[0] & 1
    ways = granules(e)
    for t in range(max(map(len, ways))):
        pair = [way[min(t, len(way) - 1)] - e * 32 for way in ways]
        kept[t] = grads[jnp.where(side == 0, pair[0], pair[1])]
        store_piece(sent, t, grads[jnp.where(side == 0, pair[1], pair[0])])
    if last:
        for i in range(4):
            kept[PARITY + i] = extra[2 * i + side]
            store_piece(sent, PARITY + i, extra[2 * i + 1 - side])


def critic_pass(e, rows_scale, split, me, inputs, lagged, keep, first, second, bias, head, head_bias, after, before):
    rows = inputs.shape[1]
    last = e == CRITICS - 1
    if split[0]:
        block = lambda count: jax.ShapeDtypeStruct((count, 16, LANES), BF)
        sent = SENT if last else (PARITY,)
        out_shape = [block(count) for count in sent] + [block(sum(sent))]
    else:
        out_shape = [jax.ShapeDtypeStruct((HIDDEN_SIZE // 16, 16, LANES), BF)]
    if not last:
        out_shape += [
            jax.ShapeDtypeStruct((CRITICS * SLOT, HIDDEN_SIZE), F32),
            jax.ShapeDtypeStruct((8, PADDED), F32),
            jax.ShapeDtypeStruct((1, rows), F32),
        ]
    elif not split[0]:
        out_shape += [
            jax.ShapeDtypeStruct((PADDED, HIDDEN_SIZE), F32),
            jax.ShapeDtypeStruct((8, PADDED), F32),
        ]
    return pl.pallas_call(
        functools.partial(critic_kernel, e, len(after), rows_scale, split),
        in_specs=[SCALAR] + [WHOLE] * 8 + [UNREAD] * len(after) + [WHOLE] * len(before),
        out_specs=[WHOLE] * len(out_shape),
        out_shape=out_shape,
        scratch_shapes=[
            pltpu.VMEM((HIDDEN_SIZE, HIDDEN_SIZE), BF),
            pltpu.VMEM((32, HIDDEN_SIZE), F32),
            pltpu.VMEM((HIDDEN_SIZE, rows), BF),
            pltpu.VMEM((HIDDEN_SIZE, rows), BF),
            pltpu.VMEM((SLOT, rows), F32),
            pltpu.VMEM((2 * QUANTS * 16, rows), BF),
            pltpu.VMEM((HIDDEN_SIZE // 16, 16, LANES), BF),
            pltpu.VMEM((136, HIDDEN_SIZE), F32),
            pltpu.VMEM((8, 16, LANES), BF),
        ],
        compiler_params=params(24),
        cost_estimate=cost(7e9, 4e6),
        name="critic_pass",
    )(me, inputs, lagged, keep, first, second, bias, head, head_bias, *after, *before)


def add_kernel(a, b, out):
    out[:HALF] = (a[:HALF].astype(F32) + b[:HALF].astype(F32)).astype(BF)
    pair = [r[HALF:].astype(F32) for r in (a, b)]
    pair = [p[:8, :PADDED] + p[:8, PADDED:] for p in pair]
    out[HALF:] = two_terms(pair[0] + pair[1])


def add_actor(a, b):
    return pl.pallas_call(
        add_kernel,
        in_specs=[WHOLE, WHOLE],
        out_specs=WHOLE,
        out_shape=jax.ShapeDtypeStruct(a.shape, BF),
        compiler_params=params(),
        cost_estimate=cost(1e5, 6e5),
        name="add_actor",
    )(a, b)


def core_kernel(chunk, depth, waits, me, places, *refs):
    count = len(chunk)
    refs = refs[waits:]
    kept, got, outs, sums = refs[:count], refs[count:-5], refs[-5:-1], refs[-1]
    size = count * PARITY
    first = 0
    for piece in got:
        i, inside = min(first // PARITY, count - 1), first - min(first // PARITY, count - 1) * PARITY
        own = kept[i][inside : inside + piece.shape[0]]
        sums[first : first + piece.shape[0]] = (own.astype(F32) + piece[...].astype(F32)).astype(BF)
        first += piece.shape[0]
    z_first = chunk[-1] // 3 * depth
    for k in range(4):
        j = (me[0] & 7) ^ (2 * k)
        for z in range(depth):
            owner = (z_first + z) * 8 + j
            for i in range(CRITICS):
                outs[k][z * CRITICS + i] = sums[places[owner * CRITICS + i]]
        if chunk[-1] == CRITICS - 1:
            outs[k][depth * CRITICS] = sums[size + j // 2]


def add_core(chunk, depth, me, kept, got, after=()):
    tail = kept[-1].shape[0] - PARITY
    count = depth * CRITICS + (1 if tail else 0)
    return pl.pallas_call(
        functools.partial(core_kernel, chunk, depth, len(after)),
        in_specs=[SCALAR, SCALAR] + [UNREAD] * len(after) + [WHOLE] * (len(kept) + len(got)),
        out_specs=[WHOLE] * 4,
        out_shape=[jax.ShapeDtypeStruct((count, 16, LANES), BF)] * 4,
        scratch_shapes=[pltpu.VMEM((len(kept) * PARITY + tail, 16, LANES), BF)],
        compiler_params=params(),
        cost_estimate=cost(1e6, 8e6),
        name="add_core",
    )(me, jnp.asarray(granule_places(chunk)), *after, *kept, *got)


def tree(values):
    while len(values) > 1:
        values = [a + b for a, b in zip(values[::2], values[1::2])]
    return values[0]


def square_kernel(*refs):
    refs[4][...] = tree([r[...].astype(F32) for r in refs[:4]]).astype(BF)


def add_square(parts):
    return pl.pallas_call(
        square_kernel,
        in_specs=[WHOLE] * 4,
        out_specs=WHOLE,
        out_shape=jax.ShapeDtypeStruct(parts[0].shape, BF),
        compiler_params=params(),
        cost_estimate=cost(1e6, 10 * parts[0].size),
        name="add_square",
    )(*parts)


def line_kernel(me, early, *refs):
    late, outs, sums = refs[:4], refs[4:-1], refs[-1]
    count = early.shape[0]
    sums[:count] = early[...]
    total = tree([r[...].astype(F32) for r in late])
    sums[count:] = total[:count].astype(BF)
    extra = total[count]
    lane = lax.broadcasted_iota(jnp.int32, (16, PADDED), 1)
    for z in range(len(outs)):
        first = extra[:, 2 * z * PADDED : (2 * z + 1) * PADDED]
        second = extra[:, (2 * z + 1) * PADDED : (2 * z + 2) * PADDED]
        for i, value in enumerate((first, second, pltpu.roll(first, 64, 1))):
            old = sums[z * CRITICS + i, :, LANES - PADDED :].astype(F32)
            sums[z * CRITICS + i, :, LANES - PADDED :] = jnp.where(lane < 64, old, value).astype(BF)
    for k, out in enumerate(outs):
        first = ((me[0] // 8) ^ k) * CRITICS
        for i in range(CRITICS):
            out[i] = sums[first + i]


def add_line(me, early, late, depth):
    return pl.pallas_call(
        line_kernel,
        in_specs=[SCALAR] + [WHOLE] * 5,
        out_specs=[WHOLE] * depth,
        out_shape=[jax.ShapeDtypeStruct((CRITICS, 16, LANES), BF)] * depth,
        scratch_shapes=[pltpu.VMEM((2 * early.shape[0], 16, LANES), BF)],
        compiler_params=params(),
        cost_estimate=cost(1e6, 6e6),
        name="add_line",
    )(me, early, *late)


def adamw(weight, first, second, grad, rate, factors, outs):
    first_new = BETA_FIRST * first[...] + (1.0 - BETA_FIRST) * grad
    second_new = BETA_SECOND * second[...] + (1.0 - BETA_SECOND) * grad * grad
    old = weight[...]
    step = (first_new * factors[0]) / (jnp.sqrt(second_new * factors[1]) + EPSILON)
    outs[0][...] = old - rate * (step + WEIGHT_DECAY * old)
    outs[1][...] = first_new
    outs[2][...] = second_new


def actor_update_kernel(me, factors, own, peer, weight, first, second, w_out, m_out, v_out, small, grad):
    side = me[0] & 1
    grad[pl.ds(pl.multiple_of(side * HALF, 16), HALF)] = own[:HALF].astype(F32)
    grad[pl.ds(pl.multiple_of((1 - side) * HALF, 16), HALF)] = peer[:HALF].astype(F32)
    count = weight.shape[0]
    adamw(weight, first, second, grad[:count], RATE_MATRIX, factors, (w_out, m_out, v_out))
    pair = own[HALF:].astype(F32)
    small[...] = pair[:8, :PADDED] + pair[:8, PADDED:]


def actor_update(me, factors, own, peer, weight, first, second):
    shape = jax.ShapeDtypeStruct(weight.shape, F32)
    return pl.pallas_call(
        actor_update_kernel,
        in_specs=[SCALAR, SCALAR] + [WHOLE] * 5,
        out_specs=[WHOLE] * 4,
        out_shape=[shape, shape, shape, jax.ShapeDtypeStruct((8, PADDED), F32)],
        scratch_shapes=[pltpu.VMEM((2 * HALF, ACTOR_HIDDEN), F32)],
        compiler_params=params(),
        cost_estimate=cost(2e6, 5e6),
        name="actor_update",
    )(me, factors, own, peer, weight, first, second)


def update_kernel(samples, count, direct, factors, *refs):
    blocks, refs = refs[:count], refs[count:]
    if direct:
        small_sums, refs = refs[0], refs[1:]
        total = tree([b[...].astype(F32) for b in blocks]).reshape(-1, LANES)
        corner = pltpu.roll(total[:48, LANES - PADDED :], 64, 1)[:, :64]
        head_grad = corner[:SLOT]
        row = jnp.concatenate([corner[SLOT : SLOT + 1], corner[SLOT + 1 : SLOT + 2]], 1)
        critic_loss = corner[SLOT + 2 : SLOT + 3, :1]
    else:
        total = blocks[0][...]
        small_sums, refs = refs[2], (refs[0], refs[1]) + refs[3:]
        head_grad, row, critic_loss = refs[0][...], refs[1][:1], refs[1][1:2, :1]
        refs = refs[2:]
    state, outs, grad = refs[:18], refs[18:37], refs[37]
    adamw(*state[0:3], total[:, HIDDEN_SIZE : HIDDEN_SIZE + INPUTS], RATE_MATRIX, factors, outs[1:4])
    adamw(*state[3:6], total[:, :HIDDEN_SIZE], RATE_MATRIX, factors, outs[4:7])
    edge = INPUTS - HIDDEN_SIZE + PADDED
    bias_grad = jnp.transpose(total[:, LANES - PADDED :])[edge : edge + 2]
    adamw(*state[6:9], bias_grad, RATE_VECTOR, factors, outs[7:10])
    adamw(*state[9:12], head_grad, RATE_MATRIX, factors, outs[10:13])
    for i in range(4):
        grad[:, i * PADDED : (i + 1) * PADDED] = small_sums[i : i + 1]
    wide = jnp.concatenate([jnp.broadcast_to(row, (8, PADDED)), jnp.zeros((8, PADDED), F32)], 1)
    wide = pltpu.roll(wide, 2 * ACT_DIM, 1)[:1]
    wide = wide + jnp.concatenate([small_sums[4:5], jnp.zeros((1, PADDED), F32)], 1)
    grad[:, 4 * PADDED :] = wide
    adamw(*state[12:15], grad[:, :SMALL_VEC], RATE_VECTOR, factors, outs[13:16])
    heat = state[15][...]
    logp_sum = small_sums[6:7, :1]
    shortfall = (ACT_DIM * samples - logp_sum) / samples
    adamw(*state[15:18], shortfall, STEP_SIZE_SCALE, factors, outs[16:19])
    actor_loss = (jnp.exp(heat) * logp_sum - small_sums[5:6, :1] / MERGED_SUPPORTS) / samples
    outs[0][...] = critic_loss + actor_loss + heat * shortfall


def update(samples, factors, blocks, others, state):
    shapes = [jax.ShapeDtypeStruct((1, 1), F32)] + [jax.ShapeDtypeStruct(a.shape, F32) for a in state]
    count = len(blocks)
    return pl.pallas_call(
        functools.partial(update_kernel, samples, count, len(others) == 1),
        in_specs=[SCALAR] + [WHOLE] * (count + len(others) + len(state)),
        out_specs=[WHOLE] * len(shapes),
        out_shape=shapes,
        scratch_shapes=[pltpu.VMEM((1, 6 * PADDED), F32)],
        compiler_params=params(),
        cost_estimate=cost(2e6, 6e6),
        name="update",
    )(factors, *blocks, *others, *state)


def exchange(value, flip):
    count = lax.axis_size("rows") * lax.axis_size("quant")
    return lax.ppermute(value, AXES, [(i, i ^ flip) for i in range(count)])


def all_sum(value):
    total = lax.axis_size("rows") * lax.axis_size("quant")
    flip = 1
    while flip < total:
        value = value + exchange(value, flip)
        flip *= 2
    return value


def scatter_sum(pieces):
    total = pieces.shape[0]
    flip = total // 2
    while flip:
        low = pieces.astype(BF)
        pieces = low[:flip].astype(F32) + exchange(low[flip:], flip).astype(F32)
        flip //= 2
    return pieces[0]


def local(
    obs, chosen, noise_now, next_obs, noise_next, payoffs, done, order,
    w_one, w_two, biases, head_part, t_one, t_two, t_biases, t_head_part, t_head_bias,
    actor, counter,
    in_w, in_m, in_v, mid_w, mid_m, mid_v, bias_w, bias_m, bias_v, head_w, head_m, head_v,
    actor_w, actor_m, actor_v, small_w, small_m, small_v, heat, heat_m, heat_v,
):
    n_rows, n_quant = lax.axis_size("rows"), lax.axis_size("quant")
    devices = n_rows * n_quant
    rows = obs.shape[0]
    samples = rows * devices
    index = lax.axis_index("quant").reshape(1)
    device = lax.axis_index("rows") * n_quant + lax.axis_index("quant")
    me = device.reshape(1)
    direct = n_rows == 8 and n_quant == 4
    small_row = small_w.reshape(1, -1)
    tally = counter.astype(F32)
    factors = jnp.concatenate(
        [1.0 / (1.0 - jnp.power(BETA_FIRST, tally)), 1.0 / (1.0 - jnp.power(BETA_SECOND, tally))]
    )

    own_head = jnp.concatenate([head_part.T, t_head_part.T], 1)
    got = [
        lax.ppermute(own_head, "quant", [(i, i ^ k) for i in range(n_quant)]) for k in (1, 2, 3)
    ]
    head, head_bias = heads(index, own_head, got, small_row, t_head_bias.reshape(1, -1))

    level = float(np.asarray(-1.0 / (MERGED_SUPPORTS * samples), ml_dtypes.bfloat16))
    own, send, x_now, x_target, logp = pilot_pass(
        level, 1.0 / samples, me, index, heat, obs.T, next_obs.T, noise_now.T, noise_next.T, chosen.T,
        actor, small_row, w_one, w_two, biases, head, head_bias,
    )
    lagged, keep = target_pass(
        index, heat, x_target, logp, payoffs.reshape(1, -1), done.reshape(1, -1), order,
        t_one, t_two, t_biases, head, head_bias, own,
    )
    own = add_actor(own, exchange(send, 1))
    flips = [1 << i for i in range(1, devices.bit_length() - 1)]
    scale = 1.0 / (samples * MERGED_SUPPORTS * KEPT_ATOMS)
    split = (n_rows, n_quant) if direct else (0, 0)
    kept, got, before, early = [], [], (), None
    for e in range(CRITICS):
        after = [own]
        if direct and e == CRITICS - 1:
            early = add_core((0, 1, 2), 2, me, kept[:3], got[:3])
            early = [early[0]] + [exchange(early[k], 2 * k) for k in (1, 2, 3)]
            after.append(early[0])
        outs = critic_pass(
            e, scale, split, me, x_now, lagged, keep, w_one, w_two, biases, head, head_bias, after, before
        )
        if direct:
            count = len(SENT) if e == CRITICS - 1 else 1
            got.extend(exchange(piece, 1) for piece in outs[:count])
            outs = outs[count:]
        kept.append(outs[0])
        before = outs[1:]
        for flip in flips[e : e + 1] if e < CRITICS - 1 else flips[e:]:
            own = add_actor(own, exchange(own, flip))
    peer = exchange(own, 1)
    *actor_new, small_sums = actor_update(me, factors, own, peer, actor_w, actor_m, actor_v)

    if direct:
        early = add_square(early)
        late = add_core((2, 3, 4), 2, me, kept[2:], got[2:], (early,))
        late = [late[0]] + [exchange(late[k], 2 * k) for k in (1, 2, 3)]
        blocks = add_line(me, early, late, n_rows // 2)
        blocks = [blocks[0]] + [exchange(blocks[k], 8 * k) for k in range(1, len(blocks))]
        others = [small_sums]
    else:
        grads = jnp.stack(kept).reshape(devices, -1, LANES)
        order_of = device ^ jnp.arange(devices)
        blocks = [scatter_sum(jnp.take(grads, order_of, axis=0))]
        head_grad = before[0].reshape(n_quant, PADDED // n_quant, n_rows, HIDDEN_SIZE // n_rows)
        head_grad = head_grad.transpose(2, 0, 1, 3).reshape((devices,) + (PADDED // n_quant, -1))
        head_grad = scatter_sum(jnp.take(head_grad, order_of, axis=0))
        others = [head_grad, all_sum(before[1]), small_sums]
    state = (
        in_w.T, in_m.T, in_v.T, mid_w.T, mid_m.T, mid_v.T, bias_w, bias_m, bias_v,
        head_w.T, head_m.T, head_v.T, small_row, small_m.reshape(1, -1), small_v.reshape(1, -1),
        heat.reshape(1, 1), heat_m.reshape(1, 1), heat_v.reshape(1, 1),
    )
    objective, *new = update(samples, factors, blocks, others, state)
    return (
        objective.reshape(()),
        *(a.T for a in new[:6]),
        *new[6:9],
        *(a.T for a in new[9:12]),
        *actor_new,
        *(a.reshape(-1) for a in new[12:]),
    )


def solution(mesh):
    both, row, none = P(AXES), P("rows"), P()
    column_of, shard = P(None, "quant"), P(None, AXES)
    placed = (
        (both,) * 3 + (row,) * 5 + (none,) * 3 + (column_of,) + (none,) * 3 + (column_of,) + (none,) * 3
        + (shard,) * 9 + (P("rows", "quant"),) * 3 + (none,) * 9
    )
    return jax.shard_map(
        local,
        mesh=mesh,
        in_specs=placed,
        out_specs=(none,) + (shard,) * 9 + (P("rows", "quant"),) * 3 + (none,) * 9,
        check_vma=False,
    )
```

```python
import functools
import math

import jax
import jax.numpy as jnp
import ml_dtypes
import numpy as np
from jax import lax
from jax.experimental import pallas as pl
from jax.experimental.pallas import tpu as pltpu
from jax.sharding import PartitionSpec as P

OBS_DIM = 376
ACT_DIM = 17
HIDDEN_SIZE = 512
ACTOR_HIDDEN = 256
CRITICS = 5
QUANTS = 25
SLOT = 32
PADDED = 128
MERGED_SUPPORTS = 125
KEPT_ATOMS = 115
INPUTS = 393
FEATURES = 2560
SMALL_VEC = 674
LANES = 1024
EXTRA = 128
TILE = 512
MiB = 1024 * 1024

DISCOUNT = 0.99
BETA_FIRST = 0.9
BETA_SECOND = 0.999
EPSILON = 1e-08
WEIGHT_DECAY = 0.01
RATE_MATRIX = 0.05
RATE_VECTOR = 0.3
STEP_SIZE_SCALE = 0.5
LOG_TWO = math.log(2.0)
HALF_LOG_CIRCLE = 0.5 * math.log(2.0 * math.pi)
AXES = ("rows", "quant")
BF = jnp.bfloat16
F32 = jnp.float32
WHOLE = pl.BlockSpec(memory_space=pltpu.VMEM)
SCALAR = pl.BlockSpec(memory_space=pltpu.SMEM)
UNREAD = pl.BlockSpec(memory_space=pl.ANY)


def dot_nn(left, right):
    return jnp.dot(left, right, preferred_element_type=F32)


def dot_tn(left, right):
    return lax.dot_general(left, right, (((0,), (0,)), ((), ())), preferred_element_type=F32)


def dot_nt(left, right):
    return lax.dot_general(left, right, (((1,), (1,)), ((), ())), preferred_element_type=F32)


def params(limit=32, steps=0):
    semantics = ("arbitrary",) * steps if steps else None
    return pltpu.CompilerParams(vmem_limit_bytes=limit * MiB, dimension_semantics=semantics)


def cost(flops, moved):
    return pl.CostEstimate(flops=int(flops), bytes_accessed=int(moved), transcendentals=0)


def column(row):
    return jnp.transpose(jnp.broadcast_to(row, (8, row.shape[1])))[:, :1]


def fill_inputs(tall, inputs, obs, act):
    rows = obs.shape[1]
    body = OBS_DIM // 16 * 16
    inputs[:body] = obs[:body]
    tall[:8] = obs[body:OBS_DIM].astype(F32)
    tall[8 : 8 + ACT_DIM] = act.astype(F32)
    tall[8 + ACT_DIM : 32] = jnp.zeros((24 - ACT_DIM, rows), F32)
    tall[8 + ACT_DIM : 11 + ACT_DIM] = jnp.ones((3, rows), F32)
    inputs[body : body + 32] = tall[...].astype(BF)
    inputs[body + 32 :] = jnp.zeros((HIDDEN_SIZE - body - 32, rows), BF)


def actor_layers(inputs, draw, actor, small, out_scratch):
    s_one = column(small[:, :ACTOR_HIDDEN])
    s_two = column(small[:, ACTOR_HIDDEN : 2 * ACTOR_HIDDEN])
    s_three = column(small[:, 2 * ACTOR_HIDDEN : 2 * ACTOR_HIDDEN + PADDED])[: 2 * ACT_DIM]
    g_one = jnp.maximum(dot_tn(actor[:OBS_DIM], inputs) + s_one, 0.0).astype(BF)
    g_two = jnp.maximum(dot_tn(actor[OBS_DIM : OBS_DIM + ACTOR_HIDDEN], g_one) + s_two, 0.0).astype(BF)
    out_scratch[: 2 * ACT_DIM] = dot_nn(actor[OBS_DIM + ACTOR_HIDDEN :], g_two) + s_three
    mean = out_scratch[:ACT_DIM]
    log_std = out_scratch[ACT_DIM : 2 * ACT_DIM]
    scaled = jnp.exp(log_std) * draw
    pre = mean + scaled
    act = jnp.tanh(pre)
    soft = jnp.maximum(-2.0 * pre, 0.0) + jnp.log(1.0 + jnp.exp(-2.0 * jnp.abs(pre)))
    logp = jnp.sum(
        -0.5 * draw * draw - log_std - HALF_LOG_CIRCLE - 2.0 * (LOG_TWO - pre - soft),
        axis=0,
        keepdims=True,
    )
    return g_one, g_two, scaled, act, logp


def heads_kernel(me, own, got_one, got_two, got_three, small, lag_bias, out, bias_out, stage, col):
    quarter = own.shape[0]
    for k, got in enumerate((own, got_one, got_two, got_three)):
        first = pl.multiple_of((me[0] ^ k) * quarter, quarter)
        stage[pl.ds(first, quarter)] = got[...].astype(F32)
    keep = lax.broadcasted_iota(jnp.int32, (SLOT, 1), 0) < QUANTS
    bias = small[:, SMALL_VEC - PADDED :]
    both = jnp.concatenate([bias, lag_bias[...], jnp.zeros((6, PADDED), F32)], 0)
    col[:PADDED] = jnp.transpose(both)
    for e in range(CRITICS):
        rows = pl.ds(e * QUANTS, SLOT)
        out[e] = jnp.where(keep, stage[rows], 0.0).astype(BF)
        columns = jnp.where(keep, col[rows], 0.0)
        for net in range(2):
            bias_out[net, e] = jnp.broadcast_to(columns[:, net : net + 1], (SLOT, PADDED))


def heads(me, own, got, small, lag_bias):
    return pl.pallas_call(
        heads_kernel,
        in_specs=[SCALAR] + [WHOLE] * 6,
        out_specs=[WHOLE, WHOLE],
        out_shape=[
            jax.ShapeDtypeStruct((CRITICS, SLOT, 2 * HIDDEN_SIZE), BF),
            jax.ShapeDtypeStruct((2, CRITICS, SLOT, PADDED), F32),
        ],
        scratch_shapes=[pltpu.VMEM((136, 2 * HIDDEN_SIZE), F32), pltpu.VMEM((136, 8), F32)],
        compiler_params=params(),
        cost_estimate=cost(3e10, 1e6),
        name="heads",
    )(me, own, *got, small, lag_bias)


def fill_first(tall, filled, first, bias):
    body = INPUTS // 16 * 16
    high = bias.astype(BF).astype(F32)
    middle = (bias - high).astype(BF).astype(F32)
    filled[:body] = first[:body]
    tall[: INPUTS - body] = first[body:].astype(F32)
    tall[INPUTS - body : 32] = jnp.zeros((32 - INPUTS + body, HIDDEN_SIZE), F32)
    tall[INPUTS - body : INPUTS - body + 1] = high
    tall[INPUTS - body + 1 : INPUTS - body + 2] = middle
    tall[INPUTS - body + 2 : INPUTS - body + 3] = bias - high - middle
    filled[body : body + 32] = tall[...].astype(BF)
    filled[body + 32 :] = jnp.zeros((HIDDEN_SIZE - body - 32, HIDDEN_SIZE), BF)


def tiles(rows):
    width = min(rows, TILE)
    return [pl.ds(i * width, width) for i in range(rows // width)]


def critic_lanes(e):
    return pl.ds(pl.multiple_of(e * HIDDEN_SIZE, HIDDEN_SIZE), HIDDEN_SIZE)


def target_kernel(
    index, heat, inputs, logp, payoffs, done, order_in, first, second, bias, head, head_bias, after,
    lagged, keep, filled, tall_w, slots, packed, order, sems,
):
    rows = inputs.shape[1]
    mine = pl.ds(pl.multiple_of(index[0] * rows, PADDED), rows)
    copy = pltpu.make_async_copy(order_in.at[mine], order, sems.at[0])
    copy.start()
    def one_critic(e, carry):
        lanes = critic_lanes(e)
        fill_first(tall_w, filled, first[:, lanes], bias[:1, lanes])
        b_two = column(bias[1:2, lanes])
        w_two = second[:, lanes]
        for part in tiles(rows):
            h_one = jnp.maximum(dot_tn(filled[...], inputs[:, part]), 0.0).astype(BF)
            h_two = jnp.maximum(dot_tn(w_two, h_one) + b_two, 0.0).astype(BF)
            value = dot_nn(head[e, :, HIDDEN_SIZE:], h_two) + head_bias[1, e, :, :1]
            slots[pl.ds(pl.multiple_of(e * SLOT, SLOT), SLOT), part] = value
        return carry

    lax.fori_loop(0, CRITICS, one_critic, 0)
    for e in range(CRITICS):
        packed[e * QUANTS : e * QUANTS + SLOT] = slots[e * SLOT : (e + 1) * SLOT]
    copy.wait()
    for i in range(rows // PADDED):
        part = pl.ds(i * PADDED, PADDED)
        kept = (order[part] < KEPT_ATOMS).astype(F32)
        kept = jnp.concatenate([kept, jnp.zeros((PADDED, PADDED - MERGED_SUPPORTS), F32)], 1)
        keep[:, part] = jnp.transpose(kept).astype(BF)
    decay = DISCOUNT * (1.0 - done[:, mine].astype(F32))
    temperature = jnp.exp(jnp.full((1, 1), heat[0], F32))
    lagged[...] = payoffs[:, mine] + decay * (packed[:PADDED] - temperature * logp[...])


def target_pass(index, heat, inputs, logp, payoffs, done, order, first, second, bias, head, head_bias, after):
    rows = inputs.shape[1]
    return pl.pallas_call(
        target_kernel,
        in_specs=[SCALAR] * 2 + [WHOLE] * 4 + [pl.BlockSpec(memory_space=pltpu.HBM)] + [WHOLE] * 5 + [UNREAD],
        out_specs=[WHOLE] * 2,
        out_shape=[jax.ShapeDtypeStruct((PADDED, rows), F32), jax.ShapeDtypeStruct((PADDED, rows), BF)],
        scratch_shapes=[
            pltpu.VMEM((HIDDEN_SIZE, HIDDEN_SIZE), BF),
            pltpu.VMEM((32, HIDDEN_SIZE), F32),
            pltpu.VMEM((CRITICS * SLOT, rows), F32),
            pltpu.VMEM((136, rows), F32),
            pltpu.VMEM((rows, MERGED_SUPPORTS), jnp.int32),
            pltpu.SemaphoreType.DMA((1,)),
        ],
        compiler_params=params(24),
        cost_estimate=cost(7e9, 7e6),
        name="target_pass",
    )(index, heat, inputs, logp, payoffs, done, order, first, second, bias, head, head_bias, after)


HALF = 336


def two_terms(value):
    high = value.astype(BF).astype(F32)
    both = jnp.concatenate([high, value - high], 1)
    return jnp.concatenate([both, jnp.zeros((8, 2 * PADDED), F32)], 0).astype(BF)


def pilot_kernel(
    level, share, me, index, heat, obs, next_in, noise, noise_next_in, chosen, actor, small,
    first, second, bias, head, head_bias,
    own_out, send_out, x_now, x_target, logp_next,
    inputs, filled, tall_x, tall_w, dact, total, out_scratch, grad_out, small_out, next_obs, noise_next, sems,
):
    rows = obs.shape[1]
    mine = pl.ds(pl.multiple_of(index[0] * rows, PADDED), rows)
    copies = [
        pltpu.make_async_copy(next_in.at[:, mine], next_obs, sems.at[0]),
        pltpu.make_async_copy(noise_next_in.at[:, mine], noise_next, sems.at[1]),
    ]
    for copy in copies:
        copy.start()
    g_one, g_two, scaled, act, logp = actor_layers(obs[...], noise[...], actor, small, out_scratch)
    fill_inputs(tall_x, inputs, obs, act.astype(BF))
    fill_inputs(tall_x, x_now, obs, chosen[...])
    for copy in copies:
        copy.wait()
    _, _, _, next_act, next_logp = actor_layers(next_obs[...], noise_next[...], actor, small, out_scratch)
    fill_inputs(tall_x, x_target, next_obs, next_act.astype(BF))
    logp_next[...] = next_logp

    dact[...] = jnp.zeros(dact.shape, F32)
    total[...] = jnp.zeros(total.shape, F32)

    def one_critic(e, tail):
        lanes = critic_lanes(e)
        fill_first(tall_w, filled, first[:, lanes], bias[:1, lanes])
        b_two = column(bias[1:2, lanes])
        head_sum = jnp.sum(head[e, :, :HIDDEN_SIZE].astype(F32), axis=0, keepdims=True)
        weight = column(head_sum)
        push = column(head_sum * level)
        w_two = second[:, lanes]
        for part in tiles(rows):
            h_one = jnp.maximum(dot_tn(filled[...], inputs[:, part]), 0.0).astype(BF)
            h_two = jnp.maximum(dot_tn(w_two, h_one) + b_two, 0.0)
            weighted = h_two * weight
            total[:, part] += jnp.sum(weighted.reshape(-1, 8, weighted.shape[1]), axis=0)
            dz_two = jnp.where(h_two > 0, push, 0.0).astype(BF)
            grad = dot_nn(w_two, dz_two)
            dz_one = jnp.where(h_one > 0, grad, 0.0).astype(BF)
            dact[:, part] += dot_nn(first[OBS_DIM // 16 * 16 :, lanes], dz_one)
        return tail + head_bias[0, e, :, :1]

    tail = lax.fori_loop(0, CRITICS, one_critic, jnp.zeros((SLOT, 1), F32))
    temperature_share = jnp.exp(jnp.full((1, 1), heat[0], F32)) * share
    skip = OBS_DIM % 16
    action_grad = dact[skip : skip + ACT_DIM]
    pre = action_grad * (1.0 - act * act) + 2.0 * temperature_share * act
    out_scratch[:ACT_DIM] = pre
    out_scratch[ACT_DIM : 2 * ACT_DIM] = pre * scaled - temperature_share
    dout = out_scratch[: 2 * ACT_DIM].astype(BF)
    a_two = actor[OBS_DIM : OBS_DIM + ACTOR_HIDDEN]
    a_three = actor[OBS_DIM + ACTOR_HIDDEN :]
    dz_two = jnp.where(g_two > 0, dot_tn(a_three, dout), 0.0).astype(BF)
    dz_one = jnp.where(g_one > 0, dot_nn(a_two, dz_two), 0.0).astype(BF)
    grad_out[OBS_DIM + ACTOR_HIDDEN : OBS_DIM + ACTOR_HIDDEN + 2 * ACT_DIM] = dot_nt(dout, g_two)
    grad_out[OBS_DIM + ACTOR_HIDDEN + 2 * ACT_DIM :] = jnp.zeros((6, ACTOR_HIDDEN), F32)
    grad_out[OBS_DIM : OBS_DIM + ACTOR_HIDDEN] = dot_nt(g_one, dz_two)
    grad_out[:OBS_DIM] = dot_nt(obs[...], dz_one)
    ones = jnp.ones((16, rows), BF)
    small_out[...] = jnp.zeros(small_out.shape, F32)
    sum_one = dot_nt(ones, dz_one)[:1]
    sum_two = dot_nt(ones, dz_two)[:1]
    small_out[0:1] = sum_one[:, :PADDED]
    small_out[1:2] = sum_one[:, PADDED:]
    small_out[2:3] = sum_two[:, :PADDED]
    small_out[3:4] = sum_two[:, PADDED:]
    small_out[4:5, : 2 * ACT_DIM] = dot_nt(ones, dout)[:1]
    pilot_total = jnp.sum(total[...]) + rows * jnp.sum(tail)
    small_out[5:6] = jnp.broadcast_to(pilot_total, (1, PADDED))
    small_out[6:7] = jnp.broadcast_to(jnp.sum(logp), (1, PADDED))
    packed = two_terms(small_out[...])
    side = me[0] & 1
    for out, which in ((own_out, side), (send_out, 1 - side)):
        out[:HALF] = grad_out[pl.ds(pl.multiple_of(which * HALF, 16), HALF)].astype(BF)
        out[HALF:] = packed


def pilot_pass(
    level, share, me, index, heat, obs, next_obs, noise, noise_next, chosen, actor, small,
    first, second, bias, head, head_bias,
):
    rows = obs.shape[1]
    far = pl.BlockSpec(memory_space=pltpu.HBM)
    filled = jax.ShapeDtypeStruct((HIDDEN_SIZE, rows), BF)
    return pl.pallas_call(
        functools.partial(pilot_kernel, level, share),
        in_specs=[SCALAR] * 3 + [WHOLE, far, WHOLE, far] + [WHOLE] * 8,
        out_specs=[WHOLE] * 5,
        out_shape=[jax.ShapeDtypeStruct((HALF + 16, ACTOR_HIDDEN), BF)] * 2
        + [filled, filled, jax.ShapeDtypeStruct((1, rows), F32)],
        scratch_shapes=[
            pltpu.VMEM((HIDDEN_SIZE, rows), BF),
            pltpu.VMEM((HIDDEN_SIZE, HIDDEN_SIZE), BF),
            pltpu.VMEM((32, rows), F32),
            pltpu.VMEM((32, HIDDEN_SIZE), F32),
            pltpu.VMEM((INPUTS - OBS_DIM // 16 * 16, rows), F32),
            pltpu.VMEM((8, rows), F32),
            pltpu.VMEM((40, rows), F32),
            pltpu.VMEM((2 * HALF, ACTOR_HIDDEN), F32),
            pltpu.VMEM((8, PADDED), F32),
            pltpu.VMEM((OBS_DIM, rows), BF),
            pltpu.VMEM((ACT_DIM, rows), F32),
            pltpu.SemaphoreType.DMA((2,)),
        ],
        compiler_params=params(24),
        cost_estimate=cost(14e9, 9e6),
        name="pilot_pass",
    )(me, index, heat, obs, next_obs, noise, noise_next, chosen, actor, small, first, second, bias, head, head_bias)


def pair_terms(q_ref, lagged, keep, parts, rows):
    def group(i, carry):
        part = pl.ds(pl.multiple_of(i * PADDED, PADDED), PADDED)
        q = q_ref[:, part]
        shift = jnp.sum(q, axis=0, keepdims=True) * (1.0 / QUANTS)
        y = (lagged[:, part] - shift).astype(BF).reshape(8, 16, PADDED)
        upper = keep[:, part].reshape(8, 16, PADDED)
        lower = -upper
        q_ref[:, part] = q - shift
        for j in range(QUANTS):
            level = jnp.broadcast_to(q_ref[j : j + 1, part], (16, PADDED)).astype(BF)
            d = y - level[None]
            c = jnp.minimum(jnp.maximum(d, lower), upper)
            half = c * jnp.asarray(0.5, BF)
            g = half + jnp.abs(c) * jnp.asarray((j + 0.5) / QUANTS - 0.5, BF)
            h = g * (d - half)
            g = g[:4] + g[4:]
            g = g[:2] + g[2:]
            parts[j * 16 : j * 16 + 16, part] = g[0] + g[1]
            h = h[:4] + h[4:]
            h = h[:2] + h[2:]
            parts[(QUANTS + j) * 16 : (QUANTS + j) * 16 + 16, part] = h[0] + h[1]
        return carry

    lax.fori_loop(0, rows // PADDED, group, 0)
    shape = (48, 2 * QUANTS * 16)
    row = lax.broadcasted_iota(jnp.int32, shape, 0)
    owner = jnp.minimum(lax.broadcasted_iota(jnp.int32, shape, 1) // 16, SLOT)
    owner = jnp.where(owner >= QUANTS, SLOT, owner)
    return dot_nn((row == owner).astype(F32).astype(BF), parts[...])


PARITY = 18


def granules(e):
    mine = range(32 * e, 32 * e + 32)
    return [[g for g in mine if g // CRITICS % 2 == parity] for parity in range(2)]


def granule_places(chunk):
    places = np.zeros(CRITICS * 32, np.int32)
    for i, e in enumerate(chunk):
        for way in granules(e):
            for t, g in enumerate(way):
                places[g] = i * PARITY + t
    return places


SENT = (6, 6, 6, 4)


def store_piece(outs, t, value):
    for out in outs:
        if t < out.shape[0]:
            out[t] = value
            return
        t -= out.shape[0]


def critic_kernel(
    e, waits, rows_scale, split, me, inputs, lagged, keep, first, second, bias, head, head_bias, *refs,
):
    last = e == CRITICS - 1
    refs = refs[waits:]
    if e:
        before, refs = refs[:3], refs[3:]
    outs, scratch = refs[:-9], refs[-9:]
    filled, tall_w, h_one, h_two, q, parts, grads, packed, extra = scratch
    rows = inputs.shape[1]
    lanes = slice(e * HIDDEN_SIZE, (e + 1) * HIDDEN_SIZE)
    second = second.at[:, lanes]
    head = head.at[e : e + 1, :, :HIDDEN_SIZE]
    head_bias = head_bias.at[:1, e : e + 1]
    fill_first(tall_w, filled, first[:, lanes], bias[:1, lanes])
    b_two = column(bias[1:2, lanes])
    for part in tiles(rows):
        one = jnp.maximum(dot_tn(filled[...], inputs[:, part]), 0.0).astype(BF)
        h_one[:, part] = one
        two = jnp.maximum(dot_tn(second[...], one) + b_two, 0.0).astype(BF)
        h_two[:, part] = two
        q[:, part] = dot_nn(head[0], two) + head_bias[0, 0, :, :1]
    terms = pair_terms(q, lagged, keep, parts, rows)
    low = (terms[:SLOT] * -rows_scale).astype(BF)
    loss = terms[SLOT : SLOT + 1]
    head_grad = dot_nt(low, h_two[...])
    count = jnp.ones((8, rows), BF)
    bias_grad = dot_nt(count, low)[:1]
    sums = jnp.zeros((HIDDEN_SIZE, PADDED), F32)
    for part in tiles(rows):
        two = h_two[:, part]
        dz_two = jnp.where(two > 0, dot_tn(head[0], low[:, part.start : part.start + part.size]), 0.0)
        for i in range(part.size // PADDED):
            sums = sums + dz_two[:, i * PADDED : (i + 1) * PADDED]
        dz_two = dz_two.astype(BF)
        h_two[:, part] = dz_two
        one = h_one[:, part]
        h_one[:, part] = jnp.where(one > 0, dot_nn(second[...], dz_two), 0.0).astype(BF)
        second_part = dot_nt(dz_two, one)
        second_grad = second_grad + second_part if part.start else second_part
    grads[:, :, :HIDDEN_SIZE] = second_grad.astype(BF).reshape(-1, 16, HIDDEN_SIZE)
    first_grad = dot_nt(h_one[...], inputs[...])
    grads[:, :, HIDDEN_SIZE : LANES - PADDED] = (
        first_grad[:, : HIDDEN_SIZE - PADDED].astype(BF).reshape(-1, 16, HIDDEN_SIZE - PADDED)
    )
    lane = lax.broadcasted_iota(jnp.int32, (HIDDEN_SIZE, PADDED), 1)
    tail = jnp.where(
        lane == INPUTS + 1 - HIDDEN_SIZE + PADDED,
        jnp.sum(sums, axis=1, keepdims=True),
        first_grad[:, HIDDEN_SIZE - PADDED :],
    )
    grads[:, :, LANES - PADDED : LANES] = tail.astype(BF).reshape(-1, 16, PADDED)
    direct = split[0] > 0
    rest = outs[1 + (len(SENT) if last else 1) :] if direct else outs[1:]
    if not last:
        all_heads, all_bias, all_loss = rest
        if e:
            all_heads[...] = before[0][...]
            all_bias[...] = before[1][...]
            all_loss[...] = before[2][...] + loss
        else:
            all_heads[...] = jnp.zeros(all_heads.shape, F32)
            all_bias[...] = jnp.zeros(all_bias.shape, F32)
            all_loss[...] = loss
        all_heads[e * SLOT : (e + 1) * SLOT] = head_grad
        all_bias[e : e + 1, :SLOT] = bias_grad
    else:
        n_rows, n_quant = split
        for i in range(CRITICS):
            packed[i * QUANTS : i * QUANTS + SLOT] = (
                before[0][i * SLOT : (i + 1) * SLOT] if i < e else head_grad
            )
        bias_row = jnp.zeros((1, PADDED), F32)
        lane = lax.broadcasted_iota(jnp.int32, (1, PADDED), 1)
        spare = jnp.zeros((1, PADDED - SLOT), F32)
        for i in range(CRITICS):
            piece = before[1][i : i + 1] if i < e else jnp.concatenate([bias_grad, spare], 1)
            piece = pltpu.roll(jnp.broadcast_to(piece, (8, PADDED)), i * QUANTS, 1)[:1]
            inside = (lane >= i * QUANTS) & (lane < (i + 1) * QUANTS)
            bias_row = jnp.where(inside, piece, bias_row)
        value = jnp.sum(before[2][...] + loss, axis=1, keepdims=True) * rows_scale
        value = jnp.broadcast_to(value, (1, PADDED))
        if direct:
            width = HIDDEN_SIZE // n_rows
            high = PADDED // n_quant
            lane = lax.broadcasted_iota(jnp.int32, (16, PADDED), 1)
            halves = [bias_row, pltpu.roll(jnp.broadcast_to(bias_row, (8, PADDED)), 64, 1)[:1], value]
            common = jnp.concatenate(halves + [jnp.zeros((13, PADDED), F32)], 0)
            for j in range(8):
                y, c = j // 4, j % 4
                for z in range(n_rows // 2):
                    r = 2 * z + y
                    block = packed[c * high : (c + 1) * high, r // 2 * PADDED : (r // 2 + 1) * PADDED]
                    if r % 2 == 0:
                        block = pltpu.roll(block, width, 1)
                    base = 2 * z * PADDED
                    extra[j, :, base : base + PADDED] = jnp.where(lane < 64, common, block[:16]).astype(BF)
                    extra[j, :, base + PADDED : base + 2 * PADDED] = block[16:].astype(BF)
        else:
            rest[0][...] = packed[:PADDED]
            rest[1][...] = jnp.concatenate([bias_row, value, jnp.zeros((6, PADDED), F32)], 0)
    if not direct:
        outs[0][...] = grads[...]
        return
    sent, kept = outs[: len(SENT) if last else 1], outs[len(SENT) if last else 1]
    side = me[0] & 1
    ways = granules(e)
    for t in range(max(map(len, ways))):
        pair = [way[min(t, len(way) - 1)] - e * 32 for way in ways]
        kept[t] = grads[jnp.where(side == 0, pair[0], pair[1])]
        store_piece(sent, t, grads[jnp.where(side == 0, pair[1], pair[0])])
    if last:
        for i in range(4):
            kept[PARITY + i] = extra[2 * i + side]
            store_piece(sent, PARITY + i, extra[2 * i + 1 - side])


def critic_pass(e, rows_scale, split, me, inputs, lagged, keep, first, second, bias, head, head_bias, after, before):
    rows = inputs.shape[1]
    last = e == CRITICS - 1
    if split[0]:
        block = lambda count: jax.ShapeDtypeStruct((count, 16, LANES), BF)
        sent = SENT if last else (PARITY,)
        out_shape = [block(count) for count in sent] + [block(sum(sent))]
    else:
        out_shape = [jax.ShapeDtypeStruct((HIDDEN_SIZE // 16, 16, LANES), BF)]
    if not last:
        out_shape += [
            jax.ShapeDtypeStruct((CRITICS * SLOT, HIDDEN_SIZE), F32),
            jax.ShapeDtypeStruct((8, PADDED), F32),
            jax.ShapeDtypeStruct((1, rows), F32),
        ]
    elif not split[0]:
        out_shape += [
            jax.ShapeDtypeStruct((PADDED, HIDDEN_SIZE), F32),
            jax.ShapeDtypeStruct((8, PADDED), F32),
        ]
    return pl.pallas_call(
        functools.partial(critic_kernel, e, len(after), rows_scale, split),
        in_specs=[SCALAR] + [WHOLE] * 8 + [UNREAD] * len(after) + [WHOLE] * len(before),
        out_specs=[WHOLE] * len(out_shape),
        out_shape=out_shape,
        scratch_shapes=[
            pltpu.VMEM((HIDDEN_SIZE, HIDDEN_SIZE), BF),
            pltpu.VMEM((32, HIDDEN_SIZE), F32),
            pltpu.VMEM((HIDDEN_SIZE, rows), BF),
            pltpu.VMEM((HIDDEN_SIZE, rows), BF),
            pltpu.VMEM((SLOT, rows), F32),
            pltpu.VMEM((2 * QUANTS * 16, rows), BF),
            pltpu.VMEM((HIDDEN_SIZE // 16, 16, LANES), BF),
            pltpu.VMEM((136, HIDDEN_SIZE), F32),
            pltpu.VMEM((8, 16, LANES), BF),
        ],
        compiler_params=params(24),
        cost_estimate=cost(7e9, 4e6),
        name="critic_pass",
    )(me, inputs, lagged, keep, first, second, bias, head, head_bias, *after, *before)


def add_kernel(a, b, out):
    out[:HALF] = (a[:HALF].astype(F32) + b[:HALF].astype(F32)).astype(BF)
    pair = [r[HALF:].astype(F32) for r in (a, b)]
    pair = [p[:8, :PADDED] + p[:8, PADDED:] for p in pair]
    out[HALF:] = two_terms(pair[0] + pair[1])


def add_actor(a, b):
    return pl.pallas_call(
        add_kernel,
        in_specs=[WHOLE, WHOLE],
        out_specs=WHOLE,
        out_shape=jax.ShapeDtypeStruct(a.shape, BF),
        compiler_params=params(),
        cost_estimate=cost(1e5, 6e5),
        name="add_actor",
    )(a, b)


def core_kernel(chunk, depth, waits, me, places, *refs):
    count = len(chunk)
    refs = refs[waits:]
    kept, got, outs, sums = refs[:count], refs[count:-3], refs[-3:-1], refs[-1]
    size = count * PARITY
    first = 0
    for piece in got:
        i, inside = min(first // PARITY, count - 1), first - min(first // PARITY, count - 1) * PARITY
        own = kept[i][inside : inside + piece.shape[0]]
        sums[first : first + piece.shape[0]] = (own.astype(F32) + piece[...].astype(F32)).astype(BF)
        first += piece.shape[0]
    z_first = chunk[-1] // 3 * depth
    side = me[0] & 1
    for k in range(4):
        flip = (0, 4 - 2 * side, 2 + 2 * side, 6)[k]
        j = (me[0] & 7) ^ flip
        out = outs[k // 2]
        for z in range(depth):
            owner = (z_first + z) * 8 + j
            for i in range(CRITICS):
                out[k % 2, z * CRITICS + i] = sums[places[owner * CRITICS + i]]
        if chunk[-1] == CRITICS - 1:
            out[k % 2, depth * CRITICS] = sums[size + j // 2]


def add_core(chunk, depth, me, kept, got, after=()):
    tail = kept[-1].shape[0] - PARITY
    count = depth * CRITICS + (1 if tail else 0)
    return pl.pallas_call(
        functools.partial(core_kernel, chunk, depth, len(after)),
        in_specs=[SCALAR, SCALAR] + [UNREAD] * len(after) + [WHOLE] * (len(kept) + len(got)),
        out_specs=[WHOLE] * 2,
        out_shape=[jax.ShapeDtypeStruct((2, count, 16, LANES), BF)] * 2,
        scratch_shapes=[pltpu.VMEM((len(kept) * PARITY + tail, 16, LANES), BF)],
        compiler_params=params(),
        cost_estimate=cost(1e6, 8e6),
        name="add_core",
    )(me, jnp.asarray(granule_places(chunk)), *after, *kept, *got)


def tree(values):
    while len(values) > 1:
        values = [a + b for a, b in zip(values[::2], values[1::2])]
    return values[0]


def half_kernel(kept, got, own, send):
    for k, out in enumerate((own, send)):
        out[...] = (kept[k].astype(F32) + got[k].astype(F32)).astype(BF)


def add_half(kept, got, after=()):
    waits = len(after)
    return pl.pallas_call(
        lambda *refs: half_kernel(*refs[waits:]),
        in_specs=[UNREAD] * waits + [WHOLE] * 2,
        out_specs=[WHOLE] * 2,
        out_shape=[jax.ShapeDtypeStruct(kept.shape[1:], BF)] * 2,
        compiler_params=params(8),
        cost_estimate=cost(1e5, 1e5),
        name="add_half",
    )(*after, kept, got)


def line_kernel(me, early, early_got, late, late_got, *refs):
    outs, sums = refs[:-1], refs[-1]
    count = early.shape[0]
    sums[:count] = (early[...].astype(F32) + early_got[...].astype(F32)).astype(BF)
    total = late[...].astype(F32) + late_got[...].astype(F32)
    sums[count:] = total[:count].astype(BF)
    extra = total[count]
    lane = lax.broadcasted_iota(jnp.int32, (16, PADDED), 1)
    for z in range(len(outs)):
        first = extra[:, 2 * z * PADDED : (2 * z + 1) * PADDED]
        second = extra[:, (2 * z + 1) * PADDED : (2 * z + 2) * PADDED]
        for i, value in enumerate((first, second, pltpu.roll(first, 64, 1))):
            old = sums[z * CRITICS + i, :, LANES - PADDED :].astype(F32)
            sums[z * CRITICS + i, :, LANES - PADDED :] = jnp.where(lane < 64, old, value).astype(BF)
    for k, out in enumerate(outs):
        first = ((me[0] // 8) ^ k) * CRITICS
        for i in range(CRITICS):
            out[i] = sums[first + i]


def add_line(me, early, late, depth, after=()):
    waits = len(after)
    return pl.pallas_call(
        lambda *refs: line_kernel(*refs[waits:]),
        in_specs=[UNREAD] * waits + [SCALAR] + [WHOLE] * 4,
        out_specs=[WHOLE] * depth,
        out_shape=[jax.ShapeDtypeStruct((CRITICS, 16, LANES), BF)] * depth,
        scratch_shapes=[pltpu.VMEM((2 * early[0].shape[0], 16, LANES), BF)],
        compiler_params=params(),
        cost_estimate=cost(1e6, 6e6),
        name="add_line",
    )(*after, me, *early, *late)


def adamw(weight, first, second, grad, rate, factors, outs):
    first_new = BETA_FIRST * first[...] + (1.0 - BETA_FIRST) * grad
    second_new = BETA_SECOND * second[...] + (1.0 - BETA_SECOND) * grad * grad
    old = weight[...]
    step = (first_new * factors[0]) / (jnp.sqrt(second_new * factors[1]) + EPSILON)
    outs[0][...] = old - rate * (step + WEIGHT_DECAY * old)
    outs[1][...] = first_new
    outs[2][...] = second_new


def row_kernel(*refs):
    total = tree([r[2, :, LANES - PADDED :].astype(F32) for r in refs[:-1]])
    total = pltpu.roll(total, 64, 1)
    row = jnp.concatenate([total[:1, :64], total[1:2, :64]], 1)
    refs[-1][...] = jnp.concatenate([row, jnp.broadcast_to(total[2:3, :1], (7, PADDED))], 0)


def sum_row(blocks):
    return pl.pallas_call(
        row_kernel,
        in_specs=[WHOLE] * len(blocks),
        out_specs=WHOLE,
        out_shape=jax.ShapeDtypeStruct((8, PADDED), F32),
        compiler_params=params(8),
        cost_estimate=cost(1e5, 1e5),
        name="sum_row",
    )(*blocks)


def update_kernel(count, direct, factors, *refs):
    blocks, refs = refs[:count], refs[count:]
    if direct:
        total = tree([b[...].astype(F32) for b in blocks]).reshape(-1, LANES)
        head_grad = pltpu.roll(total[:SLOT, LANES - PADDED :], 64, 1)[:, :64]
    else:
        total = blocks[0][...]
        head_grad, refs = refs[0][...], refs[1:]
    state, outs = refs[:12], refs[12:]
    adamw(*state[0:3], total[:, HIDDEN_SIZE : HIDDEN_SIZE + INPUTS], RATE_MATRIX, factors, outs[0:3])
    adamw(*state[3:6], total[:, :HIDDEN_SIZE], RATE_MATRIX, factors, outs[3:6])
    edge = INPUTS - HIDDEN_SIZE + PADDED
    bias_grad = jnp.transpose(total[:, LANES - PADDED :])[edge : edge + 2]
    adamw(*state[6:9], bias_grad, RATE_VECTOR, factors, outs[6:9])
    adamw(*state[9:12], head_grad, RATE_MATRIX, factors, outs[9:12])


def update(factors, blocks, others, state):
    shapes = [jax.ShapeDtypeStruct(a.shape, F32) for a in state]
    count = len(blocks)
    return pl.pallas_call(
        functools.partial(update_kernel, count, not others),
        in_specs=[SCALAR] + [WHOLE] * (count + len(others) + len(state)),
        out_specs=[WHOLE] * len(shapes),
        out_shape=shapes,
        compiler_params=params(),
        cost_estimate=cost(2e6, 6e6),
        name="update",
    )(factors, *blocks, *others, *state)


def actor_update_kernel(me, factors, own, peer, *refs):
    state, outs, grad = refs[:3], refs[3:7], refs[7]
    side = me[0] & 1
    grad[pl.ds(pl.multiple_of(side * HALF, 16), HALF)] = own[:HALF].astype(F32)
    grad[pl.ds(pl.multiple_of((1 - side) * HALF, 16), HALF)] = peer[:HALF].astype(F32)
    adamw(*state, grad[: state[0].shape[0]], RATE_MATRIX, factors, outs[:3])
    pair = own[HALF:].astype(F32)
    outs[3][...] = pair[:8, :PADDED] + pair[:8, PADDED:]


def actor_update(me, factors, own, peer, state):
    shapes = [jax.ShapeDtypeStruct(a.shape, F32) for a in state] + [jax.ShapeDtypeStruct((8, PADDED), F32)]
    return pl.pallas_call(
        actor_update_kernel,
        in_specs=[SCALAR, SCALAR] + [WHOLE] * (2 + len(state)),
        out_specs=[WHOLE] * len(shapes),
        out_shape=shapes,
        scratch_shapes=[pltpu.VMEM((2 * HALF, ACTOR_HIDDEN), F32)],
        compiler_params=params(),
        cost_estimate=cost(2e6, 5e6),
        name="actor_update",
    )(me, factors, own, peer, *state)


def small_update_kernel(samples, me, factors, row_own, row_peer, small_sums, *refs):
    state, outs, vector = refs[:6], refs[6:13], refs[13]
    row = jnp.where((me[0] & 1) == 0, row_own[...], row_peer[...])
    for i in range(4):
        vector[i * PADDED : (i + 1) * PADDED] = small_sums[i]
    wide = jnp.concatenate([row, jnp.zeros((8, PADDED), F32)], 1)
    wide = pltpu.roll(wide, 2 * ACT_DIM, 1)
    wide = wide + jnp.concatenate([small_sums[4:5], jnp.zeros((1, PADDED), F32)], 1)
    vector[4 * PADDED :] = wide[0]
    adamw(*state[:3], vector[:SMALL_VEC], RATE_VECTOR, factors, outs[1:4])
    heat = state[3][...]
    logp_sum = small_sums[6:7, :1]
    shortfall = (ACT_DIM * samples - logp_sum) / samples
    adamw(*state[3:6], shortfall, STEP_SIZE_SCALE, factors, outs[4:7])
    actor_loss = (jnp.exp(heat) * logp_sum - small_sums[5:6, :1] / MERGED_SUPPORTS) / samples
    outs[0][...] = row[1:2, :1] + actor_loss + heat * shortfall


def small_update(samples, me, factors, row, row_peer, small_sums, state):
    shapes = [jax.ShapeDtypeStruct((1, 1), F32)] + [jax.ShapeDtypeStruct(a.shape, F32) for a in state]
    return pl.pallas_call(
        functools.partial(small_update_kernel, samples),
        in_specs=[SCALAR, SCALAR] + [WHOLE] * (3 + len(state)),
        out_specs=[WHOLE] * len(shapes),
        out_shape=shapes,
        scratch_shapes=[pltpu.VMEM((6 * PADDED,), F32)],
        compiler_params=params(8),
        cost_estimate=cost(1e6, 1e5),
        name="small_update",
    )(me, factors, row, row_peer, small_sums, *state)


def exchange(value, flip):
    count = lax.axis_size("rows") * lax.axis_size("quant")
    return lax.ppermute(value, AXES, [(i, i ^ flip) for i in range(count)])


def exchange_sides(value, even, odd):
    count = lax.axis_size("rows") * lax.axis_size("quant")
    return lax.ppermute(value, AXES, [(i, i ^ (odd if i % 2 else even)) for i in range(count)])


def all_sum(value):
    total = lax.axis_size("rows") * lax.axis_size("quant")
    flip = 1
    while flip < total:
        value = value + exchange(value, flip)
        flip *= 2
    return value


def scatter_sum(pieces):
    total = pieces.shape[0]
    flip = total // 2
    while flip:
        low = pieces.astype(BF)
        pieces = low[:flip].astype(F32) + exchange(low[flip:], flip).astype(F32)
        flip //= 2
    return pieces[0]


def local(
    obs, chosen, noise_now, next_obs, noise_next, payoffs, done, order,
    w_one, w_two, biases, head_part, t_one, t_two, t_biases, t_head_part, t_head_bias,
    actor, counter,
    in_w, in_m, in_v, mid_w, mid_m, mid_v, bias_w, bias_m, bias_v, head_w, head_m, head_v,
    actor_w, actor_m, actor_v, small_w, small_m, small_v, heat, heat_m, heat_v,
):
    n_rows, n_quant = lax.axis_size("rows"), lax.axis_size("quant")
    devices = n_rows * n_quant
    rows = obs.shape[0]
    samples = rows * devices
    index = lax.axis_index("quant").reshape(1)
    device = lax.axis_index("rows") * n_quant + lax.axis_index("quant")
    me = device.reshape(1)
    direct = n_rows == 8 and n_quant == 4
    small_row = small_w.reshape(1, -1)
    tally = counter.astype(F32)
    factors = jnp.concatenate(
        [1.0 / (1.0 - jnp.power(BETA_FIRST, tally)), 1.0 / (1.0 - jnp.power(BETA_SECOND, tally))]
    )

    own_head = jnp.concatenate([head_part.T, t_head_part.T], 1)
    got = [
        lax.ppermute(own_head, "quant", [(i, i ^ k) for i in range(n_quant)]) for k in (1, 2, 3)
    ]
    head, head_bias = heads(index, own_head, got, small_row, t_head_bias.reshape(1, -1))

    level = float(np.asarray(-1.0 / (MERGED_SUPPORTS * samples), ml_dtypes.bfloat16))
    own, send, x_now, x_target, logp = pilot_pass(
        level, 1.0 / samples, me, index, heat, obs.T, next_obs.T, noise_now.T, noise_next.T, chosen.T,
        actor, small_row, w_one, w_two, biases, head, head_bias,
    )
    lagged, keep = target_pass(
        index, heat, x_target, logp, payoffs.reshape(1, -1), done.reshape(1, -1), order,
        t_one, t_two, t_biases, head, head_bias, own,
    )
    own = add_actor(own, exchange(send, 1))
    flips = [1 << i for i in range(1, devices.bit_length() - 1)]
    scale = 1.0 / (samples * MERGED_SUPPORTS * KEPT_ATOMS)
    split = (n_rows, n_quant) if direct else (0, 0)
    kept, got, before, early = [], [], (), None
    for e in range(CRITICS):
        after = [own] if e < 4 else []
        if direct and e == CRITICS - 1:
            early = add_core((0, 1, 2), 2, me, kept[:3], got[:3])
            early = [early[0], exchange_sides(early[1], 2, 4)]
            after = [early[0]]
        outs = critic_pass(
            e, scale, split, me, x_now, lagged, keep, w_one, w_two, biases, head, head_bias, after, before
        )
        if direct:
            count = len(SENT) if e == CRITICS - 1 else 1
            got.extend(exchange(piece, 1) for piece in outs[:count])
            outs = outs[count:]
        kept.append(outs[0])
        before = outs[1:]
        for flip in flips[e : e + 1] if e < CRITICS - 1 else flips[e:]:
            own = add_actor(own, exchange(own, flip))
    peer = exchange(own, 1)
    *actor_new, small_sums = actor_update(me, factors, own, peer, (actor_w, actor_m, actor_v))

    if direct:
        early = add_half(*early)
        late = add_core((2, 3, 4), 2, me, kept[2:], got[2:], (early[0],))
        early = [early[0], exchange_sides(early[1], 4, 2)]
        late = add_half(late[0], exchange_sides(late[1], 2, 4), (own, early[1]))
        late = [late[0], exchange_sides(late[1], 4, 2)]
        blocks = add_line(me, early, late, n_rows // 2, (small_sums,))
        blocks = [blocks[0]] + [exchange(blocks[k], 8 * k) for k in range(1, len(blocks))]
        others = []
        row = sum_row(blocks)
        row_peer = exchange(row, 1)
    else:
        grads = jnp.stack(kept).reshape(devices, -1, LANES)
        order_of = device ^ jnp.arange(devices)
        blocks = [scatter_sum(jnp.take(grads, order_of, axis=0))]
        head_grad = before[0].reshape(n_quant, PADDED // n_quant, n_rows, HIDDEN_SIZE // n_rows)
        head_grad = head_grad.transpose(2, 0, 1, 3).reshape((devices,) + (PADDED // n_quant, -1))
        head_grad = scatter_sum(jnp.take(head_grad, order_of, axis=0))
        others = [head_grad]
        row = row_peer = all_sum(before[1])
    state = (
        in_w.T, in_m.T, in_v.T, mid_w.T, mid_m.T, mid_v.T, bias_w, bias_m, bias_v, head_w.T, head_m.T, head_v.T,
    )
    new = update(factors, blocks, others, state)
    state = (
        small_w, small_m, small_v,
        heat.reshape(1, 1), heat_m.reshape(1, 1), heat_v.reshape(1, 1),
    )
    objective, *last = small_update(samples, me, factors, row, row_peer, small_sums, state)
    return (
        objective.reshape(()),
        *(a.T for a in new[:6]),
        *new[6:9],
        *(a.T for a in new[9:]),
        *actor_new,
        *last[:3],
        *(a.reshape(-1) for a in last[3:]),
    )


def solution(mesh):
    both, row, none = P(AXES), P("rows"), P()
    column_of, shard = P(None, "quant"), P(None, AXES)
    placed = (
        (both,) * 3 + (row,) * 5 + (none,) * 3 + (column_of,) + (none,) * 3 + (column_of,) + (none,) * 3
        + (shard,) * 9 + (P("rows", "quant"),) * 3 + (none,) * 9
    )
    return jax.shard_map(
        local,
        mesh=mesh,
        in_specs=placed,
        out_specs=(none,) + (shard,) * 9 + (P("rows", "quant"),) * 3 + (none,) * 9,
        check_vma=False,
    )
```

```python
import functools
import math

import jax
import jax.numpy as jnp
import ml_dtypes
import numpy as np
from jax import lax
from jax.experimental import pallas as pl
from jax.experimental.pallas import tpu as pltpu
from jax.sharding import PartitionSpec as P

OBS_DIM = 376
ACT_DIM = 17
HIDDEN_SIZE = 512
ACTOR_HIDDEN = 256
CRITICS = 5
QUANTS = 25
SLOT = 32
PADDED = 128
MERGED_SUPPORTS = 125
KEPT_ATOMS = 115
INPUTS = 393
FEATURES = 2560
SMALL_VEC = 674
LANES = 1024
EXTRA = 128
TILE = 1024
CRITIC_TILE = 512
MiB = 1024 * 1024

DISCOUNT = 0.99
BETA_FIRST = 0.9
BETA_SECOND = 0.999
EPSILON = 1e-08
WEIGHT_DECAY = 0.01
RATE_MATRIX = 0.05
RATE_VECTOR = 0.3
STEP_SIZE_SCALE = 0.5
LOG_TWO = math.log(2.0)
HALF_LOG_CIRCLE = 0.5 * math.log(2.0 * math.pi)
AXES = ("rows", "quant")
BF = jnp.bfloat16
F32 = jnp.float32
WHOLE = pl.BlockSpec(memory_space=pltpu.VMEM)
SCALAR = pl.BlockSpec(memory_space=pltpu.SMEM)
UNREAD = pl.BlockSpec(memory_space=pl.ANY)


def dot_nn(left, right):
    return jnp.dot(left, right, preferred_element_type=F32)


def dot_tn(left, right):
    return lax.dot_general(left, right, (((0,), (0,)), ((), ())), preferred_element_type=F32)


def dot_nt(left, right):
    return lax.dot_general(left, right, (((1,), (1,)), ((), ())), preferred_element_type=F32)


def params(limit=32, steps=0):
    semantics = ("arbitrary",) * steps if steps else None
    return pltpu.CompilerParams(vmem_limit_bytes=limit * MiB, dimension_semantics=semantics)


def cost(flops, moved):
    return pl.CostEstimate(flops=int(flops), bytes_accessed=int(moved), transcendentals=0)


def column(row):
    return jnp.transpose(jnp.broadcast_to(row, (8, row.shape[1])))[:, :1]


def fill_inputs(tall, inputs, obs, act):
    rows = obs.shape[1]
    body = OBS_DIM // 16 * 16
    inputs[:body] = obs[:body]
    tall[:8] = obs[body:OBS_DIM].astype(F32)
    tall[8 : 8 + ACT_DIM] = act.astype(F32)
    tall[8 + ACT_DIM : 32] = jnp.zeros((24 - ACT_DIM, rows), F32)
    tall[8 + ACT_DIM : 11 + ACT_DIM] = jnp.ones((3, rows), F32)
    inputs[body : body + 32] = tall[...].astype(BF)
    inputs[body + 32 :] = jnp.zeros((HIDDEN_SIZE - body - 32, rows), BF)


def actor_layers(inputs, draw, actor, small, out_scratch):
    s_one = column(small[:, :ACTOR_HIDDEN])
    s_two = column(small[:, ACTOR_HIDDEN : 2 * ACTOR_HIDDEN])
    s_three = column(small[:, 2 * ACTOR_HIDDEN : 2 * ACTOR_HIDDEN + PADDED])[: 2 * ACT_DIM]
    g_one = jnp.maximum(dot_tn(actor[:OBS_DIM], inputs) + s_one, 0.0).astype(BF)
    g_two = jnp.maximum(dot_tn(actor[OBS_DIM : OBS_DIM + ACTOR_HIDDEN], g_one) + s_two, 0.0).astype(BF)
    out_scratch[: 2 * ACT_DIM] = dot_nn(actor[OBS_DIM + ACTOR_HIDDEN :], g_two) + s_three
    mean = out_scratch[:ACT_DIM]
    log_std = out_scratch[ACT_DIM : 2 * ACT_DIM]
    scaled = jnp.exp(log_std) * draw
    pre = mean + scaled
    act = jnp.tanh(pre)
    soft = jnp.maximum(-2.0 * pre, 0.0) + jnp.log(1.0 + jnp.exp(-2.0 * jnp.abs(pre)))
    logp = jnp.sum(
        -0.5 * draw * draw - log_std - HALF_LOG_CIRCLE - 2.0 * (LOG_TWO - pre - soft),
        axis=0,
        keepdims=True,
    )
    return g_one, g_two, scaled, act, logp


def heads_kernel(me, own, got_one, got_two, got_three, out, stage):
    quarter = own.shape[0]
    for k, got in enumerate((own, got_one, got_two, got_three)):
        first = pl.multiple_of((me[0] ^ k) * quarter, quarter)
        stage[pl.ds(first, quarter)] = got[...].astype(F32)
    keep = lax.broadcasted_iota(jnp.int32, (SLOT, 1), 0) < QUANTS
    for e in range(CRITICS):
        out[e] = jnp.where(keep, stage[e * QUANTS : e * QUANTS + SLOT], 0.0).astype(BF)


def heads(me, own, got):
    return pl.pallas_call(
        heads_kernel,
        in_specs=[SCALAR] + [WHOLE] * 4,
        out_specs=WHOLE,
        out_shape=jax.ShapeDtypeStruct((CRITICS, SLOT, 2 * HIDDEN_SIZE), BF),
        scratch_shapes=[pltpu.VMEM((136, 2 * HIDDEN_SIZE), F32)],
        compiler_params=params(4),
        cost_estimate=cost(3e10, 1e6),
        name="heads",
    )(me, own, *got)


def fill_biases(small, lag_bias, out, col):
    keep = lax.broadcasted_iota(jnp.int32, (SLOT, 1), 0) < QUANTS
    both = jnp.concatenate([small[:, SMALL_VEC - PADDED :], lag_bias[...], jnp.zeros((6, PADDED), F32)], 0)
    col[:PADDED] = jnp.transpose(both)
    for e in range(CRITICS):
        columns = jnp.where(keep, col[e * QUANTS : e * QUANTS + SLOT], 0.0)
        for net in range(2):
            out[net, e] = jnp.broadcast_to(columns[:, net : net + 1], (SLOT, PADDED))


def fill_first(tall, filled, first, bias):
    body = INPUTS // 16 * 16
    high = bias.astype(BF).astype(F32)
    middle = (bias - high).astype(BF).astype(F32)
    filled[:body] = first[:body]
    tall[: INPUTS - body] = first[body:].astype(F32)
    tall[INPUTS - body : 32] = jnp.zeros((32 - INPUTS + body, HIDDEN_SIZE), F32)
    tall[INPUTS - body : INPUTS - body + 1] = high
    tall[INPUTS - body + 1 : INPUTS - body + 2] = middle
    tall[INPUTS - body + 2 : INPUTS - body + 3] = bias - high - middle
    filled[body : body + 32] = tall[...].astype(BF)
    filled[body + 32 :] = jnp.zeros((HIDDEN_SIZE - body - 32, HIDDEN_SIZE), BF)


def tiles(rows, width=TILE):
    width = min(rows, width)
    return [pl.ds(i * width, width) for i in range(rows // width)]


def critic_lanes(e):
    return pl.ds(pl.multiple_of(e * HIDDEN_SIZE, HIDDEN_SIZE), HIDDEN_SIZE)


def target_kernel(
    index, heat, inputs, logp, payoffs, done, order_in, first, second, bias, head, head_bias, after,
    lagged, keep, filled, tall_w, slots, packed, order, sems,
):
    rows = inputs.shape[1]
    mine = pl.ds(pl.multiple_of(index[0] * rows, PADDED), rows)
    copy = pltpu.make_async_copy(order_in.at[mine], order, sems.at[0])
    copy.start()
    def one_critic(e, carry):
        lanes = critic_lanes(e)
        fill_first(tall_w, filled, first[:, lanes], bias[:1, lanes])
        b_two = column(bias[1:2, lanes])
        w_two = second[:, lanes]
        for part in tiles(rows):
            h_one = jnp.maximum(dot_tn(filled[...], inputs[:, part]), 0.0).astype(BF)
            h_two = jnp.maximum(dot_tn(w_two, h_one) + b_two, 0.0).astype(BF)
            value = dot_nn(head[e, :, HIDDEN_SIZE:], h_two) + head_bias[1, e, :, :1]
            slots[pl.ds(pl.multiple_of(e * SLOT, SLOT), SLOT), part] = value
        return carry

    lax.fori_loop(0, CRITICS, one_critic, 0)
    for e in range(CRITICS):
        packed[e * QUANTS : e * QUANTS + SLOT] = slots[e * SLOT : (e + 1) * SLOT]
    copy.wait()
    for i in range(rows // PADDED):
        part = pl.ds(i * PADDED, PADDED)
        kept = (order[part] < KEPT_ATOMS).astype(F32)
        kept = jnp.concatenate([kept, jnp.zeros((PADDED, PADDED - MERGED_SUPPORTS), F32)], 1)
        keep[:, part] = jnp.transpose(kept).astype(BF)
    decay = DISCOUNT * (1.0 - done[:, mine].astype(F32))
    temperature = jnp.exp(jnp.full((1, 1), heat[0], F32))
    lagged[...] = payoffs[:, mine] + decay * (packed[:PADDED] - temperature * logp[...])


def target_pass(index, heat, inputs, logp, payoffs, done, order, first, second, bias, head, head_bias, after):
    rows = inputs.shape[1]
    return pl.pallas_call(
        target_kernel,
        in_specs=[SCALAR] * 2 + [WHOLE] * 4 + [pl.BlockSpec(memory_space=pltpu.HBM)] + [WHOLE] * 5 + [UNREAD],
        out_specs=[WHOLE] * 2,
        out_shape=[jax.ShapeDtypeStruct((PADDED, rows), F32), jax.ShapeDtypeStruct((PADDED, rows), BF)],
        scratch_shapes=[
            pltpu.VMEM((HIDDEN_SIZE, HIDDEN_SIZE), BF),
            pltpu.VMEM((32, HIDDEN_SIZE), F32),
            pltpu.VMEM((CRITICS * SLOT, rows), F32),
            pltpu.VMEM((136, rows), F32),
            pltpu.VMEM((rows, MERGED_SUPPORTS), jnp.int32),
            pltpu.SemaphoreType.DMA((1,)),
        ],
        compiler_params=params(24),
        cost_estimate=cost(7e9, 7e6),
        name="target_pass",
    )(index, heat, inputs, logp, payoffs, done, order, first, second, bias, head, head_bias, after)


HALF = 336


def two_terms(value):
    high = value.astype(BF).astype(F32)
    both = jnp.concatenate([high, value - high], 1)
    return jnp.concatenate([both, jnp.zeros((8, 2 * PADDED), F32)], 0).astype(BF)


def pilot_kernel(
    level, share, me, index, heat, obs, next_in, noise, noise_next_in, chosen, actor, small,
    first_in, second_in, bias, head, lag_bias,
    own_out, send_out, x_now, x_target, logp_next, head_bias,
    inputs, filled, tall_x, tall_w, dact, total, out_scratch, grad_out, small_out, next_obs, noise_next, col,
    first, second, sems,
):
    rows = obs.shape[1]
    mine = pl.ds(pl.multiple_of(index[0] * rows, PADDED), rows)
    copies = [
        pltpu.make_async_copy(next_in.at[:, mine], next_obs, sems.at[0]),
        pltpu.make_async_copy(noise_next_in.at[:, mine], noise_next, sems.at[1]),
        pltpu.make_async_copy(first_in, first, sems.at[2]),
        pltpu.make_async_copy(second_in, second, sems.at[3]),
    ]
    for copy in copies:
        copy.start()
    g_one, g_two, scaled, act, logp = actor_layers(obs[...], noise[...], actor, small, out_scratch)
    fill_inputs(tall_x, inputs, obs, act.astype(BF))
    fill_inputs(tall_x, x_now, obs, chosen[...])
    for copy in copies[:2]:
        copy.wait()
    _, _, _, next_act, next_logp = actor_layers(next_obs[...], noise_next[...], actor, small, out_scratch)
    fill_inputs(tall_x, x_target, next_obs, next_act.astype(BF))
    logp_next[...] = next_logp
    fill_biases(small, lag_bias, head_bias, col)
    for copy in copies[2:]:
        copy.wait()

    dact[...] = jnp.zeros(dact.shape, F32)
    total[...] = jnp.zeros(total.shape, F32)

    def one_critic(e, tail):
        lanes = critic_lanes(e)
        fill_first(tall_w, filled, first[:, lanes], bias[:1, lanes])
        b_two = column(bias[1:2, lanes])
        head_sum = jnp.sum(head[e, :, :HIDDEN_SIZE].astype(F32), axis=0, keepdims=True)
        weight = column(head_sum)
        push = column(head_sum * level)
        w_two = second[:, lanes]
        for part in tiles(rows):
            h_one = jnp.maximum(dot_tn(filled[...], inputs[:, part]), 0.0).astype(BF)
            h_two = jnp.maximum(dot_tn(w_two, h_one) + b_two, 0.0)
            weighted = h_two * weight
            total[:, part] += jnp.sum(weighted.reshape(-1, 8, weighted.shape[1]), axis=0)
            dz_two = jnp.where(h_two > 0, push, 0.0).astype(BF)
            grad = dot_nn(w_two, dz_two)
            dz_one = jnp.where(h_one > 0, grad, 0.0).astype(BF)
            dact[:, part] += dot_nn(first[OBS_DIM // 16 * 16 :, lanes], dz_one)
        return tail + head_bias[0, e, :, :1]

    tail = lax.fori_loop(0, CRITICS, one_critic, jnp.zeros((SLOT, 1), F32))
    temperature_share = jnp.exp(jnp.full((1, 1), heat[0], F32)) * share
    skip = OBS_DIM % 16
    action_grad = dact[skip : skip + ACT_DIM]
    pre = action_grad * (1.0 - act * act) + 2.0 * temperature_share * act
    out_scratch[:ACT_DIM] = pre
    out_scratch[ACT_DIM : 2 * ACT_DIM] = pre * scaled - temperature_share
    dout = out_scratch[: 2 * ACT_DIM].astype(BF)
    a_two = actor[OBS_DIM : OBS_DIM + ACTOR_HIDDEN]
    a_three = actor[OBS_DIM + ACTOR_HIDDEN :]
    dz_two = jnp.where(g_two > 0, dot_tn(a_three, dout), 0.0).astype(BF)
    dz_one = jnp.where(g_one > 0, dot_nn(a_two, dz_two), 0.0).astype(BF)
    grad_out[OBS_DIM + ACTOR_HIDDEN : OBS_DIM + ACTOR_HIDDEN + 2 * ACT_DIM] = dot_nt(dout, g_two)
    grad_out[OBS_DIM + ACTOR_HIDDEN + 2 * ACT_DIM :] = jnp.zeros((6, ACTOR_HIDDEN), F32)
    grad_out[OBS_DIM : OBS_DIM + ACTOR_HIDDEN] = dot_nt(g_one, dz_two)
    grad_out[:OBS_DIM] = dot_nt(obs[...], dz_one)
    ones = jnp.ones((16, rows), BF)
    small_out[...] = jnp.zeros(small_out.shape, F32)
    sum_one = dot_nt(ones, dz_one)[:1]
    sum_two = dot_nt(ones, dz_two)[:1]
    small_out[0:1] = sum_one[:, :PADDED]
    small_out[1:2] = sum_one[:, PADDED:]
    small_out[2:3] = sum_two[:, :PADDED]
    small_out[3:4] = sum_two[:, PADDED:]
    small_out[4:5, : 2 * ACT_DIM] = dot_nt(ones, dout)[:1]
    pilot_total = jnp.sum(total[...]) + rows * jnp.sum(tail)
    small_out[5:6] = jnp.broadcast_to(pilot_total, (1, PADDED))
    small_out[6:7] = jnp.broadcast_to(jnp.sum(logp), (1, PADDED))
    packed = two_terms(small_out[...])
    side = me[0] & 1
    for out, which in ((own_out, side), (send_out, 1 - side)):
        out[:HALF] = grad_out[pl.ds(pl.multiple_of(which * HALF, 16), HALF)].astype(BF)
        out[HALF:] = packed


def pilot_pass(
    level, share, me, index, heat, obs, next_obs, noise, noise_next, chosen, actor, small,
    first, second, bias, head, lag_bias,
):
    rows = obs.shape[1]
    far = pl.BlockSpec(memory_space=pltpu.HBM)
    filled = jax.ShapeDtypeStruct((HIDDEN_SIZE, rows), BF)
    return pl.pallas_call(
        functools.partial(pilot_kernel, level, share),
        in_specs=[SCALAR] * 3 + [WHOLE, far, WHOLE, far] + [WHOLE] * 3 + [far] * 2 + [WHOLE] * 3,
        out_specs=[WHOLE] * 6,
        out_shape=[jax.ShapeDtypeStruct((HALF + 16, ACTOR_HIDDEN), BF)] * 2
        + [filled, filled, jax.ShapeDtypeStruct((1, rows), F32)]
        + [jax.ShapeDtypeStruct((2, CRITICS, SLOT, PADDED), F32)],
        scratch_shapes=[
            pltpu.VMEM((HIDDEN_SIZE, rows), BF),
            pltpu.VMEM((HIDDEN_SIZE, HIDDEN_SIZE), BF),
            pltpu.VMEM((32, rows), F32),
            pltpu.VMEM((32, HIDDEN_SIZE), F32),
            pltpu.VMEM((INPUTS - OBS_DIM // 16 * 16, rows), F32),
            pltpu.VMEM((8, rows), F32),
            pltpu.VMEM((40, rows), F32),
            pltpu.VMEM((2 * HALF, ACTOR_HIDDEN), F32),
            pltpu.VMEM((8, PADDED), F32),
            pltpu.VMEM((OBS_DIM, rows), BF),
            pltpu.VMEM((ACT_DIM, rows), F32),
            pltpu.VMEM((136, 8), F32),
            pltpu.VMEM(first.shape, BF),
            pltpu.VMEM(second.shape, BF),
            pltpu.SemaphoreType.DMA((4,)),
        ],
        compiler_params=params(48),
        cost_estimate=cost(14e9, 9e6),
        name="pilot_pass",
    )(me, index, heat, obs, next_obs, noise, noise_next, chosen, actor, small, first, second, bias, head, lag_bias)


def pair_terms(q_ref, lagged, keep, parts, rows):
    def group(i, carry):
        part = pl.ds(pl.multiple_of(i * PADDED, PADDED), PADDED)
        q = q_ref[:, part]
        shift = jnp.sum(q, axis=0, keepdims=True) * (1.0 / QUANTS)
        y = (lagged[:, part] - shift).astype(BF).reshape(8, 16, PADDED)
        upper = keep[:, part].reshape(8, 16, PADDED)
        lower = -upper
        q_ref[:, part] = q - shift
        for j in range(QUANTS):
            level = jnp.broadcast_to(q_ref[j : j + 1, part], (16, PADDED)).astype(BF)
            d = y - level[None]
            c = jnp.minimum(jnp.maximum(d, lower), upper)
            half = c * jnp.asarray(0.5, BF)
            g = half + jnp.abs(c) * jnp.asarray((j + 0.5) / QUANTS - 0.5, BF)
            h = g * (d - half)
            g = g[:4] + g[4:]
            g = g[:2] + g[2:]
            parts[j * 16 : j * 16 + 16, part] = g[0] + g[1]
            h = h[:4] + h[4:]
            h = h[:2] + h[2:]
            parts[(QUANTS + j) * 16 : (QUANTS + j) * 16 + 16, part] = h[0] + h[1]
        return carry

    lax.fori_loop(0, rows // PADDED, group, 0)
    shape = (48, 2 * QUANTS * 16)
    row = lax.broadcasted_iota(jnp.int32, shape, 0)
    owner = jnp.minimum(lax.broadcasted_iota(jnp.int32, shape, 1) // 16, SLOT)
    owner = jnp.where(owner >= QUANTS, SLOT, owner)
    return dot_nn((row == owner).astype(F32).astype(BF), parts[...])


PARITY = 18


def granules(e):
    mine = range(32 * e, 32 * e + 32)
    return [[g for g in mine if g // CRITICS % 2 == parity] for parity in range(2)]


def granule_places(chunk):
    places = np.zeros(CRITICS * 32, np.int32)
    for i, e in enumerate(chunk):
        for way in granules(e):
            for t, g in enumerate(way):
                places[g] = i * PARITY + t
    return places


SENT = (6, 6, 6, 4)


def store_piece(outs, t, value):
    for out in outs:
        if t < out.shape[0]:
            out[t] = value
            return
        t -= out.shape[0]


def critic_kernel(
    e, waits, rows_scale, split, me, inputs, lagged, keep, first, second, bias, head, head_bias, *refs,
):
    last = e == CRITICS - 1
    refs = refs[waits:]
    if e:
        before, refs = refs[:3], refs[3:]
    outs, scratch = refs[:-9], refs[-9:]
    filled, tall_w, h_one, h_two, q, parts, grads, packed, extra = scratch
    rows = inputs.shape[1]
    lanes = slice(e * HIDDEN_SIZE, (e + 1) * HIDDEN_SIZE)
    second = second.at[:, lanes]
    head = head.at[e : e + 1, :, :HIDDEN_SIZE]
    head_bias = head_bias.at[:1, e : e + 1]
    fill_first(tall_w, filled, first[:, lanes], bias[:1, lanes])
    b_two = column(bias[1:2, lanes])
    for part in tiles(rows, CRITIC_TILE):
        h_one[:, part] = jnp.maximum(dot_tn(filled[...], inputs[:, part]), 0.0).astype(BF)
    for part in tiles(rows, CRITIC_TILE):
        h_two[:, part] = jnp.maximum(dot_tn(second[...], h_one[:, part]) + b_two, 0.0).astype(BF)
    for part in tiles(rows, CRITIC_TILE):
        q[:, part] = dot_nn(head[0], h_two[:, part]) + head_bias[0, 0, :, :1]
    terms = pair_terms(q, lagged, keep, parts, rows)
    low = (terms[:SLOT] * -rows_scale).astype(BF)
    loss = terms[SLOT : SLOT + 1]
    head_grad = dot_nt(low, h_two[...])
    count = jnp.ones((8, rows), BF)
    bias_grad = dot_nt(count, low)[:1]
    sums = jnp.zeros((HIDDEN_SIZE, PADDED), F32)
    for part in tiles(rows, CRITIC_TILE):
        two = h_two[:, part]
        dz_two = jnp.where(two > 0, dot_tn(head[0], low[:, part.start : part.start + part.size]), 0.0)
        for i in range(part.size // PADDED):
            sums = sums + dz_two[:, i * PADDED : (i + 1) * PADDED]
        h_two[:, part] = dz_two.astype(BF)
    second_grad = dot_nt(h_two[...], h_one[...])
    for part in tiles(rows, CRITIC_TILE):
        one = h_one[:, part]
        h_one[:, part] = jnp.where(one > 0, dot_nn(second[...], h_two[:, part]), 0.0).astype(BF)
    grads[:, :, :HIDDEN_SIZE] = second_grad.astype(BF).reshape(-1, 16, HIDDEN_SIZE)
    first_grad = dot_nt(h_one[...], inputs[...])
    grads[:, :, HIDDEN_SIZE : LANES - PADDED] = (
        first_grad[:, : HIDDEN_SIZE - PADDED].astype(BF).reshape(-1, 16, HIDDEN_SIZE - PADDED)
    )
    lane = lax.broadcasted_iota(jnp.int32, (HIDDEN_SIZE, PADDED), 1)
    tail = jnp.where(
        lane == INPUTS + 1 - HIDDEN_SIZE + PADDED,
        jnp.sum(sums, axis=1, keepdims=True),
        first_grad[:, HIDDEN_SIZE - PADDED :],
    )
    grads[:, :, LANES - PADDED : LANES] = tail.astype(BF).reshape(-1, 16, PADDED)
    direct = split[0] > 0
    rest = outs[1 + (len(SENT) if last else 1) :] if direct else outs[1:]
    if not last:
        all_heads, all_bias, all_loss = rest
        if e:
            all_heads[...] = before[0][...]
            all_bias[...] = before[1][...]
            all_loss[...] = before[2][...] + loss
        else:
            all_heads[...] = jnp.zeros(all_heads.shape, F32)
            all_bias[...] = jnp.zeros(all_bias.shape, F32)
            all_loss[...] = loss
        all_heads[e * SLOT : (e + 1) * SLOT] = head_grad
        all_bias[e : e + 1, :SLOT] = bias_grad
    else:
        n_rows, n_quant = split
        for i in range(CRITICS):
            packed[i * QUANTS : i * QUANTS + SLOT] = (
                before[0][i * SLOT : (i + 1) * SLOT] if i < e else head_grad
            )
        bias_row = jnp.zeros((1, PADDED), F32)
        lane = lax.broadcasted_iota(jnp.int32, (1, PADDED), 1)
        spare = jnp.zeros((1, PADDED - SLOT), F32)
        for i in range(CRITICS):
            piece = before[1][i : i + 1] if i < e else jnp.concatenate([bias_grad, spare], 1)
            piece = pltpu.roll(jnp.broadcast_to(piece, (8, PADDED)), i * QUANTS, 1)[:1]
            inside = (lane >= i * QUANTS) & (lane < (i + 1) * QUANTS)
            bias_row = jnp.where(inside, piece, bias_row)
        value = jnp.sum(before[2][...] + loss, axis=1, keepdims=True) * rows_scale
        value = jnp.broadcast_to(value, (1, PADDED))
        if direct:
            width = HIDDEN_SIZE // n_rows
            high = PADDED // n_quant
            lane = lax.broadcasted_iota(jnp.int32, (16, PADDED), 1)
            halves = [bias_row, pltpu.roll(jnp.broadcast_to(bias_row, (8, PADDED)), 64, 1)[:1], value]
            common = jnp.concatenate(halves + [jnp.zeros((13, PADDED), F32)], 0)
            for j in range(8):
                y, c = j // 4, j % 4
                for z in range(n_rows // 2):
                    r = 2 * z + y
                    block = packed[c * high : (c + 1) * high, r // 2 * PADDED : (r // 2 + 1) * PADDED]
                    if r % 2 == 0:
                        block = pltpu.roll(block, width, 1)
                    base = 2 * z * PADDED
                    extra[j, :, base : base + PADDED] = jnp.where(lane < 64, common, block[:16]).astype(BF)
                    extra[j, :, base + PADDED : base + 2 * PADDED] = block[16:].astype(BF)
        else:
            rest[0][...] = packed[:PADDED]
            rest[1][...] = jnp.concatenate([bias_row, value, jnp.zeros((6, PADDED), F32)], 0)
    if not direct:
        outs[0][...] = grads[...]
        return
    sent, kept = outs[: len(SENT) if last else 1], outs[len(SENT) if last else 1]
    side = me[0] & 1
    ways = granules(e)
    for t in range(max(map(len, ways))):
        pair = [way[min(t, len(way) - 1)] - e * 32 for way in ways]
        kept[t] = grads[jnp.where(side == 0, pair[0], pair[1])]
        store_piece(sent, t, grads[jnp.where(side == 0, pair[1], pair[0])])
    if last:
        for i in range(4):
            kept[PARITY + i] = extra[2 * i + side]
            store_piece(sent, PARITY + i, extra[2 * i + 1 - side])


def critic_pass(e, rows_scale, split, me, inputs, lagged, keep, first, second, bias, head, head_bias, after, before):
    rows = inputs.shape[1]
    last = e == CRITICS - 1
    if split[0]:
        block = lambda count: jax.ShapeDtypeStruct((count, 16, LANES), BF)
        sent = SENT if last else (PARITY,)
        out_shape = [block(count) for count in sent] + [block(sum(sent))]
    else:
        out_shape = [jax.ShapeDtypeStruct((HIDDEN_SIZE // 16, 16, LANES), BF)]
    if not last:
        out_shape += [
            jax.ShapeDtypeStruct((CRITICS * SLOT, HIDDEN_SIZE), F32),
            jax.ShapeDtypeStruct((8, PADDED), F32),
            jax.ShapeDtypeStruct((1, rows), F32),
        ]
    elif not split[0]:
        out_shape += [
            jax.ShapeDtypeStruct((PADDED, HIDDEN_SIZE), F32),
            jax.ShapeDtypeStruct((8, PADDED), F32),
        ]
    return pl.pallas_call(
        functools.partial(critic_kernel, e, len(after), rows_scale, split),
        in_specs=[SCALAR] + [WHOLE] * 8 + [UNREAD] * len(after) + [WHOLE] * len(before),
        out_specs=[WHOLE] * len(out_shape),
        out_shape=out_shape,
        scratch_shapes=[
            pltpu.VMEM((HIDDEN_SIZE, HIDDEN_SIZE), BF),
            pltpu.VMEM((32, HIDDEN_SIZE), F32),
            pltpu.VMEM((HIDDEN_SIZE, rows), BF),
            pltpu.VMEM((HIDDEN_SIZE, rows), BF),
            pltpu.VMEM((SLOT, rows), F32),
            pltpu.VMEM((2 * QUANTS * 16, rows), BF),
            pltpu.VMEM((HIDDEN_SIZE // 16, 16, LANES), BF),
            pltpu.VMEM((136, HIDDEN_SIZE), F32),
            pltpu.VMEM((8, 16, LANES), BF),
        ],
        compiler_params=params(24),
        cost_estimate=cost(7e9, 4e6),
        name="critic_pass",
    )(me, inputs, lagged, keep, first, second, bias, head, head_bias, *after, *before)


def add_kernel(a, b, out):
    out[:HALF] = (a[:HALF].astype(F32) + b[:HALF].astype(F32)).astype(BF)
    pair = [r[HALF:].astype(F32) for r in (a, b)]
    pair = [p[:8, :PADDED] + p[:8, PADDED:] for p in pair]
    out[HALF:] = two_terms(pair[0] + pair[1])


def add_actor(a, b):
    return pl.pallas_call(
        add_kernel,
        in_specs=[WHOLE, WHOLE],
        out_specs=WHOLE,
        out_shape=jax.ShapeDtypeStruct(a.shape, BF),
        compiler_params=params(),
        cost_estimate=cost(1e5, 6e5),
        name="add_actor",
    )(a, b)


def core_kernel(chunk, depth, waits, me, places, *refs):
    count = len(chunk)
    refs = refs[waits:]
    kept, got, outs, sums = refs[:count], refs[count:-3], refs[-3:-1], refs[-1]
    size = count * PARITY
    first = 0
    for piece in got:
        i, inside = min(first // PARITY, count - 1), first - min(first // PARITY, count - 1) * PARITY
        own = kept[i][inside : inside + piece.shape[0]]
        sums[first : first + piece.shape[0]] = (own.astype(F32) + piece[...].astype(F32)).astype(BF)
        first += piece.shape[0]
    z_first = chunk[-1] // 3 * depth
    side = me[0] & 1
    for k in range(4):
        flip = (0, 4 - 2 * side, 2 + 2 * side, 6)[k]
        j = (me[0] & 7) ^ flip
        out = outs[k // 2]
        for z in range(depth):
            owner = (z_first + z) * 8 + j
            for i in range(CRITICS):
                out[k % 2, z * CRITICS + i] = sums[places[owner * CRITICS + i]]
        if chunk[-1] == CRITICS - 1:
            out[k % 2, depth * CRITICS] = sums[size + j // 2]


def add_core(chunk, depth, me, kept, got, after=()):
    tail = kept[-1].shape[0] - PARITY
    count = depth * CRITICS + (1 if tail else 0)
    return pl.pallas_call(
        functools.partial(core_kernel, chunk, depth, len(after)),
        in_specs=[SCALAR, SCALAR] + [UNREAD] * len(after) + [WHOLE] * (len(kept) + len(got)),
        out_specs=[WHOLE] * 2,
        out_shape=[jax.ShapeDtypeStruct((2, count, 16, LANES), BF)] * 2,
        scratch_shapes=[pltpu.VMEM((len(kept) * PARITY + tail, 16, LANES), BF)],
        compiler_params=params(),
        cost_estimate=cost(1e6, 8e6),
        name="add_core",
    )(me, jnp.asarray(granule_places(chunk)), *after, *kept, *got)


def tree(values):
    while len(values) > 1:
        values = [a + b for a, b in zip(values[::2], values[1::2])]
    return values[0]


def half_kernel(kept, got, own, send):
    for k, out in enumerate((own, send)):
        out[...] = (kept[k].astype(F32) + got[k].astype(F32)).astype(BF)


def add_half(kept, got, after=()):
    waits = len(after)
    return pl.pallas_call(
        lambda *refs: half_kernel(*refs[waits:]),
        in_specs=[UNREAD] * waits + [WHOLE] * 2,
        out_specs=[WHOLE] * 2,
        out_shape=[jax.ShapeDtypeStruct(kept.shape[1:], BF)] * 2,
        compiler_params=params(8),
        cost_estimate=cost(1e5, 1e5),
        name="add_half",
    )(*after, kept, got)


def line_kernel(me, early, early_got, late, late_got, *refs):
    outs, sums = refs[:-1], refs[-1]
    count = early.shape[0]
    sums[:count] = (early[...].astype(F32) + early_got[...].astype(F32)).astype(BF)
    total = late[...].astype(F32) + late_got[...].astype(F32)
    sums[count:] = total[:count].astype(BF)
    extra = total[count]
    lane = lax.broadcasted_iota(jnp.int32, (16, PADDED), 1)
    for z in range(len(outs)):
        first = extra[:, 2 * z * PADDED : (2 * z + 1) * PADDED]
        second = extra[:, (2 * z + 1) * PADDED : (2 * z + 2) * PADDED]
        for i, value in enumerate((first, second, pltpu.roll(first, 64, 1))):
            old = sums[z * CRITICS + i, :, LANES - PADDED :].astype(F32)
            sums[z * CRITICS + i, :, LANES - PADDED :] = jnp.where(lane < 64, old, value).astype(BF)
    for k, out in enumerate(outs):
        first = ((me[0] // 8) ^ k) * CRITICS
        for i in range(CRITICS):
            out[i] = sums[first + i]


def add_line(me, early, late, depth, after=()):
    waits = len(after)
    return pl.pallas_call(
        lambda *refs: line_kernel(*refs[waits:]),
        in_specs=[UNREAD] * waits + [SCALAR] + [WHOLE] * 4,
        out_specs=[WHOLE] * depth,
        out_shape=[jax.ShapeDtypeStruct((CRITICS, 16, LANES), BF)] * depth,
        scratch_shapes=[pltpu.VMEM((2 * early[0].shape[0], 16, LANES), BF)],
        compiler_params=params(),
        cost_estimate=cost(1e6, 6e6),
        name="add_line",
    )(*after, me, *early, *late)


def adamw(weight, first, second, grad, rate, factors, outs):
    first_new = BETA_FIRST * first[...] + (1.0 - BETA_FIRST) * grad
    second_new = BETA_SECOND * second[...] + (1.0 - BETA_SECOND) * grad * grad
    old = weight[...]
    step = (first_new * factors[0]) / (jnp.sqrt(second_new * factors[1]) + EPSILON)
    outs[0][...] = old - rate * (step + WEIGHT_DECAY * old)
    outs[1][...] = first_new
    outs[2][...] = second_new


def row_kernel(*refs):
    total = tree([r[2, :, LANES - PADDED :].astype(F32) for r in refs[:-1]])
    total = pltpu.roll(total, 64, 1)
    row = jnp.concatenate([total[:1, :64], total[1:2, :64]], 1)
    refs[-1][...] = jnp.concatenate([row, jnp.broadcast_to(total[2:3, :1], (7, PADDED))], 0)


def sum_row(blocks):
    return pl.pallas_call(
        row_kernel,
        in_specs=[WHOLE] * len(blocks),
        out_specs=WHOLE,
        out_shape=jax.ShapeDtypeStruct((8, PADDED), F32),
        compiler_params=params(8),
        cost_estimate=cost(1e5, 1e5),
        name="sum_row",
    )(*blocks)


def update_kernel(count, direct, factors, *refs):
    blocks, refs = refs[:count], refs[count:]
    if direct:
        total = tree([b[...].astype(F32) for b in blocks]).reshape(-1, LANES)
        head_grad = pltpu.roll(total[:SLOT, LANES - PADDED :], 64, 1)[:, :64]
    else:
        total = blocks[0][...]
        head_grad, refs = refs[0][...], refs[1:]
    state, outs = refs[:12], refs[12:]
    adamw(*state[0:3], total[:, HIDDEN_SIZE : HIDDEN_SIZE + INPUTS], RATE_MATRIX, factors, outs[0:3])
    adamw(*state[3:6], total[:, :HIDDEN_SIZE], RATE_MATRIX, factors, outs[3:6])
    edge = INPUTS - HIDDEN_SIZE + PADDED
    bias_grad = jnp.transpose(total[:, LANES - PADDED :])[edge : edge + 2]
    adamw(*state[6:9], bias_grad, RATE_VECTOR, factors, outs[6:9])
    adamw(*state[9:12], head_grad, RATE_MATRIX, factors, outs[9:12])


def update(factors, blocks, others, state):
    shapes = [jax.ShapeDtypeStruct(a.shape, F32) for a in state]
    count = len(blocks)
    return pl.pallas_call(
        functools.partial(update_kernel, count, not others),
        in_specs=[SCALAR] + [WHOLE] * (count + len(others) + len(state)),
        out_specs=[WHOLE] * len(shapes),
        out_shape=shapes,
        compiler_params=params(),
        cost_estimate=cost(2e6, 6e6),
        name="update",
    )(factors, *blocks, *others, *state)


def actor_update_kernel(me, factors, own, peer, *refs):
    state, outs, grad = refs[:3], refs[3:7], refs[7]
    side = me[0] & 1
    grad[pl.ds(pl.multiple_of(side * HALF, 16), HALF)] = own[:HALF].astype(F32)
    grad[pl.ds(pl.multiple_of((1 - side) * HALF, 16), HALF)] = peer[:HALF].astype(F32)
    adamw(*state, grad[: state[0].shape[0]], RATE_MATRIX, factors, outs[:3])
    pair = own[HALF:].astype(F32)
    outs[3][...] = pair[:8, :PADDED] + pair[:8, PADDED:]


def actor_update(me, factors, own, peer, state):
    shapes = [jax.ShapeDtypeStruct(a.shape, F32) for a in state] + [jax.ShapeDtypeStruct((8, PADDED), F32)]
    return pl.pallas_call(
        actor_update_kernel,
        in_specs=[SCALAR, SCALAR] + [WHOLE] * (2 + len(state)),
        out_specs=[WHOLE] * len(shapes),
        out_shape=shapes,
        scratch_shapes=[pltpu.VMEM((2 * HALF, ACTOR_HIDDEN), F32)],
        compiler_params=params(),
        cost_estimate=cost(2e6, 5e6),
        name="actor_update",
    )(me, factors, own, peer, *state)


def small_update_kernel(samples, me, factors, row_own, row_peer, small_sums, *refs):
    state, outs, vector = refs[:6], refs[6:13], refs[13]
    row = jnp.where((me[0] & 1) == 0, row_own[...], row_peer[...])
    for i in range(4):
        vector[i * PADDED : (i + 1) * PADDED] = small_sums[i]
    wide = jnp.concatenate([row, jnp.zeros((8, PADDED), F32)], 1)
    wide = pltpu.roll(wide, 2 * ACT_DIM, 1)
    wide = wide + jnp.concatenate([small_sums[4:5], jnp.zeros((1, PADDED), F32)], 1)
    vector[4 * PADDED :] = wide[0]
    adamw(*state[:3], vector[:SMALL_VEC], RATE_VECTOR, factors, outs[1:4])
    heat = state[3][...]
    logp_sum = small_sums[6:7, :1]
    shortfall = (ACT_DIM * samples - logp_sum) / samples
    adamw(*state[3:6], shortfall, STEP_SIZE_SCALE, factors, outs[4:7])
    actor_loss = (jnp.exp(heat) * logp_sum - small_sums[5:6, :1] / MERGED_SUPPORTS) / samples
    outs[0][...] = row[1:2, :1] + actor_loss + heat * shortfall


def small_update(samples, me, factors, row, row_peer, small_sums, state):
    shapes = [jax.ShapeDtypeStruct((1, 1), F32)] + [jax.ShapeDtypeStruct(a.shape, F32) for a in state]
    return pl.pallas_call(
        functools.partial(small_update_kernel, samples),
        in_specs=[SCALAR, SCALAR] + [WHOLE] * (3 + len(state)),
        out_specs=[WHOLE] * len(shapes),
        out_shape=shapes,
        scratch_shapes=[pltpu.VMEM((6 * PADDED,), F32)],
        compiler_params=params(8),
        cost_estimate=cost(1e6, 1e5),
        name="small_update",
    )(me, factors, row, row_peer, small_sums, *state)


def exchange(value, flip):
    count = lax.axis_size("rows") * lax.axis_size("quant")
    return lax.ppermute(value, AXES, [(i, i ^ flip) for i in range(count)])


def exchange_sides(value, even, odd):
    count = lax.axis_size("rows") * lax.axis_size("quant")
    return lax.ppermute(value, AXES, [(i, i ^ (odd if i % 2 else even)) for i in range(count)])


def all_sum(value):
    total = lax.axis_size("rows") * lax.axis_size("quant")
    flip = 1
    while flip < total:
        value = value + exchange(value, flip)
        flip *= 2
    return value


def scatter_sum(pieces):
    total = pieces.shape[0]
    flip = total // 2
    while flip:
        low = pieces.astype(BF)
        pieces = low[:flip].astype(F32) + exchange(low[flip:], flip).astype(F32)
        flip //= 2
    return pieces[0]


def local(
    obs, chosen, noise_now, next_obs, noise_next, payoffs, done, order,
    w_one, w_two, biases, head_part, t_one, t_two, t_biases, t_head_part, t_head_bias,
    actor, counter,
    in_w, in_m, in_v, mid_w, mid_m, mid_v, bias_w, bias_m, bias_v, head_w, head_m, head_v,
    actor_w, actor_m, actor_v, small_w, small_m, small_v, heat, heat_m, heat_v,
):
    n_rows, n_quant = lax.axis_size("rows"), lax.axis_size("quant")
    devices = n_rows * n_quant
    rows = obs.shape[0]
    samples = rows * devices
    index = lax.axis_index("quant").reshape(1)
    device = lax.axis_index("rows") * n_quant + lax.axis_index("quant")
    me = device.reshape(1)
    direct = n_rows == 8 and n_quant == 4
    small_row = small_w.reshape(1, -1)
    tally = counter.astype(F32)
    factors = jnp.concatenate(
        [1.0 / (1.0 - jnp.power(BETA_FIRST, tally)), 1.0 / (1.0 - jnp.power(BETA_SECOND, tally))]
    )

    own_head = jnp.concatenate([head_part.T, t_head_part.T], 1)
    got = [
        lax.ppermute(own_head, "quant", [(i, i ^ k) for i in range(n_quant)]) for k in (1, 2, 3)
    ]
    head = heads(index, own_head, got)

    level = float(np.asarray(-1.0 / (MERGED_SUPPORTS * samples), ml_dtypes.bfloat16))
    own, send, x_now, x_target, logp, head_bias = pilot_pass(
        level, 1.0 / samples, me, index, heat, obs.T, next_obs.T, noise_now.T, noise_next.T, chosen.T,
        actor, small_row, w_one, w_two, biases, head, t_head_bias.reshape(1, -1),
    )
    lagged, keep = target_pass(
        index, heat, x_target, logp, payoffs.reshape(1, -1), done.reshape(1, -1), order,
        t_one, t_two, t_biases, head, head_bias, own,
    )
    own = add_actor(own, exchange(send, 1))
    flips = [1 << i for i in range(1, devices.bit_length() - 1)]
    scale = 1.0 / (samples * MERGED_SUPPORTS * KEPT_ATOMS)
    split = (n_rows, n_quant) if direct else (0, 0)
    kept, got, before, early = [], [], (), None
    for e in range(CRITICS):
        after = [own] if e < 4 else []
        if direct and e == CRITICS - 1:
            early = add_core((0, 1, 2), 2, me, kept[:3], got[:3])
            early = [early[0], exchange_sides(early[1], 2, 4)]
            after = [early[0]]
        outs = critic_pass(
            e, scale, split, me, x_now, lagged, keep, w_one, w_two, biases, head, head_bias, after, before
        )
        if direct:
            count = len(SENT) if e == CRITICS - 1 else 1
            got.extend(exchange(piece, 1) for piece in outs[:count])
            outs = outs[count:]
        kept.append(outs[0])
        before = outs[1:]
        for flip in flips[e : e + 1] if e < CRITICS - 1 else flips[e:]:
            own = add_actor(own, exchange(own, flip))
    peer = exchange(own, 1)
    *actor_new, small_sums = actor_update(me, factors, own, peer, (actor_w, actor_m, actor_v))

    if direct:
        early = add_half(*early)
        late = add_core((2, 3, 4), 2, me, kept[2:], got[2:], (early[0],))
        early = [early[0], exchange_sides(early[1], 4, 2)]
        late = add_half(late[0], exchange_sides(late[1], 2, 4), (own, early[1]))
        late = [late[0], exchange_sides(late[1], 4, 2)]
        blocks = add_line(me, early, late, n_rows // 2, (small_sums,))
        blocks = [blocks[0]] + [exchange(blocks[k], 8 * k) for k in range(1, len(blocks))]
        others = []
        row = sum_row(blocks)
        row_peer = exchange(row, 1)
    else:
        grads = jnp.stack(kept).reshape(devices, -1, LANES)
        order_of = device ^ jnp.arange(devices)
        blocks = [scatter_sum(jnp.take(grads, order_of, axis=0))]
        head_grad = before[0].reshape(n_quant, PADDED // n_quant, n_rows, HIDDEN_SIZE // n_rows)
        head_grad = head_grad.transpose(2, 0, 1, 3).reshape((devices,) + (PADDED // n_quant, -1))
        head_grad = scatter_sum(jnp.take(head_grad, order_of, axis=0))
        others = [head_grad]
        row = row_peer = all_sum(before[1])
    state = (
        in_w.T, in_m.T, in_v.T, mid_w.T, mid_m.T, mid_v.T, bias_w, bias_m, bias_v, head_w.T, head_m.T, head_v.T,
    )
    new = update(factors, blocks, others, state)
    state = (
        small_w, small_m, small_v,
        heat.reshape(1, 1), heat_m.reshape(1, 1), heat_v.reshape(1, 1),
    )
    objective, *last = small_update(samples, me, factors, row, row_peer, small_sums, state)
    return (
        objective.reshape(()),
        *(a.T for a in new[:6]),
        *new[6:9],
        *(a.T for a in new[9:]),
        *actor_new,
        *last[:3],
        *(a.reshape(-1) for a in last[3:]),
    )


def solution(mesh):
    both, row, none = P(AXES), P("rows"), P()
    column_of, shard = P(None, "quant"), P(None, AXES)
    placed = (
        (both,) * 3 + (row,) * 5 + (none,) * 3 + (column_of,) + (none,) * 3 + (column_of,) + (none,) * 3
        + (shard,) * 9 + (P("rows", "quant"),) * 3 + (none,) * 9
    )
    return jax.shard_map(
        local,
        mesh=mesh,
        in_specs=placed,
        out_specs=(none,) + (shard,) * 9 + (P("rows", "quant"),) * 3 + (none,) * 9,
        check_vma=False,
    )
```

```python
import functools
import math

import jax
import jax.numpy as jnp
import ml_dtypes
import numpy as np
from jax import lax
from jax.experimental import pallas as pl
from jax.experimental.pallas import tpu as pltpu
from jax.sharding import PartitionSpec as P

OBS_DIM = 376
ACT_DIM = 17
HIDDEN_SIZE = 512
ACTOR_HIDDEN = 256
CRITICS = 5
QUANTS = 25
SLOT = 32
PADDED = 128
MERGED_SUPPORTS = 125
KEPT_ATOMS = 115
INPUTS = 393
FEATURES = 2560
SMALL_VEC = 674
LANES = 1024
EXTRA = 128
TILE = 1024
CRITIC_TILE = 512
MiB = 1024 * 1024

DISCOUNT = 0.99
BETA_FIRST = 0.9
BETA_SECOND = 0.999
EPSILON = 1e-08
WEIGHT_DECAY = 0.01
RATE_MATRIX = 0.05
RATE_VECTOR = 0.3
STEP_SIZE_SCALE = 0.5
LOG_TWO = math.log(2.0)
HALF_LOG_CIRCLE = 0.5 * math.log(2.0 * math.pi)
AXES = ("rows", "quant")
BF = jnp.bfloat16
F32 = jnp.float32
WHOLE = pl.BlockSpec(memory_space=pltpu.VMEM)
SCALAR = pl.BlockSpec(memory_space=pltpu.SMEM)
UNREAD = pl.BlockSpec(memory_space=pl.ANY)


def dot_nn(left, right):
    return jnp.dot(left, right, preferred_element_type=F32)


def dot_tn(left, right):
    return lax.dot_general(left, right, (((0,), (0,)), ((), ())), preferred_element_type=F32)


def dot_nt(left, right):
    return lax.dot_general(left, right, (((1,), (1,)), ((), ())), preferred_element_type=F32)


def relu(value):
    return jnp.maximum(value.astype(BF), jnp.zeros((), BF))


def gate(kept, value):
    return jnp.where(kept > 0, value.astype(BF), jnp.zeros((), BF))


def params(limit=32, steps=0):
    semantics = ("arbitrary",) * steps if steps else None
    return pltpu.CompilerParams(vmem_limit_bytes=limit * MiB, dimension_semantics=semantics)


def cost(flops, moved):
    return pl.CostEstimate(flops=int(flops), bytes_accessed=int(moved), transcendentals=0)


def column(row):
    return jnp.transpose(jnp.broadcast_to(row, (8, row.shape[1])))[:, :1]


def fill_inputs(tall, inputs, obs, act):
    rows = obs.shape[1]
    body = OBS_DIM // 16 * 16
    inputs[:body] = obs[:body]
    tall[:8] = obs[body:OBS_DIM].astype(F32)
    tall[8 : 8 + ACT_DIM] = act.astype(F32)
    tall[8 + ACT_DIM : 32] = jnp.zeros((24 - ACT_DIM, rows), F32)
    tall[8 + ACT_DIM : 11 + ACT_DIM] = jnp.ones((3, rows), F32)
    inputs[body : body + 32] = tall[...].astype(BF)
    inputs[body + 32 :] = jnp.zeros((HIDDEN_SIZE - body - 32, rows), BF)


def actor_layers(inputs, draw, actor, small, out_scratch):
    s_one = column(small[:, :ACTOR_HIDDEN])
    s_two = column(small[:, ACTOR_HIDDEN : 2 * ACTOR_HIDDEN])
    s_three = column(small[:, 2 * ACTOR_HIDDEN : 2 * ACTOR_HIDDEN + PADDED])[: 2 * ACT_DIM]
    g_one = relu(dot_tn(actor[:OBS_DIM], inputs) + s_one)
    g_two = relu(dot_tn(actor[OBS_DIM : OBS_DIM + ACTOR_HIDDEN], g_one) + s_two)
    out_scratch[: 2 * ACT_DIM] = dot_nn(actor[OBS_DIM + ACTOR_HIDDEN :], g_two) + s_three
    mean = out_scratch[:ACT_DIM]
    log_std = out_scratch[ACT_DIM : 2 * ACT_DIM]
    scaled = jnp.exp(log_std) * draw
    pre = mean + scaled
    act = jnp.tanh(pre)
    soft = jnp.maximum(-2.0 * pre, 0.0) + jnp.log(1.0 + jnp.exp(-2.0 * jnp.abs(pre)))
    logp = jnp.sum(
        -0.5 * draw * draw - log_std - HALF_LOG_CIRCLE - 2.0 * (LOG_TWO - pre - soft),
        axis=0,
        keepdims=True,
    )
    return g_one, g_two, scaled, act, logp


def heads_kernel(me, own, got_one, got_two, got_three, out, stage):
    quarter = own.shape[0]
    for k, got in enumerate((own, got_one, got_two, got_three)):
        first = pl.multiple_of((me[0] ^ k) * quarter, quarter)
        stage[pl.ds(first, quarter)] = got[...].astype(F32)
    keep = lax.broadcasted_iota(jnp.int32, (SLOT, 1), 0) < QUANTS
    for e in range(CRITICS):
        out[e] = jnp.where(keep, stage[e * QUANTS : e * QUANTS + SLOT], 0.0).astype(BF)


def heads(me, own, got):
    return pl.pallas_call(
        heads_kernel,
        in_specs=[SCALAR] + [WHOLE] * 4,
        out_specs=WHOLE,
        out_shape=jax.ShapeDtypeStruct((CRITICS, SLOT, 2 * HIDDEN_SIZE), BF),
        scratch_shapes=[pltpu.VMEM((136, 2 * HIDDEN_SIZE), F32)],
        compiler_params=params(4),
        cost_estimate=cost(3e10, 1e6),
        name="heads",
    )(me, own, *got)


def fill_biases(small, lag_bias, out, col):
    keep = lax.broadcasted_iota(jnp.int32, (SLOT, 1), 0) < QUANTS
    both = jnp.concatenate([small[:, SMALL_VEC - PADDED :], lag_bias[...], jnp.zeros((6, PADDED), F32)], 0)
    col[:PADDED] = jnp.transpose(both)
    for e in range(CRITICS):
        columns = jnp.where(keep, col[e * QUANTS : e * QUANTS + SLOT], 0.0)
        for net in range(2):
            out[net, e] = jnp.broadcast_to(columns[:, net : net + 1], (SLOT, PADDED))


def fill_first(tall, filled, first, bias):
    body = INPUTS // 16 * 16
    high = bias.astype(BF).astype(F32)
    middle = (bias - high).astype(BF).astype(F32)
    filled[:body] = first[:body]
    tall[: INPUTS - body] = first[body:].astype(F32)
    tall[INPUTS - body : 32] = jnp.zeros((32 - INPUTS + body, HIDDEN_SIZE), F32)
    tall[INPUTS - body : INPUTS - body + 1] = high
    tall[INPUTS - body + 1 : INPUTS - body + 2] = middle
    tall[INPUTS - body + 2 : INPUTS - body + 3] = bias - high - middle
    filled[body : body + 32] = tall[...].astype(BF)
    filled[body + 32 :] = jnp.zeros((HIDDEN_SIZE - body - 32, HIDDEN_SIZE), BF)


def tiles(rows, width=TILE):
    width = min(rows, width)
    return [pl.ds(i * width, width) for i in range(rows // width)]


def critic_lanes(e):
    return pl.ds(pl.multiple_of(e * HIDDEN_SIZE, HIDDEN_SIZE), HIDDEN_SIZE)


def target_kernel(
    index, heat, inputs, logp, payoffs, done, order_in, first, second, bias, head, head_bias, after,
    lagged, keep, filled, tall_w, slots, packed, order, sems,
):
    rows = inputs.shape[1]
    mine = pl.ds(pl.multiple_of(index[0] * rows, PADDED), rows)
    copy = pltpu.make_async_copy(order_in.at[mine], order, sems.at[0])
    copy.start()
    def one_critic(e, carry):
        lanes = critic_lanes(e)
        fill_first(tall_w, filled, first[:, lanes], bias[:1, lanes])
        b_two = column(bias[1:2, lanes])
        w_two = second[:, lanes]
        for part in tiles(rows):
            h_one = relu(dot_tn(filled[...], inputs[:, part]))
            h_two = relu(dot_tn(w_two, h_one) + b_two)
            value = dot_nn(head[e, :, HIDDEN_SIZE:], h_two) + head_bias[1, e, :, :1]
            slots[pl.ds(pl.multiple_of(e * SLOT, SLOT), SLOT), part] = value
        return carry

    lax.fori_loop(0, CRITICS, one_critic, 0, unroll=True)
    for e in range(CRITICS):
        packed[e * QUANTS : e * QUANTS + SLOT] = slots[e * SLOT : (e + 1) * SLOT]
    copy.wait()
    for i in range(rows // PADDED):
        part = pl.ds(i * PADDED, PADDED)
        kept = (order[part] < KEPT_ATOMS).astype(F32)
        kept = jnp.concatenate([kept, jnp.zeros((PADDED, PADDED - MERGED_SUPPORTS), F32)], 1)
        keep[:, part] = jnp.transpose(kept).astype(BF)
    decay = DISCOUNT * (1.0 - done[:, mine].astype(F32))
    temperature = jnp.exp(jnp.full((1, 1), heat[0], F32))
    lagged[...] = payoffs[:, mine] + decay * (packed[:PADDED] - temperature * logp[...])


def target_pass(index, heat, inputs, logp, payoffs, done, order, first, second, bias, head, head_bias, after):
    rows = inputs.shape[1]
    return pl.pallas_call(
        target_kernel,
        in_specs=[SCALAR] * 2 + [WHOLE] * 4 + [pl.BlockSpec(memory_space=pltpu.HBM)] + [WHOLE] * 5 + [UNREAD],
        out_specs=[WHOLE] * 2,
        out_shape=[jax.ShapeDtypeStruct((PADDED, rows), F32), jax.ShapeDtypeStruct((PADDED, rows), BF)],
        scratch_shapes=[
            pltpu.VMEM((HIDDEN_SIZE, HIDDEN_SIZE), BF),
            pltpu.VMEM((32, HIDDEN_SIZE), F32),
            pltpu.VMEM((CRITICS * SLOT, rows), F32),
            pltpu.VMEM((136, rows), F32),
            pltpu.VMEM((rows, MERGED_SUPPORTS), jnp.int32),
            pltpu.SemaphoreType.DMA((1,)),
        ],
        compiler_params=params(24),
        cost_estimate=cost(7e9, 7e6),
        name="target_pass",
    )(index, heat, inputs, logp, payoffs, done, order, first, second, bias, head, head_bias, after)


HALF = 336


def two_terms(value):
    high = value.astype(BF).astype(F32)
    both = jnp.concatenate([high, value - high], 1)
    return jnp.concatenate([both, jnp.zeros((8, 2 * PADDED), F32)], 0).astype(BF)


def pilot_kernel(
    level, share, me, index, heat, obs, next_in, noise, noise_next_in, chosen, actor, small,
    first_in, second_in, bias, head, lag_bias,
    own_out, send_out, x_now, x_target, logp_next, head_bias,
    inputs, filled, tall_x, tall_w, dact, total, out_scratch, grad_out, small_out, next_obs, noise_next, col,
    first, second, sems,
):
    rows = obs.shape[1]
    mine = pl.ds(pl.multiple_of(index[0] * rows, PADDED), rows)
    copies = [
        pltpu.make_async_copy(next_in.at[:, mine], next_obs, sems.at[0]),
        pltpu.make_async_copy(noise_next_in.at[:, mine], noise_next, sems.at[1]),
        pltpu.make_async_copy(first_in, first, sems.at[2]),
        pltpu.make_async_copy(second_in, second, sems.at[3]),
    ]
    for copy in copies:
        copy.start()
    g_one, g_two, scaled, act, logp = actor_layers(obs[...], noise[...], actor, small, out_scratch)
    fill_inputs(tall_x, inputs, obs, act.astype(BF))
    fill_inputs(tall_x, x_now, obs, chosen[...])
    for copy in copies[:2]:
        copy.wait()
    _, _, _, next_act, next_logp = actor_layers(next_obs[...], noise_next[...], actor, small, out_scratch)
    fill_inputs(tall_x, x_target, next_obs, next_act.astype(BF))
    logp_next[...] = next_logp
    fill_biases(small, lag_bias, head_bias, col)
    for copy in copies[2:]:
        copy.wait()

    dact[...] = jnp.zeros(dact.shape, F32)
    total[...] = jnp.zeros(total.shape, F32)

    def one_critic(e, tail):
        lanes = critic_lanes(e)
        fill_first(tall_w, filled, first[:, lanes], bias[:1, lanes])
        b_two = column(bias[1:2, lanes])
        head_sum = jnp.sum(head[e, :, :HIDDEN_SIZE].astype(F32), axis=0, keepdims=True)
        weight = column(head_sum)
        push = column(head_sum * level)
        w_two = second[:, lanes]
        for part in tiles(rows):
            h_one = relu(dot_tn(filled[...], inputs[:, part]))
            h_two = relu(dot_tn(w_two, h_one) + b_two)
            weighted = h_two.astype(F32) * weight
            total[:, part] += jnp.sum(weighted.reshape(-1, 8, weighted.shape[1]), axis=0)
            dz_two = jnp.where(h_two > 0, push.astype(BF), jnp.zeros((), BF))
            dz_one = gate(h_one, dot_nn(w_two, dz_two))
            dact[:, part] += dot_nn(first[OBS_DIM // 16 * 16 :, lanes], dz_one)
        return tail + head_bias[0, e, :, :1]

    tail = lax.fori_loop(0, CRITICS, one_critic, jnp.zeros((SLOT, 1), F32))
    temperature_share = jnp.exp(jnp.full((1, 1), heat[0], F32)) * share
    skip = OBS_DIM % 16
    action_grad = dact[skip : skip + ACT_DIM]
    pre = action_grad * (1.0 - act * act) + 2.0 * temperature_share * act
    out_scratch[:ACT_DIM] = pre
    out_scratch[ACT_DIM : 2 * ACT_DIM] = pre * scaled - temperature_share
    dout = out_scratch[: 2 * ACT_DIM].astype(BF)
    a_two = actor[OBS_DIM : OBS_DIM + ACTOR_HIDDEN]
    a_three = actor[OBS_DIM + ACTOR_HIDDEN :]
    dz_two = gate(g_two, dot_tn(a_three, dout))
    dz_one = gate(g_one, dot_nn(a_two, dz_two))
    grad_out[OBS_DIM + ACTOR_HIDDEN : OBS_DIM + ACTOR_HIDDEN + 2 * ACT_DIM] = dot_nt(dout, g_two)
    grad_out[OBS_DIM + ACTOR_HIDDEN + 2 * ACT_DIM :] = jnp.zeros((6, ACTOR_HIDDEN), F32)
    grad_out[OBS_DIM : OBS_DIM + ACTOR_HIDDEN] = dot_nt(g_one, dz_two)
    grad_out[:OBS_DIM] = dot_nt(obs[...], dz_one)
    ones = jnp.ones((16, rows), BF)
    small_out[...] = jnp.zeros(small_out.shape, F32)
    sum_one = dot_nt(ones, dz_one)[:1]
    sum_two = dot_nt(ones, dz_two)[:1]
    small_out[0:1] = sum_one[:, :PADDED]
    small_out[1:2] = sum_one[:, PADDED:]
    small_out[2:3] = sum_two[:, :PADDED]
    small_out[3:4] = sum_two[:, PADDED:]
    small_out[4:5, : 2 * ACT_DIM] = dot_nt(ones, dout)[:1]
    pilot_total = jnp.sum(total[...]) + rows * jnp.sum(tail)
    small_out[5:6] = jnp.broadcast_to(pilot_total, (1, PADDED))
    small_out[6:7] = jnp.broadcast_to(jnp.sum(logp), (1, PADDED))
    packed = two_terms(small_out[...])
    side = me[0] & 1
    for out, which in ((own_out, side), (send_out, 1 - side)):
        out[:HALF] = grad_out[pl.ds(pl.multiple_of(which * HALF, 16), HALF)].astype(BF)
        out[HALF:] = packed


def pilot_pass(
    level, share, me, index, heat, obs, next_obs, noise, noise_next, chosen, actor, small,
    first, second, bias, head, lag_bias,
):
    rows = obs.shape[1]
    far = pl.BlockSpec(memory_space=pltpu.HBM)
    filled = jax.ShapeDtypeStruct((HIDDEN_SIZE, rows), BF)
    return pl.pallas_call(
        functools.partial(pilot_kernel, level, share),
        in_specs=[SCALAR] * 3 + [WHOLE, far, WHOLE, far] + [WHOLE] * 3 + [far] * 2 + [WHOLE] * 3,
        out_specs=[WHOLE] * 6,
        out_shape=[jax.ShapeDtypeStruct((HALF + 16, ACTOR_HIDDEN), BF)] * 2
        + [filled, filled, jax.ShapeDtypeStruct((1, rows), F32)]
        + [jax.ShapeDtypeStruct((2, CRITICS, SLOT, PADDED), F32)],
        scratch_shapes=[
            pltpu.VMEM((HIDDEN_SIZE, rows), BF),
            pltpu.VMEM((HIDDEN_SIZE, HIDDEN_SIZE), BF),
            pltpu.VMEM((32, rows), F32),
            pltpu.VMEM((32, HIDDEN_SIZE), F32),
            pltpu.VMEM((INPUTS - OBS_DIM // 16 * 16, rows), F32),
            pltpu.VMEM((8, rows), F32),
            pltpu.VMEM((40, rows), F32),
            pltpu.VMEM((2 * HALF, ACTOR_HIDDEN), F32),
            pltpu.VMEM((8, PADDED), F32),
            pltpu.VMEM((OBS_DIM, rows), BF),
            pltpu.VMEM((ACT_DIM, rows), F32),
            pltpu.VMEM((136, 8), F32),
            pltpu.VMEM(first.shape, BF),
            pltpu.VMEM(second.shape, BF),
            pltpu.SemaphoreType.DMA((4,)),
        ],
        compiler_params=params(48),
        cost_estimate=cost(14e9, 9e6),
        name="pilot_pass",
    )(me, index, heat, obs, next_obs, noise, noise_next, chosen, actor, small, first, second, bias, head, lag_bias)


def pair_terms(q_ref, lagged, keep, parts, rows):
    def group(i, carry):
        part = pl.ds(pl.multiple_of(i * PADDED, PADDED), PADDED)
        q = q_ref[:, part]
        shift = jnp.sum(q, axis=0, keepdims=True) * (1.0 / QUANTS)
        y = (lagged[:, part] - shift).astype(BF).reshape(8, 16, PADDED)
        upper = keep[:, part].reshape(8, 16, PADDED)
        lower = -upper
        q_ref[:, part] = q - shift
        for j in range(QUANTS):
            level = jnp.broadcast_to(q_ref[j : j + 1, part], (16, PADDED)).astype(BF)
            d = y - level[None]
            c = jnp.minimum(jnp.maximum(d, lower), upper)
            half = c * jnp.asarray(0.5, BF)
            g = half + jnp.abs(c) * jnp.asarray((j + 0.5) / QUANTS - 0.5, BF)
            h = g * (d - half)
            g = g[:4] + g[4:]
            g = g[:2] + g[2:]
            parts[j * 16 : j * 16 + 16, part] = g[0] + g[1]
            h = h[:4] + h[4:]
            h = h[:2] + h[2:]
            parts[(QUANTS + j) * 16 : (QUANTS + j) * 16 + 16, part] = h[0] + h[1]
        return carry

    lax.fori_loop(0, rows // PADDED, group, 0, unroll=2)
    shape = (48, 2 * QUANTS * 16)
    row = lax.broadcasted_iota(jnp.int32, shape, 0)
    owner = jnp.minimum(lax.broadcasted_iota(jnp.int32, shape, 1) // 16, SLOT)
    owner = jnp.where(owner >= QUANTS, SLOT, owner)
    return dot_nn((row == owner).astype(F32).astype(BF), parts[...])


PARITY = 18


def granules(e):
    mine = range(32 * e, 32 * e + 32)
    return [[g for g in mine if g // CRITICS % 2 == parity] for parity in range(2)]


def granule_places(chunk):
    places = np.zeros(CRITICS * 32, np.int32)
    for i, e in enumerate(chunk):
        for way in granules(e):
            for t, g in enumerate(way):
                places[g] = i * PARITY + t
    return places


SENT = (6, 6, 6, 4)


def store_piece(outs, t, value):
    for out in outs:
        if t < out.shape[0]:
            out[t] = value
            return
        t -= out.shape[0]


def critic_kernel(
    e, waits, rows_scale, split, me, inputs, lagged, keep, first, second, bias, head, head_bias, *refs,
):
    last = e == CRITICS - 1
    refs = refs[waits:]
    if e:
        before, refs = refs[:3], refs[3:]
    outs, scratch = refs[:-9], refs[-9:]
    filled, tall_w, h_one, h_two, q, parts, grads, packed, extra = scratch
    rows = inputs.shape[1]
    lanes = slice(e * HIDDEN_SIZE, (e + 1) * HIDDEN_SIZE)
    second = second.at[:, lanes]
    head = head.at[e : e + 1, :, :HIDDEN_SIZE]
    head_bias = head_bias.at[:1, e : e + 1]
    fill_first(tall_w, filled, first[:, lanes], bias[:1, lanes])
    b_two = column(bias[1:2, lanes])
    for part in tiles(rows, CRITIC_TILE):
        h_one[:, part] = relu(dot_tn(filled[...], inputs[:, part]))
    for part in tiles(rows, CRITIC_TILE):
        h_two[:, part] = relu(dot_tn(second[...], h_one[:, part]) + b_two)
    for part in tiles(rows, CRITIC_TILE):
        q[:, part] = dot_nn(head[0], h_two[:, part]) + head_bias[0, 0, :, :1]
    terms = pair_terms(q, lagged, keep, parts, rows)
    low = (terms[:SLOT] * -rows_scale).astype(BF)
    loss = terms[SLOT : SLOT + 1]
    head_grad = dot_nt(low, h_two[...])
    count = jnp.ones((8, rows), BF)
    bias_grad = dot_nt(count, low)[:1]
    sums = jnp.zeros((HIDDEN_SIZE, PADDED), F32)
    for part in tiles(rows, CRITIC_TILE):
        two = h_two[:, part]
        dz_two = gate(two, dot_tn(head[0], low[:, part.start : part.start + part.size]))
        lanes_of = [dz_two[:, i * PADDED : (i + 1) * PADDED] for i in range(part.size // PADDED)]
        sums = sums + tree(lanes_of).astype(F32)
        h_two[:, part] = dz_two
    second_grad = dot_nt(h_two[...], h_one[...])
    for part in tiles(rows, CRITIC_TILE):
        one = h_one[:, part]
        h_one[:, part] = gate(one, dot_nn(second[...], h_two[:, part]))
    grads[:, :, :HIDDEN_SIZE] = second_grad.astype(BF).reshape(-1, 16, HIDDEN_SIZE)
    first_grad = dot_nt(h_one[...], inputs[...])
    grads[:, :, HIDDEN_SIZE : LANES - PADDED] = (
        first_grad[:, : HIDDEN_SIZE - PADDED].astype(BF).reshape(-1, 16, HIDDEN_SIZE - PADDED)
    )
    lane = lax.broadcasted_iota(jnp.int32, (HIDDEN_SIZE, PADDED), 1)
    tail = jnp.where(
        lane == INPUTS + 1 - HIDDEN_SIZE + PADDED,
        jnp.sum(sums, axis=1, keepdims=True),
        first_grad[:, HIDDEN_SIZE - PADDED :],
    )
    grads[:, :, LANES - PADDED : LANES] = tail.astype(BF).reshape(-1, 16, PADDED)
    direct = split[0] > 0
    rest = outs[1 + (len(SENT) if last else 1) :] if direct else outs[1:]
    if not last:
        all_heads, all_bias, all_loss = rest
        if e:
            all_heads[...] = before[0][...]
            all_bias[...] = before[1][...]
            all_loss[...] = before[2][...] + loss
        else:
            all_heads[...] = jnp.zeros(all_heads.shape, F32)
            all_bias[...] = jnp.zeros(all_bias.shape, F32)
            all_loss[...] = loss
        all_heads[e * SLOT : (e + 1) * SLOT] = head_grad
        all_bias[e : e + 1, :SLOT] = bias_grad
    else:
        n_rows, n_quant = split
        for i in range(CRITICS):
            packed[i * QUANTS : i * QUANTS + SLOT] = (
                before[0][i * SLOT : (i + 1) * SLOT] if i < e else head_grad
            )
        bias_row = jnp.zeros((1, PADDED), F32)
        lane = lax.broadcasted_iota(jnp.int32, (1, PADDED), 1)
        spare = jnp.zeros((1, PADDED - SLOT), F32)
        for i in range(CRITICS):
            piece = before[1][i : i + 1] if i < e else jnp.concatenate([bias_grad, spare], 1)
            piece = pltpu.roll(jnp.broadcast_to(piece, (8, PADDED)), i * QUANTS, 1)[:1]
            inside = (lane >= i * QUANTS) & (lane < (i + 1) * QUANTS)
            bias_row = jnp.where(inside, piece, bias_row)
        value = jnp.sum(before[2][...] + loss, axis=1, keepdims=True) * rows_scale
        value = jnp.broadcast_to(value, (1, PADDED))
        if direct:
            width = HIDDEN_SIZE // n_rows
            high = PADDED // n_quant
            lane = lax.broadcasted_iota(jnp.int32, (16, PADDED), 1)
            halves = [bias_row, pltpu.roll(jnp.broadcast_to(bias_row, (8, PADDED)), 64, 1)[:1], value]
            common = jnp.concatenate(halves + [jnp.zeros((13, PADDED), F32)], 0)
            for j in range(8):
                y, c = j // 4, j % 4
                for z in range(n_rows // 2):
                    r = 2 * z + y
                    block = packed[c * high : (c + 1) * high, r // 2 * PADDED : (r // 2 + 1) * PADDED]
                    if r % 2 == 0:
                        block = pltpu.roll(block, width, 1)
                    base = 2 * z * PADDED
                    extra[j, :, base : base + PADDED] = jnp.where(lane < 64, common, block[:16]).astype(BF)
                    extra[j, :, base + PADDED : base + 2 * PADDED] = block[16:].astype(BF)
        else:
            rest[0][...] = packed[:PADDED]
            rest[1][...] = jnp.concatenate([bias_row, value, jnp.zeros((6, PADDED), F32)], 0)
    if not direct:
        outs[0][...] = grads[...]
        return
    sent, kept = outs[: len(SENT) if last else 1], outs[len(SENT) if last else 1]
    side = me[0] & 1
    ways = granules(e)
    for t in range(max(map(len, ways))):
        pair = [way[min(t, len(way) - 1)] - e * 32 for way in ways]
        kept[t] = grads[jnp.where(side == 0, pair[0], pair[1])]
        store_piece(sent, t, grads[jnp.where(side == 0, pair[1], pair[0])])
    if last:
        for i in range(4):
            kept[PARITY + i] = extra[2 * i + side]
            store_piece(sent, PARITY + i, extra[2 * i + 1 - side])


def critic_pass(e, rows_scale, split, me, inputs, lagged, keep, first, second, bias, head, head_bias, after, before):
    rows = inputs.shape[1]
    last = e == CRITICS - 1
    if split[0]:
        block = lambda count: jax.ShapeDtypeStruct((count, 16, LANES), BF)
        sent = SENT if last else (PARITY,)
        out_shape = [block(count) for count in sent] + [block(sum(sent))]
    else:
        out_shape = [jax.ShapeDtypeStruct((HIDDEN_SIZE // 16, 16, LANES), BF)]
    if not last:
        out_shape += [
            jax.ShapeDtypeStruct((CRITICS * SLOT, HIDDEN_SIZE), F32),
            jax.ShapeDtypeStruct((8, PADDED), F32),
            jax.ShapeDtypeStruct((1, rows), F32),
        ]
    elif not split[0]:
        out_shape += [
            jax.ShapeDtypeStruct((PADDED, HIDDEN_SIZE), F32),
            jax.ShapeDtypeStruct((8, PADDED), F32),
        ]
    return pl.pallas_call(
        functools.partial(critic_kernel, e, len(after), rows_scale, split),
        in_specs=[SCALAR] + [WHOLE] * 8 + [UNREAD] * len(after) + [WHOLE] * len(before),
        out_specs=[WHOLE] * len(out_shape),
        out_shape=out_shape,
        scratch_shapes=[
            pltpu.VMEM((HIDDEN_SIZE, HIDDEN_SIZE), BF),
            pltpu.VMEM((32, HIDDEN_SIZE), F32),
            pltpu.VMEM((HIDDEN_SIZE, rows), BF),
            pltpu.VMEM((HIDDEN_SIZE, rows), BF),
            pltpu.VMEM((SLOT, rows), F32),
            pltpu.VMEM((2 * QUANTS * 16, rows), BF),
            pltpu.VMEM((HIDDEN_SIZE // 16, 16, LANES), BF),
            pltpu.VMEM((136, HIDDEN_SIZE), F32),
            pltpu.VMEM((8, 16, LANES), BF),
        ],
        compiler_params=params(24),
        cost_estimate=cost(7e9, 4e6),
        name="critic_pass",
    )(me, inputs, lagged, keep, first, second, bias, head, head_bias, *after, *before)


def add_kernel(a, b, out):
    out[:HALF] = (a[:HALF].astype(F32) + b[:HALF].astype(F32)).astype(BF)
    pair = [r[HALF:].astype(F32) for r in (a, b)]
    pair = [p[:8, :PADDED] + p[:8, PADDED:] for p in pair]
    out[HALF:] = two_terms(pair[0] + pair[1])


def add_actor(a, b):
    return pl.pallas_call(
        add_kernel,
        in_specs=[WHOLE, WHOLE],
        out_specs=WHOLE,
        out_shape=jax.ShapeDtypeStruct(a.shape, BF),
        compiler_params=params(),
        cost_estimate=cost(1e5, 6e5),
        name="add_actor",
    )(a, b)


def core_kernel(chunk, depth, waits, me, places, *refs):
    count = len(chunk)
    refs = refs[waits:]
    kept, got, outs, sums = refs[:count], refs[count:-3], refs[-3:-1], refs[-1]
    size = count * PARITY
    first = 0
    for piece in got:
        i, inside = min(first // PARITY, count - 1), first - min(first // PARITY, count - 1) * PARITY
        own = kept[i][inside : inside + piece.shape[0]]
        sums[first : first + piece.shape[0]] = own + piece[...]
        first += piece.shape[0]
    z_first = chunk[-1] // 3 * depth
    side = me[0] & 1
    for k in range(4):
        flip = (0, 4 - 2 * side, 2 + 2 * side, 6)[k]
        j = (me[0] & 7) ^ flip
        out = outs[k // 2]
        for z in range(depth):
            owner = (z_first + z) * 8 + j
            for i in range(CRITICS):
                out[k % 2, z * CRITICS + i] = sums[places[owner * CRITICS + i]]
        if chunk[-1] == CRITICS - 1:
            out[k % 2, depth * CRITICS] = sums[size + j // 2]


def add_core(chunk, depth, me, kept, got, after=()):
    tail = kept[-1].shape[0] - PARITY
    count = depth * CRITICS + (1 if tail else 0)
    return pl.pallas_call(
        functools.partial(core_kernel, chunk, depth, len(after)),
        in_specs=[SCALAR, SCALAR] + [UNREAD] * len(after) + [WHOLE] * (len(kept) + len(got)),
        out_specs=[WHOLE] * 2,
        out_shape=[jax.ShapeDtypeStruct((2, count, 16, LANES), BF)] * 2,
        scratch_shapes=[pltpu.VMEM((len(kept) * PARITY + tail, 16, LANES), BF)],
        compiler_params=params(),
        cost_estimate=cost(1e6, 8e6),
        name="add_core",
    )(me, jnp.asarray(granule_places(chunk)), *after, *kept, *got)


def tree(values):
    while len(values) > 1:
        values = [a + b for a, b in zip(values[::2], values[1::2])]
    return values[0]


def half_kernel(kept, got, own, send):
    for k, out in enumerate((own, send)):
        out[...] = kept[k] + got[k]


def add_half(kept, got, after=()):
    waits = len(after)
    return pl.pallas_call(
        lambda *refs: half_kernel(*refs[waits:]),
        in_specs=[UNREAD] * waits + [WHOLE] * 2,
        out_specs=[WHOLE] * 2,
        out_shape=[jax.ShapeDtypeStruct(kept.shape[1:], BF)] * 2,
        compiler_params=params(8),
        cost_estimate=cost(1e5, 1e5),
        name="add_half",
    )(*after, kept, got)


def line_kernel(me, early, early_got, late, late_got, *refs):
    outs, sums = refs[:-1], refs[-1]
    count = early.shape[0]
    sums[:count] = early[...] + early_got[...]
    total = late[...].astype(F32) + late_got[...].astype(F32)
    sums[count:] = total[:count].astype(BF)
    extra = total[count]
    lane = lax.broadcasted_iota(jnp.int32, (16, PADDED), 1)
    for z in range(len(outs)):
        first = extra[:, 2 * z * PADDED : (2 * z + 1) * PADDED]
        second = extra[:, (2 * z + 1) * PADDED : (2 * z + 2) * PADDED]
        for i, value in enumerate((first, second, pltpu.roll(first, 64, 1))):
            old = sums[z * CRITICS + i, :, LANES - PADDED :].astype(F32)
            sums[z * CRITICS + i, :, LANES - PADDED :] = jnp.where(lane < 64, old, value).astype(BF)
    for k, out in enumerate(outs):
        first = ((me[0] // 8) ^ k) * CRITICS
        for i in range(CRITICS):
            out[i] = sums[first + i]


def add_line(me, early, late, depth, after=()):
    waits = len(after)
    return pl.pallas_call(
        lambda *refs: line_kernel(*refs[waits:]),
        in_specs=[UNREAD] * waits + [SCALAR] + [WHOLE] * 4,
        out_specs=[WHOLE] * depth,
        out_shape=[jax.ShapeDtypeStruct((CRITICS, 16, LANES), BF)] * depth,
        scratch_shapes=[pltpu.VMEM((2 * early[0].shape[0], 16, LANES), BF)],
        compiler_params=params(),
        cost_estimate=cost(1e6, 6e6),
        name="add_line",
    )(*after, me, *early, *late)


def adamw(weight, first, second, grad, rate, factors, outs):
    first_new = BETA_FIRST * first[...] + (1.0 - BETA_FIRST) * grad
    second_new = BETA_SECOND * second[...] + (1.0 - BETA_SECOND) * grad * grad
    old = weight[...]
    step = (first_new * factors[0]) / (jnp.sqrt(second_new * factors[1]) + EPSILON)
    outs[0][...] = old - rate * (step + WEIGHT_DECAY * old)
    outs[1][...] = first_new
    outs[2][...] = second_new


def row_kernel(*refs):
    total = tree([r[2, :, LANES - PADDED :].astype(F32) for r in refs[:-1]])
    total = pltpu.roll(total, 64, 1)
    row = jnp.concatenate([total[:1, :64], total[1:2, :64]], 1)
    refs[-1][...] = jnp.concatenate([row, jnp.broadcast_to(total[2:3, :1], (7, PADDED))], 0)


def sum_row(blocks):
    return pl.pallas_call(
        row_kernel,
        in_specs=[WHOLE] * len(blocks),
        out_specs=WHOLE,
        out_shape=jax.ShapeDtypeStruct((8, PADDED), F32),
        compiler_params=params(8),
        cost_estimate=cost(1e5, 1e5),
        name="sum_row",
    )(*blocks)


def update_kernel(count, direct, factors, *refs):
    blocks, refs = refs[:count], refs[count:]
    if direct:
        total = tree([b[...].astype(F32) for b in blocks]).reshape(-1, LANES)
        head_grad = pltpu.roll(total[:SLOT, LANES - PADDED :], 64, 1)[:, :64]
    else:
        total = blocks[0][...]
        head_grad, refs = refs[0][...], refs[1:]
    state, outs = refs[:12], refs[12:]
    adamw(*state[0:3], total[:, HIDDEN_SIZE : HIDDEN_SIZE + INPUTS], RATE_MATRIX, factors, outs[0:3])
    adamw(*state[3:6], total[:, :HIDDEN_SIZE], RATE_MATRIX, factors, outs[3:6])
    edge = INPUTS - HIDDEN_SIZE + PADDED
    bias_grad = jnp.transpose(total[:, LANES - PADDED :])[edge : edge + 2]
    adamw(*state[6:9], bias_grad, RATE_VECTOR, factors, outs[6:9])
    adamw(*state[9:12], head_grad, RATE_MATRIX, factors, outs[9:12])


def update(factors, blocks, others, state):
    shapes = [jax.ShapeDtypeStruct(a.shape, F32) for a in state]
    count = len(blocks)
    return pl.pallas_call(
        functools.partial(update_kernel, count, not others),
        in_specs=[SCALAR] + [WHOLE] * (count + len(others) + len(state)),
        out_specs=[WHOLE] * len(shapes),
        out_shape=shapes,
        compiler_params=params(),
        cost_estimate=cost(2e6, 6e6),
        name="update",
    )(factors, *blocks, *others, *state)


def actor_update_kernel(me, factors, own, peer, *refs):
    state, outs, grad = refs[:3], refs[3:7], refs[7]
    side = me[0] & 1
    grad[pl.ds(pl.multiple_of(side * HALF, 16), HALF)] = own[:HALF].astype(F32)
    grad[pl.ds(pl.multiple_of((1 - side) * HALF, 16), HALF)] = peer[:HALF].astype(F32)
    adamw(*state, grad[: state[0].shape[0]], RATE_MATRIX, factors, outs[:3])
    pair = own[HALF:].astype(F32)
    outs[3][...] = pair[:8, :PADDED] + pair[:8, PADDED:]


def actor_update(me, factors, own, peer, state):
    shapes = [jax.ShapeDtypeStruct(a.shape, F32) for a in state] + [jax.ShapeDtypeStruct((8, PADDED), F32)]
    return pl.pallas_call(
        actor_update_kernel,
        in_specs=[SCALAR, SCALAR] + [WHOLE] * (2 + len(state)),
        out_specs=[WHOLE] * len(shapes),
        out_shape=shapes,
        scratch_shapes=[pltpu.VMEM((2 * HALF, ACTOR_HIDDEN), F32)],
        compiler_params=params(),
        cost_estimate=cost(2e6, 5e6),
        name="actor_update",
    )(me, factors, own, peer, *state)


def small_update_kernel(samples, me, factors, row_own, row_peer, small_sums, *refs):
    state, outs, vector = refs[:6], refs[6:13], refs[13]
    row = jnp.where((me[0] & 1) == 0, row_own[...], row_peer[...])
    for i in range(4):
        vector[i * PADDED : (i + 1) * PADDED] = small_sums[i]
    wide = jnp.concatenate([row, jnp.zeros((8, PADDED), F32)], 1)
    wide = pltpu.roll(wide, 2 * ACT_DIM, 1)
    wide = wide + jnp.concatenate([small_sums[4:5], jnp.zeros((1, PADDED), F32)], 1)
    vector[4 * PADDED :] = wide[0]
    adamw(*state[:3], vector[:SMALL_VEC], RATE_VECTOR, factors, outs[1:4])
    heat = state[3][...]
    logp_sum = small_sums[6:7, :1]
    shortfall = (ACT_DIM * samples - logp_sum) / samples
    adamw(*state[3:6], shortfall, STEP_SIZE_SCALE, factors, outs[4:7])
    actor_loss = (jnp.exp(heat) * logp_sum - small_sums[5:6, :1] / MERGED_SUPPORTS) / samples
    outs[0][...] = row[1:2, :1] + actor_loss + heat * shortfall


def small_update(samples, me, factors, row, row_peer, small_sums, state):
    shapes = [jax.ShapeDtypeStruct((1, 1), F32)] + [jax.ShapeDtypeStruct(a.shape, F32) for a in state]
    return pl.pallas_call(
        functools.partial(small_update_kernel, samples),
        in_specs=[SCALAR, SCALAR] + [WHOLE] * (3 + len(state)),
        out_specs=[WHOLE] * len(shapes),
        out_shape=shapes,
        scratch_shapes=[pltpu.VMEM((6 * PADDED,), F32)],
        compiler_params=params(8),
        cost_estimate=cost(1e6, 1e5),
        name="small_update",
    )(me, factors, row, row_peer, small_sums, *state)


def exchange(value, flip):
    count = lax.axis_size("rows") * lax.axis_size("quant")
    return lax.ppermute(value, AXES, [(i, i ^ flip) for i in range(count)])


def exchange_sides(value, even, odd):
    count = lax.axis_size("rows") * lax.axis_size("quant")
    return lax.ppermute(value, AXES, [(i, i ^ (odd if i % 2 else even)) for i in range(count)])


def all_sum(value):
    total = lax.axis_size("rows") * lax.axis_size("quant")
    flip = 1
    while flip < total:
        value = value + exchange(value, flip)
        flip *= 2
    return value


def scatter_sum(pieces):
    total = pieces.shape[0]
    flip = total // 2
    while flip:
        low = pieces.astype(BF)
        pieces = low[:flip].astype(F32) + exchange(low[flip:], flip).astype(F32)
        flip //= 2
    return pieces[0]


def local(
    obs, chosen, noise_now, next_obs, noise_next, payoffs, done, order,
    w_one, w_two, biases, head_part, t_one, t_two, t_biases, t_head_part, t_head_bias,
    actor, counter,
    in_w, in_m, in_v, mid_w, mid_m, mid_v, bias_w, bias_m, bias_v, head_w, head_m, head_v,
    actor_w, actor_m, actor_v, small_w, small_m, small_v, heat, heat_m, heat_v,
):
    n_rows, n_quant = lax.axis_size("rows"), lax.axis_size("quant")
    devices = n_rows * n_quant
    rows = obs.shape[0]
    samples = rows * devices
    index = lax.axis_index("quant").reshape(1)
    device = lax.axis_index("rows") * n_quant + lax.axis_index("quant")
    me = device.reshape(1)
    direct = n_rows == 8 and n_quant == 4
    small_row = small_w.reshape(1, -1)
    tally = counter.astype(F32)
    factors = jnp.concatenate(
        [1.0 / (1.0 - jnp.power(BETA_FIRST, tally)), 1.0 / (1.0 - jnp.power(BETA_SECOND, tally))]
    )

    own_head = jnp.concatenate([head_part.T, t_head_part.T], 1)
    got = [
        lax.ppermute(own_head, "quant", [(i, i ^ k) for i in range(n_quant)]) for k in (1, 2, 3)
    ]
    head = heads(index, own_head, got)

    level = float(np.asarray(-1.0 / (MERGED_SUPPORTS * samples), ml_dtypes.bfloat16))
    own, send, x_now, x_target, logp, head_bias = pilot_pass(
        level, 1.0 / samples, me, index, heat, obs.T, next_obs.T, noise_now.T, noise_next.T, chosen.T,
        actor, small_row, w_one, w_two, biases, head, t_head_bias.reshape(1, -1),
    )
    lagged, keep = target_pass(
        index, heat, x_target, logp, payoffs.reshape(1, -1), done.reshape(1, -1), order,
        t_one, t_two, t_biases, head, head_bias, own,
    )
    own = add_actor(own, exchange(send, 1))
    flips = [1 << i for i in range(1, devices.bit_length() - 1)]
    scale = 1.0 / (samples * MERGED_SUPPORTS * KEPT_ATOMS)
    split = (n_rows, n_quant) if direct else (0, 0)
    kept, got, before, early = [], [], (), None
    for e in range(CRITICS):
        after = [own] if e < 4 else []
        if direct and e == CRITICS - 1:
            early = add_core((0, 1, 2), 2, me, kept[:3], got[:3])
            early = [early[0], exchange_sides(early[1], 2, 4)]
            after = [early[0]]
        outs = critic_pass(
            e, scale, split, me, x_now, lagged, keep, w_one, w_two, biases, head, head_bias, after, before
        )
        if direct:
            count = len(SENT) if e == CRITICS - 1 else 1
            got.extend(exchange(piece, 1) for piece in outs[:count])
            outs = outs[count:]
        kept.append(outs[0])
        before = outs[1:]
        for flip in flips[e : e + 1] if e < CRITICS - 1 else flips[e:]:
            own = add_actor(own, exchange(own, flip))
    peer = exchange(own, 1)
    *actor_new, small_sums = actor_update(me, factors, own, peer, (actor_w, actor_m, actor_v))

    if direct:
        early = add_half(*early)
        late = add_core((2, 3, 4), 2, me, kept[2:], got[2:], (early[0],))
        early = [early[0], exchange_sides(early[1], 4, 2)]
        late = add_half(late[0], exchange_sides(late[1], 2, 4), (own, early[1]))
        late = [late[0], exchange_sides(late[1], 4, 2)]
        blocks = add_line(me, early, late, n_rows // 2, (small_sums,))
        blocks = [blocks[0]] + [exchange(blocks[k], 8 * k) for k in range(1, len(blocks))]
        others = []
        row = sum_row(blocks)
        row_peer = exchange(row, 1)
    else:
        grads = jnp.stack(kept).reshape(devices, -1, LANES)
        order_of = device ^ jnp.arange(devices)
        blocks = [scatter_sum(jnp.take(grads, order_of, axis=0))]
        head_grad = before[0].reshape(n_quant, PADDED // n_quant, n_rows, HIDDEN_SIZE // n_rows)
        head_grad = head_grad.transpose(2, 0, 1, 3).reshape((devices,) + (PADDED // n_quant, -1))
        head_grad = scatter_sum(jnp.take(head_grad, order_of, axis=0))
        others = [head_grad]
        row = row_peer = all_sum(before[1])
    state = (
        in_w.T, in_m.T, in_v.T, mid_w.T, mid_m.T, mid_v.T, bias_w, bias_m, bias_v, head_w.T, head_m.T, head_v.T,
    )
    new = update(factors, blocks, others, state)
    state = (
        small_w, small_m, small_v,
        heat.reshape(1, 1), heat_m.reshape(1, 1), heat_v.reshape(1, 1),
    )
    objective, *last = small_update(samples, me, factors, row, row_peer, small_sums, state)
    return (
        objective.reshape(()),
        *(a.T for a in new[:6]),
        *new[6:9],
        *(a.T for a in new[9:]),
        *actor_new,
        *last[:3],
        *(a.reshape(-1) for a in last[3:]),
    )


def solution(mesh):
    both, row, none = P(AXES), P("rows"), P()
    column_of, shard = P(None, "quant"), P(None, AXES)
    placed = (
        (both,) * 3 + (row,) * 5 + (none,) * 3 + (column_of,) + (none,) * 3 + (column_of,) + (none,) * 3
        + (shard,) * 9 + (P("rows", "quant"),) * 3 + (none,) * 9
    )
    return jax.shard_map(
        local,
        mesh=mesh,
        in_specs=placed,
        out_specs=(none,) + (shard,) * 9 + (P("rows", "quant"),) * 3 + (none,) * 9,
        check_vma=False,
    )
```

```python
import functools
import math

import jax
import jax.numpy as jnp
import ml_dtypes
import numpy as np
from jax import lax
from jax.experimental import pallas as pl
from jax.experimental.pallas import tpu as pltpu
from jax.sharding import PartitionSpec as P

OBS_DIM = 376
ACT_DIM = 17
HIDDEN_SIZE = 512
ACTOR_HIDDEN = 256
CRITICS = 5
QUANTS = 25
SLOT = 32
PADDED = 128
MERGED_SUPPORTS = 125
KEPT_ATOMS = 115
INPUTS = 393
FEATURES = 2560
SMALL_VEC = 674
LANES = 1024
EXTRA = 128
TILE = 1024
CRITIC_TILE = 512
MiB = 1024 * 1024

DISCOUNT = 0.99
BETA_FIRST = 0.9
BETA_SECOND = 0.999
EPSILON = 1e-08
WEIGHT_DECAY = 0.01
RATE_MATRIX = 0.05
RATE_VECTOR = 0.3
STEP_SIZE_SCALE = 0.5
LOG_TWO = math.log(2.0)
HALF_LOG_CIRCLE = 0.5 * math.log(2.0 * math.pi)
AXES = ("rows", "quant")
BF = jnp.bfloat16
F32 = jnp.float32
WHOLE = pl.BlockSpec(memory_space=pltpu.VMEM)
SCALAR = pl.BlockSpec(memory_space=pltpu.SMEM)
UNREAD = pl.BlockSpec(memory_space=pl.ANY)


def dot_nn(left, right):
    return jnp.dot(left, right, preferred_element_type=F32)


def dot_tn(left, right):
    return lax.dot_general(left, right, (((0,), (0,)), ((), ())), preferred_element_type=F32)


def dot_nt(left, right):
    return lax.dot_general(left, right, (((1,), (1,)), ((), ())), preferred_element_type=F32)


def relu(value):
    return jnp.maximum(value.astype(BF), jnp.zeros((), BF))


def gate(kept, value):
    return jnp.where(kept > 0, value.astype(BF), jnp.zeros((), BF))


def params(limit=32, steps=0):
    semantics = ("arbitrary",) * steps if steps else None
    return pltpu.CompilerParams(vmem_limit_bytes=limit * MiB, dimension_semantics=semantics)


def cost(flops, moved):
    return pl.CostEstimate(flops=int(flops), bytes_accessed=int(moved), transcendentals=0)


def column(row):
    return jnp.transpose(jnp.broadcast_to(row, (8, row.shape[1])))[:, :1]


def fill_inputs(tall, inputs, obs, act):
    rows = obs.shape[1]
    body = OBS_DIM // 16 * 16
    inputs[:body] = obs[:body]
    tall[:8] = obs[body:OBS_DIM].astype(F32)
    tall[8 : 8 + ACT_DIM] = act.astype(F32)
    tall[8 + ACT_DIM : 32] = jnp.zeros((24 - ACT_DIM, rows), F32)
    tall[8 + ACT_DIM : 11 + ACT_DIM] = jnp.ones((3, rows), F32)
    inputs[body : body + 32] = tall[...].astype(BF)
    inputs[body + 32 :] = jnp.zeros((HIDDEN_SIZE - body - 32, rows), BF)


def actor_layers(inputs, draw, actor, small, out_scratch):
    s_one = column(small[:, :ACTOR_HIDDEN])
    s_two = column(small[:, ACTOR_HIDDEN : 2 * ACTOR_HIDDEN])
    s_three = column(small[:, 2 * ACTOR_HIDDEN : 2 * ACTOR_HIDDEN + PADDED])[: 2 * ACT_DIM]
    g_one = relu(dot_tn(actor[:OBS_DIM], inputs) + s_one)
    g_two = relu(dot_tn(actor[OBS_DIM : OBS_DIM + ACTOR_HIDDEN], g_one) + s_two)
    out_scratch[: 2 * ACT_DIM] = dot_nn(actor[OBS_DIM + ACTOR_HIDDEN :], g_two) + s_three
    mean = out_scratch[:ACT_DIM]
    log_std = out_scratch[ACT_DIM : 2 * ACT_DIM]
    scaled = jnp.exp(log_std) * draw
    pre = mean + scaled
    act = jnp.tanh(pre)
    soft = jnp.maximum(-2.0 * pre, 0.0) + jnp.log(1.0 + jnp.exp(-2.0 * jnp.abs(pre)))
    logp = jnp.sum(
        -0.5 * draw * draw - log_std - HALF_LOG_CIRCLE - 2.0 * (LOG_TWO - pre - soft),
        axis=0,
        keepdims=True,
    )
    return g_one, g_two, scaled, act, logp


def heads_kernel(me, own, got_one, got_two, got_three, out, stage):
    quarter = own.shape[0]
    for k, got in enumerate((own, got_one, got_two, got_three)):
        first = pl.multiple_of((me[0] ^ k) * quarter, quarter)
        stage[pl.ds(first, quarter)] = got[...].astype(F32)
    keep = lax.broadcasted_iota(jnp.int32, (SLOT, 1), 0) < QUANTS
    for e in range(CRITICS):
        out[e] = jnp.where(keep, stage[e * QUANTS : e * QUANTS + SLOT], 0.0).astype(BF)


def heads(me, own, got):
    return pl.pallas_call(
        heads_kernel,
        in_specs=[SCALAR] + [WHOLE] * 4,
        out_specs=WHOLE,
        out_shape=jax.ShapeDtypeStruct((CRITICS, SLOT, 2 * HIDDEN_SIZE), BF),
        scratch_shapes=[pltpu.VMEM((136, 2 * HIDDEN_SIZE), F32)],
        compiler_params=params(4),
        cost_estimate=cost(3e10, 1e6),
        name="heads",
    )(me, own, *got)


def fill_biases(small, lag_bias, out, col):
    keep = lax.broadcasted_iota(jnp.int32, (SLOT, 1), 0) < QUANTS
    both = jnp.concatenate([small[:, SMALL_VEC - PADDED :], lag_bias[...], jnp.zeros((6, PADDED), F32)], 0)
    col[:PADDED] = jnp.transpose(both)
    for e in range(CRITICS):
        columns = jnp.where(keep, col[e * QUANTS : e * QUANTS + SLOT], 0.0)
        for net in range(2):
            out[net, e] = jnp.broadcast_to(columns[:, net : net + 1], (SLOT, PADDED))


def fill_first(tall, filled, first, bias):
    body = INPUTS // 16 * 16
    high = bias.astype(BF).astype(F32)
    middle = (bias - high).astype(BF).astype(F32)
    filled[:body] = first[:body]
    tall[: INPUTS - body] = first[body:].astype(F32)
    tall[INPUTS - body : 32] = jnp.zeros((32 - INPUTS + body, HIDDEN_SIZE), F32)
    tall[INPUTS - body : INPUTS - body + 1] = high
    tall[INPUTS - body + 1 : INPUTS - body + 2] = middle
    tall[INPUTS - body + 2 : INPUTS - body + 3] = bias - high - middle
    filled[body : body + 32] = tall[...].astype(BF)
    filled[body + 32 :] = jnp.zeros((HIDDEN_SIZE - body - 32, HIDDEN_SIZE), BF)


def tiles(rows, width=TILE):
    width = min(rows, width)
    return [pl.ds(i * width, width) for i in range(rows // width)]


def critic_lanes(e):
    return pl.ds(pl.multiple_of(e * HIDDEN_SIZE, HIDDEN_SIZE), HIDDEN_SIZE)


def target_kernel(
    index, heat, inputs, logp, payoffs, done, order_in, first, second, bias, head, head_bias, after,
    lagged, keep, filled, tall_w, slots, packed, order, sems,
):
    rows = inputs.shape[1]
    mine = pl.ds(pl.multiple_of(index[0] * rows, PADDED), rows)
    copy = pltpu.make_async_copy(order_in.at[mine], order, sems.at[0])
    copy.start()
    def one_critic(e, carry):
        lanes = critic_lanes(e)
        fill_first(tall_w, filled, first[:, lanes], bias[:1, lanes])
        b_two = column(bias[1:2, lanes])
        w_two = second[:, lanes]
        for part in tiles(rows):
            h_one = relu(dot_tn(filled[...], inputs[:, part]))
            h_two = relu(dot_tn(w_two, h_one) + b_two)
            value = dot_nn(head[e, :, HIDDEN_SIZE:], h_two) + head_bias[1, e, :, :1]
            slots[pl.ds(pl.multiple_of(e * SLOT, SLOT), SLOT), part] = value
        return carry

    lax.fori_loop(0, CRITICS, one_critic, 0, unroll=True)
    for e in range(CRITICS):
        packed[e * QUANTS : e * QUANTS + SLOT] = slots[e * SLOT : (e + 1) * SLOT]
    copy.wait()
    for i in range(rows // PADDED):
        part = pl.ds(i * PADDED, PADDED)
        kept = (order[part] < KEPT_ATOMS).astype(F32)
        kept = jnp.concatenate([kept, jnp.zeros((PADDED, PADDED - MERGED_SUPPORTS), F32)], 1)
        keep[:, part] = jnp.transpose(kept).astype(BF)
    decay = DISCOUNT * (1.0 - done[:, mine].astype(F32))
    temperature = jnp.exp(jnp.full((1, 1), heat[0], F32))
    lagged[...] = payoffs[:, mine] + decay * (packed[:PADDED] - temperature * logp[...])


def target_pass(index, heat, inputs, logp, payoffs, done, order, first, second, bias, head, head_bias, after):
    rows = inputs.shape[1]
    return pl.pallas_call(
        target_kernel,
        in_specs=[SCALAR] * 2 + [WHOLE] * 4 + [pl.BlockSpec(memory_space=pltpu.HBM)] + [WHOLE] * 5 + [UNREAD],
        out_specs=[WHOLE] * 2,
        out_shape=[jax.ShapeDtypeStruct((PADDED, rows), F32), jax.ShapeDtypeStruct((PADDED, rows), BF)],
        scratch_shapes=[
            pltpu.VMEM((HIDDEN_SIZE, HIDDEN_SIZE), BF),
            pltpu.VMEM((32, HIDDEN_SIZE), F32),
            pltpu.VMEM((CRITICS * SLOT, rows), F32),
            pltpu.VMEM((136, rows), F32),
            pltpu.VMEM((rows, MERGED_SUPPORTS), jnp.int32),
            pltpu.SemaphoreType.DMA((1,)),
        ],
        compiler_params=params(24),
        cost_estimate=cost(7e9, 7e6),
        name="target_pass",
    )(index, heat, inputs, logp, payoffs, done, order, first, second, bias, head, head_bias, after)


HALF = 336


def two_terms(value):
    high = value.astype(BF).astype(F32)
    both = jnp.concatenate([high, value - high], 1)
    return jnp.concatenate([both, jnp.zeros((8, 2 * PADDED), F32)], 0).astype(BF)


def pilot_kernel(
    level, share, me, index, heat, obs, next_in, noise, noise_next_in, chosen, actor, small,
    first_in, second_in, bias, head, lag_bias,
    own_out, send_out, x_now, x_target, logp_next, head_bias,
    inputs, filled, tall_x, tall_w, dact, total, out_scratch, grad_out, small_out, next_obs, noise_next, col,
    first, second, sems,
):
    rows = obs.shape[1]
    mine = pl.ds(pl.multiple_of(index[0] * rows, PADDED), rows)
    copies = [
        pltpu.make_async_copy(next_in.at[:, mine], next_obs, sems.at[0]),
        pltpu.make_async_copy(noise_next_in.at[:, mine], noise_next, sems.at[1]),
        pltpu.make_async_copy(first_in, first, sems.at[2]),
        pltpu.make_async_copy(second_in, second, sems.at[3]),
    ]
    for copy in copies:
        copy.start()
    g_one, g_two, scaled, act, logp = actor_layers(obs[...], noise[...], actor, small, out_scratch)
    fill_inputs(tall_x, inputs, obs, act.astype(BF))
    fill_inputs(tall_x, x_now, obs, chosen[...])
    for copy in copies[:2]:
        copy.wait()
    _, _, _, next_act, next_logp = actor_layers(next_obs[...], noise_next[...], actor, small, out_scratch)
    fill_inputs(tall_x, x_target, next_obs, next_act.astype(BF))
    logp_next[...] = next_logp
    fill_biases(small, lag_bias, head_bias, col)
    for copy in copies[2:]:
        copy.wait()

    dact[...] = jnp.zeros(dact.shape, F32)
    total[...] = jnp.zeros(total.shape, F32)

    def one_critic(e, tail):
        lanes = critic_lanes(e)
        fill_first(tall_w, filled, first[:, lanes], bias[:1, lanes])
        b_two = column(bias[1:2, lanes])
        head_sum = jnp.sum(head[e, :, :HIDDEN_SIZE].astype(F32), axis=0, keepdims=True)
        weight = column(head_sum)
        push = column(head_sum * level)
        w_two = second[:, lanes]
        for part in tiles(rows):
            h_one = relu(dot_tn(filled[...], inputs[:, part]))
            h_two = relu(dot_tn(w_two, h_one) + b_two)
            weighted = (h_two * weight.astype(BF)).reshape(8, -1, 16, h_two.shape[1])
            total[:, part] += jnp.sum(tree([weighted[i] for i in range(8)]).astype(F32), axis=0)
            dz_two = jnp.where(h_two > 0, push.astype(BF), jnp.zeros((), BF))
            dz_one = gate(h_one, dot_nn(w_two, dz_two))
            dact[:, part] += dot_nn(first[OBS_DIM // 16 * 16 :, lanes], dz_one)
        return tail + head_bias[0, e, :, :1]

    tail = lax.fori_loop(0, CRITICS, one_critic, jnp.zeros((SLOT, 1), F32))
    temperature_share = jnp.exp(jnp.full((1, 1), heat[0], F32)) * share
    skip = OBS_DIM % 16
    action_grad = dact[skip : skip + ACT_DIM]
    pre = action_grad * (1.0 - act * act) + 2.0 * temperature_share * act
    out_scratch[:ACT_DIM] = pre
    out_scratch[ACT_DIM : 2 * ACT_DIM] = pre * scaled - temperature_share
    dout = out_scratch[: 2 * ACT_DIM].astype(BF)
    a_two = actor[OBS_DIM : OBS_DIM + ACTOR_HIDDEN]
    a_three = actor[OBS_DIM + ACTOR_HIDDEN :]
    dz_two = gate(g_two, dot_tn(a_three, dout))
    dz_one = gate(g_one, dot_nn(a_two, dz_two))
    grad_out[OBS_DIM + ACTOR_HIDDEN : OBS_DIM + ACTOR_HIDDEN + 2 * ACT_DIM] = dot_nt(dout, g_two)
    grad_out[OBS_DIM + ACTOR_HIDDEN + 2 * ACT_DIM :] = jnp.zeros((6, ACTOR_HIDDEN), F32)
    grad_out[OBS_DIM : OBS_DIM + ACTOR_HIDDEN] = dot_nt(g_one, dz_two)
    grad_out[:OBS_DIM] = dot_nt(obs[...], dz_one)
    ones = jnp.ones((16, rows), BF)
    small_out[...] = jnp.zeros(small_out.shape, F32)
    sum_one = dot_nt(ones, dz_one)[:1]
    sum_two = dot_nt(ones, dz_two)[:1]
    small_out[0:1] = sum_one[:, :PADDED]
    small_out[1:2] = sum_one[:, PADDED:]
    small_out[2:3] = sum_two[:, :PADDED]
    small_out[3:4] = sum_two[:, PADDED:]
    small_out[4:5, : 2 * ACT_DIM] = dot_nt(ones, dout)[:1]
    pilot_total = jnp.sum(total[...]) + rows * jnp.sum(tail)
    small_out[5:6] = jnp.broadcast_to(pilot_total, (1, PADDED))
    small_out[6:7] = jnp.broadcast_to(jnp.sum(logp), (1, PADDED))
    packed = two_terms(small_out[...])
    side = me[0] & 1
    for out, which in ((own_out, side), (send_out, 1 - side)):
        out[:HALF] = grad_out[pl.ds(pl.multiple_of(which * HALF, 16), HALF)].astype(BF)
        out[HALF:] = packed


def pilot_pass(
    level, share, me, index, heat, obs, next_obs, noise, noise_next, chosen, actor, small,
    first, second, bias, head, lag_bias,
):
    rows = obs.shape[1]
    far = pl.BlockSpec(memory_space=pltpu.HBM)
    filled = jax.ShapeDtypeStruct((HIDDEN_SIZE, rows), BF)
    return pl.pallas_call(
        functools.partial(pilot_kernel, level, share),
        in_specs=[SCALAR] * 3 + [WHOLE, far, WHOLE, far] + [WHOLE] * 3 + [far] * 2 + [WHOLE] * 3,
        out_specs=[WHOLE] * 6,
        out_shape=[jax.ShapeDtypeStruct((HALF + 16, ACTOR_HIDDEN), BF)] * 2
        + [filled, filled, jax.ShapeDtypeStruct((1, rows), F32)]
        + [jax.ShapeDtypeStruct((2, CRITICS, SLOT, PADDED), F32)],
        scratch_shapes=[
            pltpu.VMEM((HIDDEN_SIZE, rows), BF),
            pltpu.VMEM((HIDDEN_SIZE, HIDDEN_SIZE), BF),
            pltpu.VMEM((32, rows), F32),
            pltpu.VMEM((32, HIDDEN_SIZE), F32),
            pltpu.VMEM((INPUTS - OBS_DIM // 16 * 16, rows), F32),
            pltpu.VMEM((16, rows), F32),
            pltpu.VMEM((40, rows), F32),
            pltpu.VMEM((2 * HALF, ACTOR_HIDDEN), F32),
            pltpu.VMEM((8, PADDED), F32),
            pltpu.VMEM((OBS_DIM, rows), BF),
            pltpu.VMEM((ACT_DIM, rows), F32),
            pltpu.VMEM((136, 8), F32),
            pltpu.VMEM(first.shape, BF),
            pltpu.VMEM(second.shape, BF),
            pltpu.SemaphoreType.DMA((4,)),
        ],
        compiler_params=params(48),
        cost_estimate=cost(14e9, 9e6),
        name="pilot_pass",
    )(me, index, heat, obs, next_obs, noise, noise_next, chosen, actor, small, first, second, bias, head, lag_bias)


def pair_terms(q_ref, lagged, keep, parts, rows):
    def group(i, loss):
        part = pl.ds(pl.multiple_of(i * PADDED, PADDED), PADDED)
        q = q_ref[:, part]
        shift = jnp.sum(q, axis=0, keepdims=True) * (1.0 / QUANTS)
        y = (lagged[:, part] - shift).astype(BF).reshape(8, 16, PADDED)
        upper = keep[:, part].reshape(8, 16, PADDED)
        lower = -upper
        q_ref[:, part] = q - shift
        for j in range(QUANTS):
            level = jnp.broadcast_to(q_ref[j : j + 1, part], (16, PADDED)).astype(BF)
            d = y - level[None]
            c = jnp.minimum(jnp.maximum(d, lower), upper)
            half = c * jnp.asarray(0.5, BF)
            g = half + jnp.abs(c) * jnp.asarray((j + 0.5) / QUANTS - 0.5, BF)
            h = g * (d - half)
            g = g[:4] + g[4:]
            g = g[:2] + g[2:]
            parts[j * 16 : j * 16 + 16, part] = g[0] + g[1]
            h = h[:4] + h[4:]
            h = h[:2] + h[2:]
            h = h[0] + h[1]
            if j % 2:
                h = h + waiting
            if j % 2 or j == QUANTS - 1:
                h = h.astype(F32)
                loss = loss + (h[:8] + h[8:])
            waiting = h
        return loss

    loss = lax.fori_loop(0, rows // PADDED, group, jnp.zeros((8, PADDED), F32), unroll=2)
    shape = (SLOT, QUANTS * 16)
    row = lax.broadcasted_iota(jnp.int32, shape, 0)
    owner = lax.broadcasted_iota(jnp.int32, shape, 1) // 16
    return dot_nn((row == owner).astype(F32).astype(BF), parts[...]), loss


PARITY = 18


def granules(e):
    mine = range(32 * e, 32 * e + 32)
    return [[g for g in mine if g // CRITICS % 2 == parity] for parity in range(2)]


def granule_places(chunk):
    places = np.zeros(CRITICS * 32, np.int32)
    for i, e in enumerate(chunk):
        for way in granules(e):
            for t, g in enumerate(way):
                places[g] = i * PARITY + t
    return places


SENT = (11, 11)


def store_piece(outs, t, value):
    for out in outs:
        if t < out.shape[0]:
            out[t] = value
            return
        t -= out.shape[0]


def critic_kernel(
    e, waits, rows_scale, split, me, inputs, lagged, keep, first, second, bias, head, head_bias, *refs,
):
    last = e == CRITICS - 1
    refs = refs[waits:]
    if e:
        before, refs = refs[:3], refs[3:]
    outs, scratch = refs[:-9], refs[-9:]
    filled, tall_w, h_one, h_two, q, parts, grads, packed, extra = scratch
    rows = inputs.shape[1]
    lanes = slice(e * HIDDEN_SIZE, (e + 1) * HIDDEN_SIZE)
    second = second.at[:, lanes]
    head = head.at[e : e + 1, :, :HIDDEN_SIZE]
    head_bias = head_bias.at[:1, e : e + 1]
    fill_first(tall_w, filled, first[:, lanes], bias[:1, lanes])
    b_two = column(bias[1:2, lanes])
    for part in tiles(rows, CRITIC_TILE):
        h_one[:, part] = relu(dot_tn(filled[...], inputs[:, part]))
    for part in tiles(rows, CRITIC_TILE):
        h_two[:, part] = relu(dot_tn(second[...], h_one[:, part]) + b_two)
    for part in tiles(rows, CRITIC_TILE):
        q[:, part] = dot_nn(head[0], h_two[:, part]) + head_bias[0, 0, :, :1]
    terms, loss = pair_terms(q, lagged, keep, parts, rows)
    low = (terms * -rows_scale).astype(BF)
    head_grad = dot_nt(low, h_two[...])
    count = jnp.ones((8, rows), BF)
    bias_grad = dot_nt(count, low)[:1]
    sums = jnp.zeros((HIDDEN_SIZE, PADDED), F32)
    for part in tiles(rows, CRITIC_TILE):
        two = h_two[:, part]
        dz_two = gate(two, dot_tn(head[0], low[:, part.start : part.start + part.size]))
        lanes_of = [dz_two[:, i * PADDED : (i + 1) * PADDED] for i in range(part.size // PADDED)]
        sums = sums + tree(lanes_of).astype(F32)
        h_two[:, part] = dz_two
    second_grad = dot_nt(h_two[...], h_one[...])
    for part in tiles(rows, CRITIC_TILE):
        one = h_one[:, part]
        h_one[:, part] = gate(one, dot_nn(second[...], h_two[:, part]))
    grads[:, :, :HIDDEN_SIZE] = second_grad.astype(BF).reshape(-1, 16, HIDDEN_SIZE)
    first_grad = dot_nt(h_one[...], inputs[...])
    grads[:, :, HIDDEN_SIZE : LANES - PADDED] = (
        first_grad[:, : HIDDEN_SIZE - PADDED].astype(BF).reshape(-1, 16, HIDDEN_SIZE - PADDED)
    )
    lane = lax.broadcasted_iota(jnp.int32, (HIDDEN_SIZE, PADDED), 1)
    tail = jnp.where(
        lane == INPUTS + 1 - HIDDEN_SIZE + PADDED,
        jnp.sum(sums, axis=1, keepdims=True),
        first_grad[:, HIDDEN_SIZE - PADDED :],
    )
    grads[:, :, LANES - PADDED : LANES] = tail.astype(BF).reshape(-1, 16, PADDED)
    direct = split[0] > 0
    rest = outs[1 + (len(SENT) if last else 1) :] if direct else outs[1:]
    if not last:
        all_heads, all_bias, all_loss = rest
        if e:
            all_heads[...] = before[0][...]
            all_bias[...] = before[1][...]
            all_loss[...] = before[2][...] + loss
        else:
            all_heads[...] = jnp.zeros(all_heads.shape, F32)
            all_bias[...] = jnp.zeros(all_bias.shape, F32)
            all_loss[...] = loss
        all_heads[e * SLOT : (e + 1) * SLOT] = head_grad
        all_bias[e : e + 1, :SLOT] = bias_grad
    else:
        n_rows, n_quant = split
        for i in range(CRITICS):
            packed[i * QUANTS : i * QUANTS + SLOT] = (
                before[0][i * SLOT : (i + 1) * SLOT] if i < e else head_grad
            )
        bias_row = jnp.zeros((1, PADDED), F32)
        lane = lax.broadcasted_iota(jnp.int32, (1, PADDED), 1)
        spare = jnp.zeros((1, PADDED - SLOT), F32)
        for i in range(CRITICS):
            piece = before[1][i : i + 1] if i < e else jnp.concatenate([bias_grad, spare], 1)
            piece = pltpu.roll(jnp.broadcast_to(piece, (8, PADDED)), i * QUANTS, 1)[:1]
            inside = (lane >= i * QUANTS) & (lane < (i + 1) * QUANTS)
            bias_row = jnp.where(inside, piece, bias_row)
        value = jnp.sum(before[2][...] + loss, axis=0, keepdims=True)
        value = jnp.sum(value, axis=1, keepdims=True) * rows_scale
        value = jnp.broadcast_to(value, (1, PADDED))
        if direct:
            width = HIDDEN_SIZE // n_rows
            high = PADDED // n_quant
            lane = lax.broadcasted_iota(jnp.int32, (16, PADDED), 1)
            halves = [bias_row, pltpu.roll(jnp.broadcast_to(bias_row, (8, PADDED)), 64, 1)[:1], value]
            common = jnp.concatenate(halves + [jnp.zeros((13, PADDED), F32)], 0)
            for j in range(8):
                y, c = j // 4, j % 4
                for z in range(n_rows // 2):
                    r = 2 * z + y
                    block = packed[c * high : (c + 1) * high, r // 2 * PADDED : (r // 2 + 1) * PADDED]
                    if r % 2 == 0:
                        block = pltpu.roll(block, width, 1)
                    base = 2 * z * PADDED
                    extra[j, :, base : base + PADDED] = jnp.where(lane < 64, common, block[:16]).astype(BF)
                    extra[j, :, base + PADDED : base + 2 * PADDED] = block[16:].astype(BF)
        else:
            rest[0][...] = packed[:PADDED]
            rest[1][...] = jnp.concatenate([bias_row, value, jnp.zeros((6, PADDED), F32)], 0)
    if not direct:
        outs[0][...] = grads[...]
        return
    sent, kept = outs[: len(SENT) if last else 1], outs[len(SENT) if last else 1]
    side = me[0] & 1
    ways = granules(e)
    for t in range(max(map(len, ways))):
        pair = [way[min(t, len(way) - 1)] - e * 32 for way in ways]
        kept[t] = grads[jnp.where(side == 0, pair[0], pair[1])]
        store_piece(sent, t, grads[jnp.where(side == 0, pair[1], pair[0])])
    if last:
        for i in range(4):
            kept[PARITY + i] = extra[2 * i + side]
            store_piece(sent, PARITY + i, extra[2 * i + 1 - side])


def critic_pass(e, rows_scale, split, me, inputs, lagged, keep, first, second, bias, head, head_bias, after, before):
    rows = inputs.shape[1]
    last = e == CRITICS - 1
    if split[0]:
        block = lambda count: jax.ShapeDtypeStruct((count, 16, LANES), BF)
        sent = SENT if last else (PARITY,)
        out_shape = [block(count) for count in sent] + [block(sum(sent))]
    else:
        out_shape = [jax.ShapeDtypeStruct((HIDDEN_SIZE // 16, 16, LANES), BF)]
    if not last:
        out_shape += [
            jax.ShapeDtypeStruct((CRITICS * SLOT, HIDDEN_SIZE), F32),
            jax.ShapeDtypeStruct((8, PADDED), F32),
            jax.ShapeDtypeStruct((8, PADDED), F32),
        ]
    elif not split[0]:
        out_shape += [
            jax.ShapeDtypeStruct((PADDED, HIDDEN_SIZE), F32),
            jax.ShapeDtypeStruct((8, PADDED), F32),
        ]
    return pl.pallas_call(
        functools.partial(critic_kernel, e, len(after), rows_scale, split),
        in_specs=[SCALAR] + [WHOLE] * 8 + [UNREAD] * len(after) + [WHOLE] * len(before),
        out_specs=[WHOLE] * len(out_shape),
        out_shape=out_shape,
        scratch_shapes=[
            pltpu.VMEM((HIDDEN_SIZE, HIDDEN_SIZE), BF),
            pltpu.VMEM((32, HIDDEN_SIZE), F32),
            pltpu.VMEM((HIDDEN_SIZE, rows), BF),
            pltpu.VMEM((HIDDEN_SIZE, rows), BF),
            pltpu.VMEM((SLOT, rows), F32),
            pltpu.VMEM((QUANTS * 16, rows), BF),
            pltpu.VMEM((HIDDEN_SIZE // 16, 16, LANES), BF),
            pltpu.VMEM((136, HIDDEN_SIZE), F32),
            pltpu.VMEM((8, 16, LANES), BF),
        ],
        compiler_params=params(24),
        cost_estimate=cost(7e9, 4e6),
        name="critic_pass",
    )(me, inputs, lagged, keep, first, second, bias, head, head_bias, *after, *before)


def add_kernel(a, b, out):
    out[:HALF] = (a[:HALF].astype(F32) + b[:HALF].astype(F32)).astype(BF)
    pair = [r[HALF:].astype(F32) for r in (a, b)]
    pair = [p[:8, :PADDED] + p[:8, PADDED:] for p in pair]
    out[HALF:] = two_terms(pair[0] + pair[1])


def add_actor(a, b):
    return pl.pallas_call(
        add_kernel,
        in_specs=[WHOLE, WHOLE],
        out_specs=WHOLE,
        out_shape=jax.ShapeDtypeStruct(a.shape, BF),
        compiler_params=params(),
        cost_estimate=cost(1e5, 6e5),
        name="add_actor",
    )(a, b)


def core_kernel(chunk, depth, waits, me, places, *refs):
    count = len(chunk)
    refs = refs[waits:]
    kept, got, outs, sums = refs[:count], refs[count:-3], refs[-3:-1], refs[-1]
    size = count * PARITY
    first = 0
    for piece in got:
        i, inside = min(first // PARITY, count - 1), first - min(first // PARITY, count - 1) * PARITY
        own = kept[i][inside : inside + piece.shape[0]]
        sums[first : first + piece.shape[0]] = own + piece[...]
        first += piece.shape[0]
    z_first = chunk[-1] // 3 * depth
    side = me[0] & 1
    for k in range(4):
        flip = (0, 4 - 2 * side, 2 + 2 * side, 6)[k]
        j = (me[0] & 7) ^ flip
        out = outs[k // 2]
        for z in range(depth):
            owner = (z_first + z) * 8 + j
            for i in range(CRITICS):
                out[k % 2, z * CRITICS + i] = sums[places[owner * CRITICS + i]]
        if chunk[-1] == CRITICS - 1:
            out[k % 2, depth * CRITICS] = sums[size + j // 2]


def add_core(chunk, depth, me, kept, got, after=()):
    tail = kept[-1].shape[0] - PARITY
    count = depth * CRITICS + (1 if tail else 0)
    return pl.pallas_call(
        functools.partial(core_kernel, chunk, depth, len(after)),
        in_specs=[SCALAR, SCALAR] + [UNREAD] * len(after) + [WHOLE] * (len(kept) + len(got)),
        out_specs=[WHOLE] * 2,
        out_shape=[jax.ShapeDtypeStruct((2, count, 16, LANES), BF)] * 2,
        scratch_shapes=[pltpu.VMEM((len(kept) * PARITY + tail, 16, LANES), BF)],
        compiler_params=params(),
        cost_estimate=cost(1e6, 8e6),
        name="add_core",
    )(me, jnp.asarray(granule_places(chunk)), *after, *kept, *got)


def tree(values):
    while len(values) > 1:
        values = [a + b for a, b in zip(values[::2], values[1::2])]
    return values[0]


def half_kernel(kept, got, own, send):
    for k, out in enumerate((own, send)):
        out[...] = kept[k] + got[k]


def add_half(kept, got, after=()):
    waits = len(after)
    return pl.pallas_call(
        lambda *refs: half_kernel(*refs[waits:]),
        in_specs=[UNREAD] * waits + [WHOLE] * 2,
        out_specs=[WHOLE] * 2,
        out_shape=[jax.ShapeDtypeStruct(kept.shape[1:], BF)] * 2,
        compiler_params=params(8),
        cost_estimate=cost(1e5, 1e5),
        name="add_half",
    )(*after, kept, got)


def line_kernel(me, early, early_got, late, late_got, *refs):
    outs, sums = refs[:-1], refs[-1]
    count = early.shape[0]
    sums[:count] = early[...] + early_got[...]
    total = late[...].astype(F32) + late_got[...].astype(F32)
    sums[count:] = total[:count].astype(BF)
    extra = total[count]
    lane = lax.broadcasted_iota(jnp.int32, (16, PADDED), 1)
    for z in range(len(outs)):
        first = extra[:, 2 * z * PADDED : (2 * z + 1) * PADDED]
        second = extra[:, (2 * z + 1) * PADDED : (2 * z + 2) * PADDED]
        for i, value in enumerate((first, second, pltpu.roll(first, 64, 1))):
            old = sums[z * CRITICS + i, :, LANES - PADDED :].astype(F32)
            sums[z * CRITICS + i, :, LANES - PADDED :] = jnp.where(lane < 64, old, value).astype(BF)
    for k, out in enumerate(outs):
        first = ((me[0] // 8) ^ k) * CRITICS
        for i in range(CRITICS):
            out[i] = sums[first + i]


def add_line(me, early, late, depth, after=()):
    waits = len(after)
    return pl.pallas_call(
        lambda *refs: line_kernel(*refs[waits:]),
        in_specs=[UNREAD] * waits + [SCALAR] + [WHOLE] * 4,
        out_specs=[WHOLE] * depth,
        out_shape=[jax.ShapeDtypeStruct((CRITICS, 16, LANES), BF)] * depth,
        scratch_shapes=[pltpu.VMEM((2 * early[0].shape[0], 16, LANES), BF)],
        compiler_params=params(),
        cost_estimate=cost(1e6, 6e6),
        name="add_line",
    )(*after, me, *early, *late)


def adamw(weight, first, second, grad, rate, factors, outs):
    first_new = BETA_FIRST * first[...] + (1.0 - BETA_FIRST) * grad
    second_new = BETA_SECOND * second[...] + (1.0 - BETA_SECOND) * grad * grad
    old = weight[...]
    step = (first_new * factors[0]) / (jnp.sqrt(second_new * factors[1]) + EPSILON)
    outs[0][...] = old - rate * (step + WEIGHT_DECAY * old)
    outs[1][...] = first_new
    outs[2][...] = second_new


def row_kernel(*refs):
    total = tree([r[2, :, LANES - PADDED :].astype(F32) for r in refs[:-1]])
    total = pltpu.roll(total, 64, 1)
    row = jnp.concatenate([total[:1, :64], total[1:2, :64]], 1)
    refs[-1][...] = jnp.concatenate([row, jnp.broadcast_to(total[2:3, :1], (7, PADDED))], 0)


def sum_row(blocks):
    return pl.pallas_call(
        row_kernel,
        in_specs=[WHOLE] * len(blocks),
        out_specs=WHOLE,
        out_shape=jax.ShapeDtypeStruct((8, PADDED), F32),
        compiler_params=params(8),
        cost_estimate=cost(1e5, 1e5),
        name="sum_row",
    )(*blocks)


def update_kernel(count, direct, factors, *refs):
    blocks, refs = refs[:count], refs[count:]
    if direct:
        total = tree([b[...].astype(F32) for b in blocks]).reshape(-1, LANES)
        head_grad = pltpu.roll(total[:SLOT, LANES - PADDED :], 64, 1)[:, :64]
    else:
        total = blocks[0][...]
        head_grad, refs = refs[0][...], refs[1:]
    state, outs = refs[:12], refs[12:]
    adamw(*state[0:3], total[:, HIDDEN_SIZE : HIDDEN_SIZE + INPUTS], RATE_MATRIX, factors, outs[0:3])
    adamw(*state[3:6], total[:, :HIDDEN_SIZE], RATE_MATRIX, factors, outs[3:6])
    edge = INPUTS - HIDDEN_SIZE + PADDED
    bias_grad = jnp.transpose(total[:, LANES - PADDED :])[edge : edge + 2]
    adamw(*state[6:9], bias_grad, RATE_VECTOR, factors, outs[6:9])
    adamw(*state[9:12], head_grad, RATE_MATRIX, factors, outs[9:12])


def update(factors, blocks, others, state):
    shapes = [jax.ShapeDtypeStruct(a.shape, F32) for a in state]
    count = len(blocks)
    return pl.pallas_call(
        functools.partial(update_kernel, count, not others),
        in_specs=[SCALAR] + [WHOLE] * (count + len(others) + len(state)),
        out_specs=[WHOLE] * len(shapes),
        out_shape=shapes,
        compiler_params=params(),
        cost_estimate=cost(2e6, 6e6),
        name="update",
    )(factors, *blocks, *others, *state)


def actor_update_kernel(me, factors, own, peer, *refs):
    state, outs, grad = refs[:3], refs[3:7], refs[7]
    side = me[0] & 1
    grad[pl.ds(pl.multiple_of(side * HALF, 16), HALF)] = own[:HALF].astype(F32)
    grad[pl.ds(pl.multiple_of((1 - side) * HALF, 16), HALF)] = peer[:HALF].astype(F32)
    adamw(*state, grad[: state[0].shape[0]], RATE_MATRIX, factors, outs[:3])
    pair = own[HALF:].astype(F32)
    outs[3][...] = pair[:8, :PADDED] + pair[:8, PADDED:]


def actor_update(me, factors, own, peer, state):
    shapes = [jax.ShapeDtypeStruct(a.shape, F32) for a in state] + [jax.ShapeDtypeStruct((8, PADDED), F32)]
    return pl.pallas_call(
        actor_update_kernel,
        in_specs=[SCALAR, SCALAR] + [WHOLE] * (2 + len(state)),
        out_specs=[WHOLE] * len(shapes),
        out_shape=shapes,
        scratch_shapes=[pltpu.VMEM((2 * HALF, ACTOR_HIDDEN), F32)],
        compiler_params=params(),
        cost_estimate=cost(2e6, 5e6),
        name="actor_update",
    )(me, factors, own, peer, *state)


def small_update_kernel(samples, me, factors, row_own, row_peer, small_sums, *refs):
    state, outs, vector = refs[:6], refs[6:13], refs[13]
    row = jnp.where((me[0] & 1) == 0, row_own[...], row_peer[...])
    for i in range(4):
        vector[i * PADDED : (i + 1) * PADDED] = small_sums[i]
    wide = jnp.concatenate([row, jnp.zeros((8, PADDED), F32)], 1)
    wide = pltpu.roll(wide, 2 * ACT_DIM, 1)
    wide = wide + jnp.concatenate([small_sums[4:5], jnp.zeros((1, PADDED), F32)], 1)
    vector[4 * PADDED :] = wide[0]
    adamw(*state[:3], vector[:SMALL_VEC], RATE_VECTOR, factors, outs[1:4])
    heat = state[3][...]
    logp_sum = small_sums[6:7, :1]
    shortfall = (ACT_DIM * samples - logp_sum) / samples
    adamw(*state[3:6], shortfall, STEP_SIZE_SCALE, factors, outs[4:7])
    actor_loss = (jnp.exp(heat) * logp_sum - small_sums[5:6, :1] / MERGED_SUPPORTS) / samples
    outs[0][...] = row[1:2, :1] + actor_loss + heat * shortfall


def small_update(samples, me, factors, row, row_peer, small_sums, state):
    shapes = [jax.ShapeDtypeStruct((1, 1), F32)] + [jax.ShapeDtypeStruct(a.shape, F32) for a in state]
    return pl.pallas_call(
        functools.partial(small_update_kernel, samples),
        in_specs=[SCALAR, SCALAR] + [WHOLE] * (3 + len(state)),
        out_specs=[WHOLE] * len(shapes),
        out_shape=shapes,
        scratch_shapes=[pltpu.VMEM((6 * PADDED,), F32)],
        compiler_params=params(8),
        cost_estimate=cost(1e6, 1e5),
        name="small_update",
    )(me, factors, row, row_peer, small_sums, *state)


def exchange(value, flip):
    count = lax.axis_size("rows") * lax.axis_size("quant")
    return lax.ppermute(value, AXES, [(i, i ^ flip) for i in range(count)])


def exchange_sides(value, even, odd):
    count = lax.axis_size("rows") * lax.axis_size("quant")
    return lax.ppermute(value, AXES, [(i, i ^ (odd if i % 2 else even)) for i in range(count)])


def all_sum(value):
    total = lax.axis_size("rows") * lax.axis_size("quant")
    flip = 1
    while flip < total:
        value = value + exchange(value, flip)
        flip *= 2
    return value


def scatter_sum(pieces):
    total = pieces.shape[0]
    flip = total // 2
    while flip:
        low = pieces.astype(BF)
        pieces = low[:flip].astype(F32) + exchange(low[flip:], flip).astype(F32)
        flip //= 2
    return pieces[0]


def local(
    obs, chosen, noise_now, next_obs, noise_next, payoffs, done, order,
    w_one, w_two, biases, head_part, t_one, t_two, t_biases, t_head_part, t_head_bias,
    actor, counter,
    in_w, in_m, in_v, mid_w, mid_m, mid_v, bias_w, bias_m, bias_v, head_w, head_m, head_v,
    actor_w, actor_m, actor_v, small_w, small_m, small_v, heat, heat_m, heat_v,
):
    n_rows, n_quant = lax.axis_size("rows"), lax.axis_size("quant")
    devices = n_rows * n_quant
    rows = obs.shape[0]
    samples = rows * devices
    index = lax.axis_index("quant").reshape(1)
    device = lax.axis_index("rows") * n_quant + lax.axis_index("quant")
    me = device.reshape(1)
    direct = n_rows == 8 and n_quant == 4
    small_row = small_w.reshape(1, -1)
    tally = counter.astype(F32)
    factors = jnp.concatenate(
        [1.0 / (1.0 - jnp.power(BETA_FIRST, tally)), 1.0 / (1.0 - jnp.power(BETA_SECOND, tally))]
    )

    own_head = jnp.concatenate([head_part.T, t_head_part.T], 1)
    got = [
        lax.ppermute(own_head, "quant", [(i, i ^ k) for i in range(n_quant)]) for k in (1, 2, 3)
    ]
    head = heads(index, own_head, got)

    level = float(np.asarray(-1.0 / (MERGED_SUPPORTS * samples), ml_dtypes.bfloat16))
    own, send, x_now, x_target, logp, head_bias = pilot_pass(
        level, 1.0 / samples, me, index, heat, obs.T, next_obs.T, noise_now.T, noise_next.T, chosen.T,
        actor, small_row, w_one, w_two, biases, head, t_head_bias.reshape(1, -1),
    )
    lagged, keep = target_pass(
        index, heat, x_target, logp, payoffs.reshape(1, -1), done.reshape(1, -1), order,
        t_one, t_two, t_biases, head, head_bias, own,
    )
    own = add_actor(own, exchange(send, 1))
    flips = [1 << i for i in range(1, devices.bit_length() - 1)]
    scale = 1.0 / (samples * MERGED_SUPPORTS * KEPT_ATOMS)
    split = (n_rows, n_quant) if direct else (0, 0)
    kept, got, before, early = [], [], (), None
    for e in range(CRITICS):
        after = [own] if e < 4 else []
        if direct and e == CRITICS - 1:
            early = add_core((0, 1, 2), 2, me, kept[:3], got[:3])
            early = [early[0], exchange_sides(early[1], 2, 4)]
            after = [early[0]]
        outs = critic_pass(
            e, scale, split, me, x_now, lagged, keep, w_one, w_two, biases, head, head_bias, after, before
        )
        if direct:
            count = len(SENT) if e == CRITICS - 1 else 1
            got.extend(exchange(piece, 1) for piece in outs[:count])
            outs = outs[count:]
        kept.append(outs[0])
        before = outs[1:]
        for flip in flips[e : e + 1] if e < CRITICS - 1 else flips[e:]:
            own = add_actor(own, exchange(own, flip))
    peer = exchange(own, 1)
    *actor_new, small_sums = actor_update(me, factors, own, peer, (actor_w, actor_m, actor_v))

    if direct:
        early = add_half(*early)
        late = add_core((2, 3, 4), 2, me, kept[2:], got[2:], (early[0],))
        early = [early[0], exchange_sides(early[1], 4, 2)]
        late = add_half(late[0], exchange_sides(late[1], 2, 4), (own, early[1]))
        late = [late[0], exchange_sides(late[1], 4, 2)]
        blocks = add_line(me, early, late, n_rows // 2, (small_sums,))
        blocks = [blocks[0]] + [exchange(blocks[k], 8 * k) for k in range(1, len(blocks))]
        others = []
        row = sum_row(blocks)
        row_peer = exchange(row, 1)
    else:
        grads = jnp.stack(kept).reshape(devices, -1, LANES)
        order_of = device ^ jnp.arange(devices)
        blocks = [scatter_sum(jnp.take(grads, order_of, axis=0))]
        head_grad = before[0].reshape(n_quant, PADDED // n_quant, n_rows, HIDDEN_SIZE // n_rows)
        head_grad = head_grad.transpose(2, 0, 1, 3).reshape((devices,) + (PADDED // n_quant, -1))
        head_grad = scatter_sum(jnp.take(head_grad, order_of, axis=0))
        others = [head_grad]
        row = row_peer = all_sum(before[1])
    state = (
        in_w.T, in_m.T, in_v.T, mid_w.T, mid_m.T, mid_v.T, bias_w, bias_m, bias_v, head_w.T, head_m.T, head_v.T,
    )
    new = update(factors, blocks, others, state)
    state = (
        small_w, small_m, small_v,
        heat.reshape(1, 1), heat_m.reshape(1, 1), heat_v.reshape(1, 1),
    )
    objective, *last = small_update(samples, me, factors, row, row_peer, small_sums, state)
    return (
        objective.reshape(()),
        *(a.T for a in new[:6]),
        *new[6:9],
        *(a.T for a in new[9:]),
        *actor_new,
        *last[:3],
        *(a.reshape(-1) for a in last[3:]),
    )


def solution(mesh):
    both, row, none = P(AXES), P("rows"), P()
    column_of, shard = P(None, "quant"), P(None, AXES)
    placed = (
        (both,) * 3 + (row,) * 5 + (none,) * 3 + (column_of,) + (none,) * 3 + (column_of,) + (none,) * 3
        + (shard,) * 9 + (P("rows", "quant"),) * 3 + (none,) * 9
    )
    return jax.shard_map(
        local,
        mesh=mesh,
        in_specs=placed,
        out_specs=(none,) + (shard,) * 9 + (P("rows", "quant"),) * 3 + (none,) * 9,
        check_vma=False,
    )
```
